32 devices in a mesh: section: 2 (over x), dp: 4 (over z), seq: 4 (over y, core).
Axes of the slice: x: 2, y: 2, z: 4, core: 2. Of those that a mesh axis runs over, the one named last changes fastest.
Arguments:
- x_in: bfloat16 [2, 2, 4, 1024, 768], P('section', None, 'dp', 'seq'), may hold values from -18 to 18
- segments: int32 [2, 2, 4, 1024], P(None, None, 'dp', 'seq'), may hold values from 0 to 3, as said below
- cotangent: bfloat16 [2, 4, 1024, 768], P(None, 'dp', 'seq'), may hold values from -6 to 6
- attn_in: bfloat16 [2, 768, 2304], P('section'), may hold values from -0.15625 to 0.15625
- attn_out: bfloat16 [2, 768, 768], P('section'), may hold values from -0.625 to 0.625
- attn_bias: float32 [2, 6, 768], P('section'), may hold values from -1 to 1
- gains: float32 [2, 2, 768], P('section'), may hold values from 0.5 to 1.5
- ffn_in: bfloat16 [2, 768, 3072], P('section'), may hold values from -0.21875 to 0.21875
- ffn_bias: float32 [2, 3072], P('section'), may hold values from -1 to 1
- ffn_out: bfloat16 [2, 3072, 768], P('section'), may hold values from -0.109375 to 0.109375
- cross_q: bfloat16 [768, 768], replicated, may hold values from -0.3125 to 0.3125
- cross_kv: bfloat16 [768, 1536], replicated, may hold values from -0.21875 to 0.21875
- cross_out: bfloat16 [768, 768], replicated, may hold values from -0.625 to 0.625
- cross_bias: float32 [4, 768], replicated, may hold values from -1 to 1
- cross_gain: float32 [768], replicated, may hold values from 0.5 to 1.5
Outputs:
- layer_out: bfloat16 [2, 2, 4, 1024, 768], P('section', None, 'dp', 'seq')
- input_grad: bfloat16 [2, 2, 4, 1024, 768], P('section', None, 'dp', 'seq')
- stats: float32 [2, 2], P('section')
- attn_in_grad: float32 [2, 768, 2304], P('section', ('dp', 'seq'))
- attn_out_grad: float32 [2, 768, 768], P('section', ('dp', 'seq'))
- attn_bias_grad: float32 [2, 6, 768], P('section', None, ('dp', 'seq'))
- gains_grad: float32 [2, 2, 768], P('section', None, ('dp', 'seq'))
- ffn_in_grad: float32 [2, 768, 3072], P('section', ('dp', 'seq'))
- ffn_bias_grad: float32 [2, 3072], P('section', ('dp', 'seq'))
- ffn_out_grad: float32 [2, 3072, 768], P('section', ('dp', 'seq'))
- cross_q_grad: float32 [768, 768], P(('section', 'dp', 'seq'))
- cross_kv_grad: float32 [768, 1536], P(('section', 'dp', 'seq'))
- cross_out_grad: float32 [768, 768], P(('section', 'dp', 'seq'))
- cross_bias_grad: float32 [4, 768], P(None, ('section', 'dp', 'seq'))
- cross_gain_grad: float32 [768], P(('section', 'dp', 'seq'))
The draws below stay inside these ranges and needn't reach their ends.
Inputs may be any that keep to these rules, and one draw needn't show every extreme that they name: `segments`: ids of a row never fall, and each of 0, 1, 2, 3 appears in every row; document k of a target row attends to document k of the source row.
All inputs are finite; a program needn't handle non-finite values.
Results may differ from the reference program's by a relative error of at most 0.025.
Values may be sent and summed in bfloat16 or wider, within the bound.
A program may use at most 384 MiB of HBM per device.

```python
import math
import jax
import jax.numpy as jnp
from jax import lax

D = 768
HEADS = 12
HEAD_DIM = 64
FF = 3072
SEQ_LEN = 1024
MICRO = 2
ROWS_MB = 4
SHARD = 256


def draw_x_in(key, part):
    key = jax.random.fold_in(key, 11)
    full_shape = (2, MICRO, ROWS_MB, SEQ_LEN, D)
    base = jnp.clip(jax.random.normal(key, full_shape, jnp.float32), -6.0, 6.0)
    row_place = jnp.arange(ROWS_MB, dtype=jnp.float32) / max(ROWS_MB - 1, 1)
    position = jnp.arange(SEQ_LEN, dtype=jnp.float32) / (SEQ_LEN - 1)
    exponent = 0.5 * row_place[:, None] + 0.5 * position[None, :]
    factor = jnp.exp(exponent * jnp.log(3.0))
    return (base * factor[None, None, :, :, None]).astype(jnp.bfloat16)


def draw_segments(key, part):
    key = jax.random.fold_in(key, 23)
    first_key, second_key, third_key = jax.random.split(key, 3)
    cut_shape = (2, MICRO, ROWS_MB, 1)
    first_cut = jax.random.randint(first_key, cut_shape, 1, SHARD)
    second_cut = jax.random.randint(second_key, cut_shape, SEQ_LEN - SHARD + 1, SEQ_LEN - 1)
    third_cut = jax.random.randint(third_key, cut_shape, second_cut + 1, SEQ_LEN)
    position = jnp.arange(SEQ_LEN, dtype=jnp.int32)[None, None, None, :]
    return (position >= first_cut).astype(jnp.int32) + (position >= second_cut).astype(jnp.int32) + (position >= third_cut).astype(jnp.int32)


def levels(key, extent, cuts, least, top_value):
    factor_of = 1.0
    for dim, parts in cuts:
        heights = jax.random.uniform(jax.random.fold_in(jax.random.fold_in(key, 6), dim), (parts,), jnp.float32, least / len(cuts), top_value / len(cuts))
        factor_of = factor_of * jnp.repeat(jnp.exp(heights), extent[dim] // parts).reshape((-1,) + (1,) * (len(extent) - 1 - dim))
    return factor_of


def centred(own_key, extent, scale, reach, pieces=(), kind=jnp.bfloat16):
    array = jax.random.normal(own_key, extent, jnp.float32) * scale
    if len(pieces) > 0:
        array = levels(own_key, extent, pieces, -0.22, 0.18) * array
    return jnp.clip(array, min=-reach, max=reach).astype(kind)


def setup_inputs(seed: int = 0) -> dict:
    key_list = jax.random.split(jax.random.key(seed), 16)
    x_in = draw_x_in(jax.random.fold_in(key_list[15], 71), 0)
    segments = draw_segments(jax.random.fold_in(key_list[15], 71), 0)
    cotangent = centred(key_list[2], (MICRO, ROWS_MB, SEQ_LEN, D), 1.0, 6.0, ((1, 4), (2, 4)))
    attn_in = centred(key_list[3], (2, D, 3 * D), (2 * D) ** -0.5, 0.15625, ((0, 2),))
    attn_out = centred(key_list[4], (2, D, D), (D // 8) ** -0.5, 0.625, ((0, 2),))
    attn_bias = centred(key_list[5], (2, 6, D), 0.2, 1.0, ((0, 2),), jnp.float32)
    gains = jnp.clip(1.0 + 0.1 * jax.random.normal(key_list[6], (2, 2, D), jnp.float32), 0.5, 1.5)
    ffn_in = centred(key_list[7], (2, D, FF), D ** -0.5, 0.21875, ((0, 2),))
    ffn_bias = centred(key_list[8], (2, FF), 0.2, 1.0, ((0, 2),), jnp.float32)
    ffn_out = centred(key_list[9], (2, FF, D), FF ** -0.5, 0.109375, ((0, 2),))
    cross_q = centred(key_list[10], (D, D), (D // 2) ** -0.5, 0.3125)
    cross_kv = centred(key_list[11], (D, 2 * D), D ** -0.5, 0.21875)
    cross_out = centred(key_list[12], (D, D), (D // 8) ** -0.5, 0.625)
    cross_bias = centred(key_list[13], (4, D), 0.2, 1.0, (), jnp.float32)
    cross_gain = jnp.clip(1.0 + 0.1 * jax.random.normal(key_list[14], (D,), jnp.float32), 0.5, 1.5)
    return dict(x_in=x_in, segments=segments, cotangent=cotangent, attn_in=attn_in, attn_out=attn_out, attn_bias=attn_bias, gains=gains, ffn_in=ffn_in, ffn_bias=ffn_bias, ffn_out=ffn_out, cross_q=cross_q, cross_kv=cross_kv, cross_out=cross_out, cross_bias=cross_bias, cross_gain=cross_gain)


PRECISE = lax.Precision.HIGHEST
EPSILON = 1e-05
MASKED = -1000000000.0

@jax.custom_vjp
def low(v):
    return lax.optimization_barrier(v.astype(jnp.bfloat16)).astype(jnp.float32)

@jax.custom_vjp
def low_back(v):
    return v

def low_keep(v):
    return (low(v), None)

def low_pass(kept, grad):
    return (grad,)

def back_keep(v):
    return (v, None)

def back_low(kept, grad):
    return (low(grad),)
low.defvjp(low_keep, low_pass)
low_back.defvjp(back_keep, back_low)

def norm_apply(tensor, scale_gain, offset):
    average = lax.optimization_barrier(jnp.mean(tensor, -1, keepdims=True))
    centered = tensor - average
    spread = lax.optimization_barrier(jnp.mean(centered * centered, -1, keepdims=True))
    return centered * lax.rsqrt(spread + EPSILON) * scale_gain + offset

def dense_layer(activation, weight, offset):
    return jnp.dot(activation, weight, precision=PRECISE, preferred_element_type=jnp.float32) + offset

def attend(queries, key_rows, value_rows, ids_query, ids_key, causal):
    length = queries.shape[0]
    key_count = key_rows.shape[0]
    query_heads = queries.reshape(length, HEADS, HEAD_DIM)
    key_heads = key_rows.reshape(key_count, HEADS, HEAD_DIM)
    value_heads = value_rows.reshape(key_count, HEADS, HEAD_DIM)
    raw_scores = low_back(jnp.einsum('qhd,khd->hqk', query_heads, key_heads, precision=PRECISE) * (1.0 / math.sqrt(HEAD_DIM)))
    query_pos = jnp.arange(length)
    key_pos = jnp.arange(key_count)
    before = (key_pos[None, :] <= query_pos[:, None]) | jnp.logical_not(causal)
    allowed = (ids_query[:, None] == ids_key[None, :]) & before
    scores = jnp.where(allowed[None], raw_scores, MASKED)
    row_peak = lax.optimization_barrier(jnp.max(scores, -1, keepdims=True))
    log_total = row_peak + jnp.log(lax.optimization_barrier(jnp.sum(jnp.exp(scores - row_peak), -1, keepdims=True)))
    weights = low(jnp.exp(scores - log_total))
    mixed_heads = jnp.einsum('hqk,khd->qhd', weights, value_heads, precision=PRECISE)
    return low(low_back(mixed_heads.reshape(length, D)))

def self_block(inputs, ids_own, w_qkv, w_mix, bias_rows, gain_rows, causal):
    qkv_bias = jnp.concatenate([bias_rows[0], jnp.zeros_like(bias_rows[0]), bias_rows[1]])
    qkv_rows = low(low_back(dense_layer(low(inputs), w_qkv, qkv_bias)))
    queries, key_rows, value_rows = jnp.split(qkv_rows, 3, axis=-1)
    mixed = attend(queries, key_rows, value_rows, ids_own, ids_own, causal)
    branch = low_back(dense_layer(mixed, w_mix, bias_rows[2]))
    summed = inputs + branch
    return (norm_apply(summed, gain_rows[0], bias_rows[4]), summed, branch)

def cross_block(hidden, memory, ids_own, ids_source, w_query, w_pair, w_cross, cross_rows, cross_scale):
    queries = low(low_back(dense_layer(low(hidden), w_query, cross_rows[0])))
    pair_bias = jnp.concatenate([jnp.zeros_like(cross_rows[1]), cross_rows[1]])
    pair_rows = low(low_back(dense_layer(memory, w_pair, pair_bias)))
    key_rows, value_rows = jnp.split(pair_rows, 2, axis=-1)
    mixed = attend(queries, key_rows, value_rows, ids_own, ids_source, False)
    branch = low_back(dense_layer(mixed, w_cross, cross_rows[2]))
    return norm_apply(hidden + branch, cross_scale, cross_rows[3])

def ffn_block(middle, w_inner, b_inner, w_outer, bias_rows, gain_rows):
    inner_act = low_back(dense_layer(low(middle), w_inner, b_inner))
    activation = low(jax.nn.gelu(inner_act, approximate=False))
    branch = low_back(dense_layer(activation, w_outer, bias_rows[3]))
    return norm_apply(middle + branch, gain_rows[1], bias_rows[5])

def forward(params, x_src, x_tgt, ids_src, ids_tgt):

    def row_fn(params_row, src_row, tgt_row, src_ids, tgt_ids):
        attn_in, attn_out, attn_bias, gains, ffn_in, ffn_bias, ffn_out, cross_q, cross_kv, cross_out, cross_bias, cross_gain = params_row
        enc_hidden, enc_sum, enc_branch = self_block(src_row, src_ids, attn_in[0], attn_out[0], attn_bias[0], gains[0], False)
        enc_out = ffn_block(enc_hidden, ffn_in[0], ffn_bias[0], ffn_out[0], attn_bias[0], gains[0])
        memory = low(low_back(enc_out))
        dec_hidden, dec_sum, dec_branch = self_block(tgt_row, tgt_ids, attn_in[1], attn_out[1], attn_bias[1], gains[1], True)
        dec_middle = cross_block(dec_hidden, memory, tgt_ids, src_ids, cross_q, cross_kv, cross_out, cross_bias, cross_gain)
        dec_out = ffn_block(dec_middle, ffn_in[1], ffn_bias[1], ffn_out[1], attn_bias[1], gains[1])
        squares = jnp.stack([jnp.sum(enc_sum * enc_sum), jnp.sum(enc_branch * enc_branch), jnp.sum(dec_sum * dec_sum), jnp.sum(dec_branch * dec_branch)])
        return (enc_out, dec_out, squares)
    checked = jax.checkpoint(row_fn)

    def step_row(totals, row_items):
        enc_out, dec_out, squares = checked(params, row_items[0], row_items[1], row_items[2], row_items[3])
        return (totals + squares, (enc_out, dec_out))
    totals, (enc_all, dec_all) = lax.scan(step_row, jnp.zeros((4,), jnp.float32), (x_src, x_tgt, ids_src, ids_tgt))
    return ((enc_all, dec_all), totals)

def reference(x_in, segments, cotangent, attn_in, attn_out, attn_bias, gains, ffn_in, ffn_bias, ffn_out, cross_q, cross_kv, cross_out, cross_bias, cross_gain):
    row_total = MICRO * ROWS_MB
    x_src = x_in[0].astype(jnp.float32).reshape(row_total, SEQ_LEN, D)
    x_tgt = x_in[1].astype(jnp.float32).reshape(row_total, SEQ_LEN, D)
    ids_src = segments[0].reshape(row_total, SEQ_LEN)
    ids_tgt = segments[1].reshape(row_total, SEQ_LEN)
    params = tuple((weight.astype(jnp.float32) for weight in (attn_in, attn_out, attn_bias, gains, ffn_in, ffn_bias, ffn_out, cross_q, cross_kv, cross_out, cross_bias, cross_gain)))

    def whole(params_all, src_all, tgt_all):
        return forward(params_all, src_all, tgt_all, ids_src, ids_tgt)
    (enc_all, dec_all), back_fn, totals = jax.vjp(whole, params, x_src, x_tgt, has_aux=True)
    dec_cot = cotangent.astype(jnp.float32).reshape(row_total, SEQ_LEN, D)
    grad_params, grad_src, grad_tgt = back_fn((jnp.zeros_like(enc_all), dec_cot))
    layer_out = jnp.stack([enc_all, dec_all]).reshape(2, MICRO, ROWS_MB, SEQ_LEN, D).astype(jnp.bfloat16)
    input_grad = jnp.stack([grad_src, grad_tgt]).reshape(2, MICRO, ROWS_MB, SEQ_LEN, D).astype(jnp.bfloat16)
    count = MICRO * ROWS_MB * SEQ_LEN * D
    stats = jnp.sqrt(totals / count).reshape(2, 2)
    return (layer_out, input_grad, stats, grad_params[0], grad_params[1], grad_params[2], grad_params[3], grad_params[4], grad_params[5], grad_params[6], grad_params[7], grad_params[8], grad_params[9], grad_params[10], grad_params[11])
```

```python
from functools import partial
import math

import jax
import jax.numpy as jnp
from jax import lax
from jax.sharding import PartitionSpec as P

HEADS = 12
HEAD_DIM = 64


EPSILON = 1e-05
MASKED = -1000000000.0


def for_sending(x):
    return jax.tree.map(lambda a: a.astype(jnp.bfloat16) if a.dtype == jnp.float32 else a, x)


def from_behind(x, axis, by):
    length = lax.axis_size(axis)
    pairs = [(i, i + by) for i in range(length) if 0 <= i + by < length]
    return lax.ppermute(x, axis, pairs)


def norm_apply(tensor, scale_gain, offset):
    average = jnp.mean(tensor, -1, keepdims=True)
    centered = tensor - average
    spread = jnp.mean(centered * centered, -1, keepdims=True)
    return centered * lax.rsqrt(spread + EPSILON) * scale_gain + offset


def exact_gelu(tensor):
    return jax.nn.gelu(tensor, approximate=False)


def project(activation, weight, offset):
    return jnp.dot(activation, weight, preferred_element_type=jnp.float32) + offset


def project_back(gradient, weight):
    return jnp.einsum("rsj,ij->rsi", gradient, weight, preferred_element_type=jnp.float32)


def weight_grad(activation, gradient):
    return jnp.einsum("rsi,rsj->ij", activation, gradient, preferred_element_type=jnp.float32)


def column_total(gradient):
    return jnp.sum(gradient.astype(jnp.float32), axis=(0, 1))


def pick_row(stacked, position):
    return lax.dynamic_index_in_dim(stacked, position, 0, keepdims=False)


def masked_scores(queries, key_rows, ids_query, ids_key, query_pos, key_pos, causal):
    row_count, length = (queries.shape[0], queries.shape[1])
    key_count = key_rows.shape[1]
    query_heads = queries.reshape(row_count, length, HEADS, HEAD_DIM)
    key_heads = key_rows.reshape(row_count, key_count, HEADS, HEAD_DIM)
    raw_scores = jnp.einsum(
        "rqhd,rkhd->rhqk", query_heads, key_heads, preferred_element_type=jnp.float32
    ) * (1.0 / math.sqrt(HEAD_DIM))
    before = (key_pos[None, :] <= query_pos[:, None]) | jnp.logical_not(causal)
    allowed = (ids_query[:, :, None] == ids_key[:, None, :]) & before[None]
    return jnp.where(allowed[:, None], raw_scores, MASKED)


def attend_forward(queries, key_rows, value_rows, ids_query, ids_key, query_pos, causal):
    key_pos = jnp.arange(key_rows.shape[1])
    scores = masked_scores(queries, key_rows, ids_query, ids_key, query_pos, key_pos, causal)
    row_peak = jnp.max(scores, -1, keepdims=True)
    log_total = row_peak + jnp.log(jnp.sum(jnp.exp(scores - row_peak), -1, keepdims=True))
    weights = jnp.exp(scores - log_total).astype(jnp.bfloat16)
    row_count, length = (queries.shape[0], queries.shape[1])
    value_heads = value_rows.reshape(row_count, value_rows.shape[1], HEADS, HEAD_DIM)
    mixed_heads = jnp.einsum(
        "rhqk,rkhd->rqhd", weights, value_heads, preferred_element_type=jnp.float32
    )
    return (
        mixed_heads.reshape(row_count, length, HEADS * HEAD_DIM).astype(jnp.bfloat16),
        log_total,
    )


def attend_back(
    queries, key_rows, value_rows, mixed_grad, log_total, ids_query, ids_key, query_pos, causal
):
    key_pos = jnp.arange(key_rows.shape[1])
    scores = masked_scores(queries, key_rows, ids_query, ids_key, query_pos, key_pos, causal)
    prob_rows = jnp.exp(scores - log_total)
    row_count, length = (queries.shape[0], queries.shape[1])
    key_count = key_rows.shape[1]
    query_heads = queries.reshape(row_count, length, HEADS, HEAD_DIM)
    key_heads = key_rows.reshape(row_count, key_count, HEADS, HEAD_DIM)
    value_heads = value_rows.reshape(row_count, key_count, HEADS, HEAD_DIM)
    grad_heads = mixed_grad.reshape(row_count, length, HEADS, HEAD_DIM)
    prob_grad = jnp.einsum(
        "rqhd,rkhd->rhqk", grad_heads, value_heads, preferred_element_type=jnp.float32
    )
    score_grad = (
        prob_rows * (prob_grad - jnp.sum(prob_rows * prob_grad, -1, keepdims=True))
    ).astype(jnp.bfloat16)
    scale_factor = 1.0 / math.sqrt(HEAD_DIM)
    query_grad = (
        jnp.einsum("rhqk,rkhd->rqhd", score_grad, key_heads, preferred_element_type=jnp.float32)
        * scale_factor
    )
    key_grad = (
        jnp.einsum("rhqk,rqhd->rkhd", score_grad, query_heads, preferred_element_type=jnp.float32)
        * scale_factor
    )
    value_grad = jnp.einsum(
        "rhqk,rqhd->rkhd",
        prob_rows.astype(jnp.bfloat16),
        grad_heads,
        preferred_element_type=jnp.float32,
    )
    width = HEADS * HEAD_DIM
    return (
        query_grad.reshape(row_count, length, width),
        key_grad.reshape(row_count, key_count, width),
        value_grad.reshape(row_count, key_count, width),
    )


def share_keys(key_local, value_local):
    return (
        lax.all_gather(for_sending(key_local), "seq", axis=1, tiled=True).astype(key_local.dtype),
        lax.all_gather(for_sending(value_local), "seq", axis=1, tiled=True).astype(
            value_local.dtype
        ),
    )


def return_key_grads(key_term, value_term):
    return (
        lax.psum_scatter(
            key_term.astype(jnp.bfloat16), "seq", scatter_dimension=1, tiled=True
        ).astype(jnp.float32),
        lax.psum_scatter(
            value_term.astype(jnp.bfloat16), "seq", scatter_dimension=1, tiled=True
        ).astype(jnp.float32),
    )


def group_sum(parts, axis, members, stride, kind):
    length = lax.axis_size(axis)
    mine = (lax.axis_index(axis) // stride) % members
    total = pick_row(parts, mine).astype(jnp.float32)
    for step in range(1, members):
        pairs = []
        for i in range(length):
            at = (i // stride) % members
            pairs.append((i, i + ((at + step) % members - at) * stride))
        arrived = lax.ppermute(pick_row(parts, (mine + step) % members), axis, pairs)
        total = total + arrived.astype(jnp.float32)
    return total.astype(kind)


def scatter_sum(total):
    dp_size = lax.axis_size("dp")
    chips = lax.axis_size("seq") // 2
    rows = total.shape[0] // (dp_size * chips * 2)
    parts = jnp.moveaxis(total.reshape(dp_size, chips, 2, rows, *total.shape[1:]), 2, 0)
    parts = group_sum(parts, "seq", 2, 1, total.dtype)
    parts = group_sum(jnp.moveaxis(parts, 1, 0), "seq", chips, 2, total.dtype)
    return group_sum(parts, "dp", dp_size, 1, jnp.float32)


def section_half(total):
    parts = total.reshape(2, total.shape[0] // 2, *total.shape[1:])
    return group_sum(parts, "section", 2, 1, total.dtype)


def per_device(
    x_in,
    segments,
    cotangent,
    attn_in,
    attn_out,
    attn_bias,
    gains,
    ffn_in,
    ffn_bias,
    ffn_out,
    cross_q,
    cross_kv,
    cross_out,
    cross_bias,
    cross_gain,
):
    section = lax.axis_index("section")
    seq_index = lax.axis_index("seq")
    decoder = section.astype(jnp.float32)
    causal = section == 1
    micro = x_in.shape[1]
    row_count = x_in.shape[2]
    shard_len = x_in.shape[3]
    width = x_in.shape[4]
    query_pos = seq_index * shard_len + jnp.arange(shard_len)
    whole_ids = lax.all_gather(segments, "seq", axis=3, tiled=True)
    own_ids_all = lax.dynamic_index_in_dim(whole_ids, section, 0, keepdims=False)
    source_ids_all = whole_ids[0]
    local_ids_all = lax.dynamic_index_in_dim(segments, section, 0, keepdims=False)
    inputs_all = x_in[0]
    w_qkv = attn_in[0]
    w_mix = attn_out[0]
    bias_rows = attn_bias[0]
    gain_rows = gains[0]
    w_inner = ffn_in[0]
    b_inner = ffn_bias[0]
    w_outer = ffn_out[0]
    zeros_row = jnp.zeros_like(bias_rows[0])
    qkv_bias = jnp.concatenate([bias_rows[0], zeros_row, bias_rows[1]])
    pair_bias = jnp.concatenate([zeros_row, cross_bias[1]])

    def layer_forward(inputs, memory, ids_local, ids_own, ids_source):
        qkv_rows = project(inputs, w_qkv, qkv_bias).astype(jnp.bfloat16)
        queries, key_local, value_local = jnp.split(qkv_rows, 3, axis=-1)
        key_rows, value_rows = share_keys(key_local, value_local)
        mixed, log_self = attend_forward(
            queries, key_rows, value_rows, ids_local, ids_own, query_pos, causal
        )
        branch = project(mixed, w_mix, bias_rows[2])
        summed = inputs.astype(jnp.float32) + branch
        hidden = norm_apply(summed, gain_rows[0], bias_rows[4])
        cross_query = project(hidden.astype(jnp.bfloat16), cross_q, cross_bias[0]).astype(
            jnp.bfloat16
        )
        pair_rows = project(memory, cross_kv, pair_bias).astype(jnp.bfloat16)
        cross_key_local, cross_value_local = jnp.split(pair_rows, 2, axis=-1)
        cross_keys, cross_values = share_keys(cross_key_local, cross_value_local)
        cross_mixed, log_cross = attend_forward(
            cross_query, cross_keys, cross_values, ids_local, ids_source, query_pos, False
        )
        cross_branch = project(cross_mixed, cross_out, cross_bias[2])
        cross_sum = hidden + cross_branch
        cross_normed = norm_apply(cross_sum, cross_gain, cross_bias[3])
        middle = hidden + decoder * (cross_normed - hidden)
        inner_act = project(middle.astype(jnp.bfloat16), w_inner, b_inner)
        activation = exact_gelu(inner_act).astype(jnp.bfloat16)
        ffn_branch = project(activation, w_outer, bias_rows[3])
        final_sum = middle + ffn_branch
        result = norm_apply(final_sum, gain_rows[1], bias_rows[5])
        kept_tick = {
            "inputs": inputs,
            "queries": queries,
            "key_local": key_local,
            "value_local": value_local,
            "log_self": log_self,
            "mixed": mixed,
            "summed": summed,
            "hidden": hidden,
            "cross_query": cross_query,
            "memory": memory,
            "cross_key_local": cross_key_local,
            "cross_value_local": cross_value_local,
            "log_cross": log_cross,
            "cross_mixed": cross_mixed,
            "cross_sum": cross_sum,
            "middle": middle,
            "inner_act": inner_act,
            "activation": activation,
            "final_sum": final_sum,
        }
        kept_tick["key_rows"] = key_rows
        kept_tick["value_rows"] = value_rows
        kept_tick["cross_keys"] = cross_keys
        kept_tick["cross_values"] = cross_values
        squares = jnp.stack([jnp.sum(summed * summed), jnp.sum(branch * branch)])
        return (result, kept_tick, squares)

    def forward_tick(state_pair, tick_index):
        memory, square_sums = state_pair
        micro_index = tick_index - section
        is_valid = ((micro_index >= 0) & (micro_index < micro)).astype(jnp.float32)
        safe_index = jnp.clip(micro_index, 0, micro - 1)
        inputs = pick_row(inputs_all, safe_index)
        result, kept_tick, squares = layer_forward(
            inputs,
            memory,
            pick_row(local_ids_all, safe_index),
            pick_row(own_ids_all, safe_index),
            pick_row(source_ids_all, safe_index),
        )
        sent_rows = result.astype(jnp.bfloat16)
        arrived = from_behind(sent_rows, "section", 1)
        return ((arrived, square_sums + is_valid * squares), (sent_rows, kept_tick))

    start_state = (
        jnp.zeros((row_count, shard_len, width), jnp.bfloat16),
        jnp.zeros((2,), jnp.float32),
    )
    (_, square_sums), (outputs_all, kept_all) = lax.scan(
        forward_tick, start_state, jnp.arange(micro + 1)
    )

    def layer_backward(kept_tick, out_grad, ids_local, ids_own, ids_source):
        key_rows, value_rows = (kept_tick["key_rows"], kept_tick["value_rows"])
        cross_keys, cross_values = (kept_tick["cross_keys"], kept_tick["cross_values"])
        _, back_final = jax.vjp(norm_apply, kept_tick["final_sum"], gain_rows[1], bias_rows[5])
        final_grad, gain_final, shift_final = back_final(out_grad)
        ffn_grad = final_grad.astype(jnp.bfloat16)
        grad_outer = weight_grad(kept_tick["activation"], ffn_grad)
        grad_b2 = column_total(ffn_grad)
        act_grad = project_back(ffn_grad, w_outer)
        _, back_gelu = jax.vjp(exact_gelu, kept_tick["inner_act"])
        inner_grad = back_gelu(act_grad)[0].astype(jnp.bfloat16)
        grad_inner = weight_grad(kept_tick["middle"].astype(jnp.bfloat16), inner_grad)
        grad_b1 = column_total(inner_grad)
        middle_grad = final_grad + project_back(inner_grad, w_inner)
        normed_grad = decoder * middle_grad
        hidden_grad = middle_grad - normed_grad
        _, back_cross = jax.vjp(norm_apply, kept_tick["cross_sum"], cross_gain, cross_bias[3])
        cross_sum_grad, grad_cgain, grad_cshift = back_cross(normed_grad)
        hidden_grad = hidden_grad + cross_sum_grad
        cross_branch_grad = cross_sum_grad.astype(jnp.bfloat16)
        grad_cout = weight_grad(kept_tick["cross_mixed"], cross_branch_grad)
        grad_cbo = column_total(cross_branch_grad)
        cross_mixed_grad = project_back(cross_branch_grad, cross_out).astype(jnp.bfloat16)
        cq_grad, ck_term, cv_term = attend_back(
            kept_tick["cross_query"],
            cross_keys,
            cross_values,
            cross_mixed_grad,
            kept_tick["log_cross"],
            ids_local,
            ids_source,
            query_pos,
            False,
        )
        ck_grad, cv_grad = return_key_grads(ck_term, cv_term)
        pair_grad = jnp.concatenate([ck_grad, cv_grad], -1).astype(jnp.bfloat16)
        cq_grad = cq_grad.astype(jnp.bfloat16)
        grad_cq = weight_grad(kept_tick["hidden"].astype(jnp.bfloat16), cq_grad)
        grad_cbq = column_total(cq_grad)
        hidden_grad = hidden_grad + project_back(cq_grad, cross_q)
        grad_ckv = weight_grad(kept_tick["memory"], pair_grad)
        grad_cbv = column_total(pair_grad)[width:]
        memory_grad = project_back(pair_grad, cross_kv)
        _, back_first = jax.vjp(norm_apply, kept_tick["summed"], gain_rows[0], bias_rows[4])
        summed_grad, gain_first, shift_first = back_first(hidden_grad)
        branch_grad = summed_grad.astype(jnp.bfloat16)
        grad_mix = weight_grad(kept_tick["mixed"], branch_grad)
        grad_bo = column_total(branch_grad)
        mixed_grad = project_back(branch_grad, w_mix).astype(jnp.bfloat16)
        q_grad, k_term, v_term = attend_back(
            kept_tick["queries"],
            key_rows,
            value_rows,
            mixed_grad,
            kept_tick["log_self"],
            ids_local,
            ids_own,
            query_pos,
            causal,
        )
        k_grad, v_grad = return_key_grads(k_term, v_term)
        qkv_grad = jnp.concatenate([q_grad, k_grad, v_grad], -1).astype(jnp.bfloat16)
        grad_qkv = weight_grad(kept_tick["inputs"], qkv_grad)
        qkv_total = column_total(qkv_grad)
        input_grad = summed_grad + project_back(qkv_grad, w_qkv)
        bias_grad = jnp.stack(
            [qkv_total[:width], qkv_total[2 * width :], grad_bo, grad_b2, shift_first, shift_final]
        )
        gain_grad = jnp.stack([gain_first, gain_final])
        cross_bias_grad = jnp.stack([grad_cbq, grad_cbv, grad_cbo, grad_cshift])
        grads = (
            grad_qkv,
            grad_mix,
            bias_grad,
            gain_grad,
            grad_inner,
            grad_b1,
            grad_outer,
            grad_cq,
            grad_ckv,
            grad_cout,
            cross_bias_grad,
            grad_cgain,
        )
        return (input_grad, memory_grad, grads)

    def backward_tick(state_pair, tick_index):
        arrived, totals = state_pair
        micro_index = tick_index - 1 + section
        is_valid = ((micro_index >= 0) & (micro_index < micro)).astype(jnp.float32)
        safe_index = jnp.clip(micro_index, 0, micro - 1)
        saved_at = jnp.clip(micro_index + section, 0, micro)
        kept_tick = jax.tree.map(partial(pick_row, position=saved_at), kept_all)
        from_cotangent = pick_row(cotangent, safe_index).astype(jnp.float32)
        out_grad = jnp.where(causal, from_cotangent, arrived.astype(jnp.float32)) * is_valid
        input_grad, memory_grad, grads = layer_backward(
            kept_tick,
            out_grad,
            pick_row(local_ids_all, safe_index),
            pick_row(own_ids_all, safe_index),
            pick_row(source_ids_all, safe_index),
        )
        sent_grad = memory_grad.astype(jnp.bfloat16)
        returned = from_behind(sent_grad, "section", -1)
        return ((returned, jax.tree.map(jnp.add, totals, grads)), input_grad.astype(jnp.bfloat16))

    grad_zeros = (
        jnp.zeros(w_qkv.shape, jnp.float32),
        jnp.zeros(w_mix.shape, jnp.float32),
        jnp.zeros((6, width), jnp.float32),
        jnp.zeros((2, width), jnp.float32),
        jnp.zeros(w_inner.shape, jnp.float32),
        jnp.zeros(b_inner.shape, jnp.float32),
        jnp.zeros(w_outer.shape, jnp.float32),
        jnp.zeros(cross_q.shape, jnp.float32),
        jnp.zeros(cross_kv.shape, jnp.float32),
        jnp.zeros(cross_out.shape, jnp.float32),
        jnp.zeros((4, width), jnp.float32),
        jnp.zeros((width,), jnp.float32),
    )
    back_start = (jnp.zeros((row_count, shard_len, width), jnp.bfloat16), grad_zeros)
    (_, totals), grads_in = lax.scan(backward_tick, back_start, jnp.arange(micro + 1))
    low = jnp.bfloat16
    ffn_in_part = scatter_sum(totals[4].astype(low))
    ffn_out_part = scatter_sum(totals[6].astype(low))
    attn_in_part = scatter_sum(totals[0].astype(low))
    attn_out_part = scatter_sum(totals[1].astype(low))
    cross_part = scatter_sum(
        section_half(jnp.concatenate([totals[7], totals[8], totals[9]], -1).astype(low))
    )
    blocks = lax.axis_size("dp") * lax.axis_size("seq")
    cross_small = section_half(jnp.concatenate([totals[10], totals[11][None]], 0).T)
    small = jnp.concatenate(
        [
            jnp.concatenate([totals[2], totals[3]], 0).T.reshape(blocks, -1),
            totals[5].reshape(blocks, -1),
            cross_small.reshape(blocks, -1),
            jnp.broadcast_to(square_sums[None], (blocks, 2)),
        ],
        -1,
    )
    small = scatter_sum(small)[0]
    per = width // blocks
    half = per // 2
    section_small = small[: 8 * per].reshape(per, 8).T
    ffn_bias_part = small[8 * per : 8 * per + b_inner.shape[0] // blocks]
    rest = small[8 * per + b_inner.shape[0] // blocks :]
    cross_rows = rest[: 5 * half].reshape(half, 5).T
    moments = rest[5 * half :]
    count = micro * row_count * lax.axis_size("dp") * shard_len * lax.axis_size("seq") * width
    stats = jnp.sqrt(moments / count)[None]
    layer_out = lax.dynamic_slice_in_dim(outputs_all, section, micro, 0)[None]
    input_grad = lax.dynamic_slice_in_dim(grads_in, 1 - section, micro, 0)[None]
    return (
        layer_out,
        input_grad,
        stats,
        attn_in_part[None],
        attn_out_part[None],
        section_small[None, :6],
        section_small[None, 6:],
        ffn_in_part[None],
        ffn_bias_part[None],
        ffn_out_part[None],
        cross_part[:, :width],
        cross_part[:, width : 3 * width],
        cross_part[:, 3 * width :],
        cross_rows[:4],
        cross_rows[4],
    )


def solution(mesh):
    return jax.shard_map(
        per_device,
        mesh=mesh,
        in_specs=(
            P("section", None, "dp", "seq", None),
            P(None, None, "dp", "seq"),
            P(None, "dp", "seq", None),
            P("section", None, None),
            P("section", None, None),
            P("section", None, None),
            P("section", None, None),
            P("section", None, None),
            P("section", None),
            P("section", None, None),
            P(),
            P(),
            P(),
            P(),
            P(),
        ),
        out_specs=(
            P("section", None, "dp", "seq", None),
            P("section", None, "dp", "seq", None),
            P("section", None),
            P("section", ("dp", "seq"), None),
            P("section", ("dp", "seq"), None),
            P("section", None, ("dp", "seq")),
            P("section", None, ("dp", "seq")),
            P("section", ("dp", "seq"), None),
            P("section", ("dp", "seq")),
            P("section", ("dp", "seq"), None),
            P(("section", "dp", "seq"), None),
            P(("section", "dp", "seq"), None),
            P(("section", "dp", "seq"), None),
            P(None, ("section", "dp", "seq")),
            P(("section", "dp", "seq")),
        ),
        check_vma=False,
    )
```

```python
import functools
import math

import jax
import jax.numpy as jnp
from jax import lax
from jax.experimental import pallas as pl
from jax.experimental.pallas import tpu as pltpu
from jax.sharding import PartitionSpec as P

HEADS = 12
HEAD_DIM = 64
PAIR = 2 * HEAD_DIM
LSE_ROWS = 16
EPSILON = 1e-05
MASKED = -1000000000.0
SCALE = 1.0 / math.sqrt(HEAD_DIM)
VMEM_LIMIT = 40 * 1024 * 1024

F32 = jnp.float32
BF16 = jnp.bfloat16


def mm(a, b):
    return jnp.dot(a, b, preferred_element_type=F32)


def mm_nt(a, b):
    return lax.dot_general(a, b, (((1,), (1,)), ((), ())), preferred_element_type=F32)


def norm_parts(tensor):
    average = jnp.mean(tensor, -1, keepdims=True)
    centered = tensor - average
    spread = jnp.mean(centered * centered, -1, keepdims=True)
    scale = lax.rsqrt(spread + EPSILON)
    return centered * scale, scale


def norm_back(tensor, gain, grad):
    normed, scale = norm_parts(tensor)
    scaled = gain * grad
    product = grad * normed
    first = jnp.mean(scaled, -1, keepdims=True)
    second = jnp.mean(scaled * normed, -1, keepdims=True)
    out = (scaled - first - normed * second) * scale
    return out, jnp.sum(product, 0, keepdims=True), jnp.sum(grad, 0, keepdims=True)


def column_sum(tensor):
    return jnp.sum(tensor.astype(F32), 0, keepdims=True)


def gelu_pair(x):
    bell = jnp.exp(-0.5 * x * x)
    t = 1.0 / (1.0 + (0.3275911 / math.sqrt(2.0)) * jnp.abs(x))
    poly = t * (
        0.5 * 0.254829592
        + t
        * (
            0.5 * -0.284496736
            + t * (0.5 * 1.421413741 + t * (0.5 * -1.453152027 + t * (0.5 * 1.061405429)))
        )
    )
    tail = poly * bell
    cdf = jnp.where(x < 0, tail, 1.0 - tail)
    return x * cdf, cdf + x * bell * (1.0 / math.sqrt(2.0 * math.pi))


def row_blocks(count, body):
    step = min(256, count)

    def run(i, carry):
        body(pl.ds(pl.multiple_of(i * step, step), step))
        return carry

    lax.fori_loop(0, count // step, run, 0)


def head_halves(rows):
    lane = lax.broadcasted_iota(jnp.int32, (rows, PAIR), 1)
    return lane < HEAD_DIM, lane >= HEAD_DIM


def attend_forward(q_ref, k_ref, v_ref, bias_ref, mixed_ref, lse_ref):
    length = q_ref.shape[0]
    lse_ref[...] = jnp.zeros_like(lse_ref)

    def pair(p, carry):
        lanes = pl.ds(pl.multiple_of(p * PAIR, PAIR), PAIR)
        keys = k_ref[:, lanes]
        values_t = v_ref[:, lanes].T
        queries = q_ref[:, lanes] * SCALE
        outs = []
        for a, half in enumerate(head_halves(length)):
            own = jnp.where(half, queries, jnp.zeros_like(queries))
            scores = mm_nt(keys, own) + bias_ref[...]
            peak = jnp.max(scores, 0, keepdims=True)
            weights = jnp.exp(scores - peak)
            total = jnp.sum(weights, 0, keepdims=True)
            lse_ref[pl.ds(2 * p + a, 1), :] = peak + jnp.log(total)
            out = mm(values_t, weights.astype(BF16))
            outs.append(out[a * HEAD_DIM : (a + 1) * HEAD_DIM] * (1.0 / total))
        mixed_ref[:, lanes] = jnp.concatenate(outs, 0).T.astype(BF16)
        return carry

    lax.fori_loop(0, HEADS // 2, pair, 0)


def attend_back(q_ref, k_ref, v_ref, grad_ref, lse_ref, delta_ref, bias_ref, dq_ref, dkv_ref):
    length, width = q_ref.shape

    def pair(p, carry):
        lanes = pl.ds(pl.multiple_of(p * PAIR, PAIR), PAIR)
        value_lanes = pl.ds(pl.multiple_of(width + p * PAIR, PAIR), PAIR)
        keys = k_ref[:, lanes]
        values = v_ref[:, lanes]
        keys_t = keys.T
        queries = q_ref[:, lanes] * SCALE
        grads = grad_ref[:, lanes]
        key_grad = value_grad = None
        outs = []
        for a, half in enumerate(head_halves(length)):
            own = jnp.where(half, queries, jnp.zeros_like(queries))
            own_grad = jnp.where(half, grads, jnp.zeros_like(grads))
            lse = lse_ref[pl.ds(2 * p + a, 1), :]
            delta = delta_ref[pl.ds(2 * p + a, 1), :]
            weights = jnp.exp(mm_nt(keys, own) + bias_ref[...] - lse)
            weight_grad = mm_nt(values, own_grad)
            score_grad = (weights * (weight_grad - delta)).astype(BF16)
            value_term = mm(weights.astype(BF16), own_grad)
            key_term = mm(score_grad, own)
            value_grad = value_term if value_grad is None else value_grad + value_term
            key_grad = key_term if key_grad is None else key_grad + key_term
            out = mm(keys_t, score_grad)
            outs.append(out[a * HEAD_DIM : (a + 1) * HEAD_DIM] * SCALE)
        dkv_ref[:, lanes] = key_grad.astype(BF16)
        dkv_ref[:, value_lanes] = value_grad.astype(BF16)
        dq_ref[:, lanes] = jnp.concatenate(outs, 0).T.astype(BF16)
        return carry

    lax.fori_loop(0, HEADS // 2, pair, 0)


def head_dots(first, second):
    product = first.astype(F32) * second.astype(F32)
    width = product.shape[1]
    row = lax.broadcasted_iota(jnp.int32, (LSE_ROWS, width), 0)
    column = lax.broadcasted_iota(jnp.int32, (LSE_ROWS, width), 1)
    select = (column // HEAD_DIM == row).astype(F32)
    return lax.dot_general(
        select,
        product,
        (((1,), (1,)), ((), ())),
        precision=lax.Precision.HIGHEST,
        preferred_element_type=F32,
    )


def self_kernel(io, x_ref, w_qkv, w_mix, vec, bias, q_out, k_out, v_out, mixed, lse, summed, hidden, squares):
    length, width = q_out.shape
    io.ready(x_ref, w_qkv, vec)
    x_own = x_ref[0:length, :]
    q_out[...] = (mm(x_own, w_qkv[:, 0:width]) + vec[0:1, :]).astype(BF16)

    def keys(rows):
        x = x_ref[rows, :]
        k_out[rows, :] = mm(x, w_qkv[:, width : 2 * width]).astype(BF16)
        v_out[rows, :] = (mm(x, w_qkv[:, 2 * width : 3 * width]) + vec[1:2, :]).astype(BF16)

    row_blocks(x_ref.shape[0], keys)
    io.done(q_out, k_out, v_out)
    io.ready(bias)
    attend_forward(q_out, k_out, v_out, bias, mixed, lse)
    io.done(mixed, lse)
    io.ready(w_mix)
    branch = mm(mixed[...], w_mix[...]) + vec[2:3, :]
    total = x_own.astype(F32) + branch
    summed[...] = total
    squares[...] = jnp.zeros_like(squares)
    squares[0:1, :] = column_sum(total * total)
    squares[1:2, :] = column_sum(branch * branch)
    hidden[...] = norm_parts(total)[0] * vec[6:7, :] + vec[4:5, :]


def ffn_kernel(io, middle, vec, w_in, b_in, w_out, act, slope, final_sum, low_middle, result):
    width = middle.shape[1]
    chunks = w_in.shape[1] // width
    io.ready(middle, vec)
    mid = middle[...]
    low = mid.astype(BF16)
    low_middle[...] = low
    final_sum[...] = mid + vec[3:4, :]
    io.ready(w_in, b_in, w_out)

    def chunk(j, carry):
        columns = pl.ds(pl.multiple_of(j * width, width), width)
        inner = mm(low, w_in[:, columns]) + b_in[:, columns]
        value, derivative = gelu_pair(inner)
        value = value.astype(BF16)
        act[:, columns] = value
        slope[:, columns] = derivative.astype(BF16)
        final_sum[...] += mm(value, w_out[columns, :])
        return carry

    lax.fori_loop(0, chunks, chunk, 0)
    io.done(act, slope, low_middle, final_sum)
    result[...] = (norm_parts(final_sum[...])[0] * vec[7:8, :] + vec[5:6, :]).astype(BF16)


def ffn_back_kernel(io, grad, final_sum, vec, w_out, slope, w_in, dy, d_inner, d_middle, small):
    width = grad.shape[1]
    chunks = w_in.shape[1] // width
    io.ready(grad, final_sum, vec)
    d_final, d_gain, d_shift = norm_back(final_sum[...], vec[7:8, :], grad[...].astype(F32))
    low = d_final.astype(BF16)
    dy[...] = low
    small[...] = jnp.zeros_like(small)
    small[0:1, :] = d_gain
    small[1:2, :] = d_shift
    small[2:3, :] = column_sum(low)
    d_middle[...] = d_final
    io.done(dy)
    io.ready(w_out, slope, w_in)

    def chunk(j, carry):
        columns = pl.ds(pl.multiple_of(j * width, width), width)
        d_act = mm_nt(low, w_out[columns, :])
        inner = (d_act * slope[:, columns].astype(F32)).astype(BF16)
        d_inner[:, columns] = inner
        small[pl.ds(3 + j, 1), :] = column_sum(inner)
        d_middle[...] += mm_nt(inner, w_in[:, columns])
        return carry

    lax.fori_loop(0, chunks, chunk, 0)


def cross_kernel(
    io, hidden, w_q, vec, memory, w_kv, bias, w_o,
    cq, ck, cv, mixed, lse, summed, middle, low_hidden,
):
    width = hidden.shape[1]
    io.ready(hidden, w_q, vec)
    low = hidden[...].astype(BF16)
    low_hidden[...] = low
    cq[...] = (mm(low, w_q[...]) + vec[0:1, :]).astype(BF16)
    io.ready(memory, w_kv)

    def keys(rows):
        mem = memory[rows, :]
        ck[rows, :] = mm(mem, w_kv[:, 0:width]).astype(BF16)
        cv[rows, :] = (mm(mem, w_kv[:, width : 2 * width]) + vec[1:2, :]).astype(BF16)

    row_blocks(memory.shape[0], keys)
    io.done(cq, ck, cv, low_hidden)
    io.ready(bias)
    attend_forward(cq, ck, cv, bias, mixed, lse)
    io.done(mixed, lse)
    io.ready(w_o)
    total = hidden[...] + mm(mixed[...], w_o[...]) + vec[2:3, :]
    summed[...] = total
    middle[...] = norm_parts(total)[0] * vec[4:5, :] + vec[3:4, :]


def cross_back_kernel(
    io, d_middle, summed, vec, w_o, mixed, cq, ck, bias, lse, cv, w_q, w_kv,
    dyc, dcq, dckv, d_hidden, keep, send, small, d_mixed, delta,
):
    length, width = d_middle.shape
    io.ready(d_middle, summed, vec)
    d_cross, d_gain, d_shift = norm_back(summed[...], vec[4:5, :], d_middle[...])
    low = d_cross.astype(BF16)
    dyc[...] = low
    d_hidden[...] = d_cross
    io.ready(w_o, mixed)
    grads = mm_nt(low, w_o[...]).astype(BF16)
    d_mixed[...] = grads
    delta[...] = head_dots(grads, mixed[...])
    io.ready(cq, ck, bias, lse, cv)
    attend_back(cq, ck, cv, d_mixed, lse, delta, bias, dcq, dckv)
    io.ready(w_q, w_kv)
    for block in range(dckv.shape[0] // length):
        target = keep if block % 2 == 0 else send
        rows = slice(block // 2 * length, (block // 2 + 1) * length)
        target[rows, :] = mm_nt(dckv[block * length : (block + 1) * length, :], w_kv[...]).astype(BF16)
    io.done(send, keep, dyc, dcq, dckv)
    d_hidden[...] += mm_nt(dcq[...], w_q[...])
    small[...] = jnp.zeros_like(small)
    small[0:1, :] = d_gain
    small[1:2, :] = d_shift
    small[2:3, :] = column_sum(low)
    small[3:4, :] = column_sum(dcq[...])
    small[4:5, :] = column_sum(dckv[:, width : 2 * width])


def self_back_kernel(
    io, d_middle, d_hidden, summed, vec, w_mix, mixed, q, k, bias, lse, v, w_qkv,
    dy, dq, dkv, own, keep, send, small, d_mixed, delta,
):
    length, width = q.shape
    io.ready(d_middle, d_hidden, summed, vec)
    grad = jnp.where(io.section() == 0, d_middle[...], d_hidden[...])
    d_sum, d_gain, d_shift = norm_back(summed[...], vec[6:7, :], grad)
    low = d_sum.astype(BF16)
    dy[...] = low
    own[...] = d_sum
    io.ready(w_mix, mixed)
    grads = mm_nt(low, w_mix[...]).astype(BF16)
    d_mixed[...] = grads
    delta[...] = head_dots(grads, mixed[...])
    io.ready(q, k, bias, lse, v)
    attend_back(q, k, v, d_mixed, lse, delta, bias, dq, dkv)
    io.done(dy, dq, dkv)
    io.ready(w_qkv)
    for block in range(dkv.shape[0] // length):
        part = mm_nt(dkv[block * length : (block + 1) * length, :], w_qkv[:, width : 3 * width])
        if block == 0:
            own[...] += part + mm_nt(dq[...], w_qkv[:, 0:width])
            continue
        target = keep if block % 2 == 0 else send
        at = (block - 2) // 2 if block % 2 == 0 else block // 2
        target[at * length : (at + 1) * length, :] = part.astype(BF16)
    io.done(send, keep, own)
    small[...] = jnp.zeros_like(small)
    small[0:1, :] = d_gain
    small[1:2, :] = d_shift
    small[2:3, :] = column_sum(low)
    small[3:4, :] = column_sum(dq[...])
    small[4:5, :] = column_sum(dkv[:, width : 2 * width])


def weight_kernel(plan, io, *refs):
    out = refs[-1]
    for lefts, rights, column in plan:
        inner = refs[lefts[0]].shape[1]
        cols = refs[rights[0]].shape[1]
        step = 256
        wide = min(cols, 1536)
        io.ready(*[refs[i] for i in lefts + rights])

        def tile(i, carry, lefts=lefts, rights=rights, column=column, cols=cols, wide=wide):
            rows = pl.ds(pl.multiple_of(i * step, step), step)
            turned = [refs[l][:, rows].T for l in lefts]
            for start in range(0, cols, wide):
                total = None
                for left, r in zip(turned, rights):
                    term = mm(left, refs[r][:, start : start + wide])
                    total = term if total is None else total + term
                out[rows, column + start : column + start + wide] = total.astype(BF16)
            return carry

        lax.fori_loop(0, inner // step, tile, 0)


def sum_kernel(terms, io, *refs):
    n_out = 1 + max(t[0] for t in terms)
    outs = refs[len(refs) - n_out :]
    io.ready(*refs[: len(refs) - n_out])
    for which, (first, first_row), (second, second_row) in terms:
        out = outs[which]
        rows = out.shape[0]
        one = refs[first][first_row : first_row + rows, :].astype(F32)
        two = refs[second][second_row : second_row + rows, :].astype(F32)
        out[...] = (one + two).astype(out.dtype)
        io.done(out)


class Moves:
    def __init__(self, section, loads, stores):
        self.section_ref, self.loads, self.stores, self.started = section, dict(loads), dict(stores), set()
        self.waited = set()
        for copies in self.loads.values():
            for copy in copies:
                copy.start()

    def section(self):
        return self.section_ref[0]

    def ready(self, *refs):
        for ref in refs:
            if id(ref) not in self.waited:
                self.waited.add(id(ref))
                for copy in self.loads[id(ref)]:
                    copy.wait()

    def done(self, *refs):
        for ref in refs:
            if id(ref) not in self.started:
                self.started.add(id(ref))
                self.stores[id(ref)].start()

    def finish(self, ins, outs):
        self.ready(*ins)
        self.done(*outs)
        for copy in self.stores.values():
            copy.wait()


def call(kernel, outs, operands, *, chain, section, flops, scratch=(), role=None, into=()):
    groups = [list(o) if isinstance(o, (list, tuple)) else [o] for o in operands]
    flat = [a for g in groups for a in g]
    n_in, n_flat, n_out = len(groups), len(flat), len(outs)
    after = [chain[-1]] if chain else []
    n_rest = len(into) + len(after)

    def body(section_ref, *refs):
        hbm_in = refs[:n_flat]
        refs = refs[n_flat + n_rest :]
        hbm_out = refs[:n_out]
        refs = refs[n_out + 1 :]
        ins, vmem_out, rest = refs[:n_in], refs[n_in : n_in + n_out], refs[n_in + n_out :]
        in_sem, out_sem, extra = rest[0], rest[1], rest[2:]

        def run():
            loads, at = [], 0
            for ref, group in zip(ins, groups):
                copies, row = [], 0
                for array in group:
                    target = ref
                    if len(group) > 1:
                        target = ref.at[row : row + array.shape[0]]
                        row += array.shape[0]
                    copies.append(pltpu.make_async_copy(hbm_in[at], target, in_sem.at[at]))
                    at += 1
                loads.append((id(ref), copies))
            stores = [
                (id(ref), pltpu.make_async_copy(ref, hbm_out[i], out_sem.at[i]))
                for i, ref in enumerate(vmem_out)
            ]
            moves = Moves(section_ref, loads, stores)
            kernel(moves, *ins, *vmem_out, *extra)
            moves.finish(ins, vmem_out)

        if role is None:
            run()
        else:
            pl.when(section_ref[0] == role)(run)

    anywhere = pl.BlockSpec(memory_space=pl.ANY)
    in_shapes = [
        pltpu.VMEM((sum(a.shape[0] for a in g), *g[0].shape[1:]), g[0].dtype) for g in groups
    ]
    out_shapes = [pltpu.VMEM(o.shape, o.dtype) for o in outs]
    size = sum(math.prod(o.shape) * o.dtype.itemsize for o in list(outs) + flat)
    results = pl.pallas_call(
        body,
        out_shape=[*outs, jax.ShapeDtypeStruct((8, 128), F32)],
        in_specs=[pl.BlockSpec(memory_space=pltpu.SMEM)] + [anywhere] * (n_flat + n_rest),
        out_specs=[anywhere] * (n_out + 1),
        scratch_shapes=in_shapes
        + out_shapes
        + [pltpu.SemaphoreType.DMA((n_flat,)), pltpu.SemaphoreType.DMA((n_out,))]
        + list(scratch),
        input_output_aliases={1 + n_flat + i: i for i in range(len(into))},
        cost_estimate=pl.CostEstimate(flops=int(flops), bytes_accessed=int(size), transcendentals=0),
        compiler_params=pltpu.CompilerParams(vmem_limit_bytes=VMEM_LIMIT),
        name=getattr(kernel, "func", kernel).__name__,
    )(section, *flat, *into, *after)
    chain.append(results[-1])
    return results[:-1]


def shaped(*shape, kind=F32):
    return jax.ShapeDtypeStruct(shape, kind)


def pick(stacked, position):
    return lax.dynamic_index_in_dim(stacked, position, 0, keepdims=False)


def group_sum(parts, axis, members, stride, kind):
    length = lax.axis_size(axis)
    mine = (lax.axis_index(axis) // stride) % members
    total = pick(parts, mine).astype(F32)
    for step in range(1, members):
        pairs = []
        for i in range(length):
            at = (i // stride) % members
            pairs.append((i, i + ((at + step) % members - at) * stride))
        arrived = lax.ppermute(pick(parts, (mine + step) % members), axis, pairs)
        total = total + arrived.astype(F32)
    return total.astype(kind)


def scatter_sum(total):
    dp_size = lax.axis_size("dp")
    chips = lax.axis_size("seq") // 2
    rows = total.shape[0] // (dp_size * chips * 2)
    parts = jnp.moveaxis(total.reshape(dp_size, chips, 2, rows, *total.shape[1:]), 2, 0)
    parts = group_sum(parts, "seq", 2, 1, total.dtype)
    parts = group_sum(jnp.moveaxis(parts, 1, 0), "seq", chips, 2, total.dtype)
    return group_sum(parts, "dp", dp_size, 1, F32)


def to_encoder_half(total, section):
    half = total.shape[0] // 2
    arrived = lax.ppermute(total[:half], "section", [(1, 0)])
    return jnp.where(section == 0, arrived, total[half:])


def twin(x):
    return lax.ppermute(x, "seq", [(i, i ^ 1) for i in range(lax.axis_size("seq"))])


def chip_shift(x, step):
    length = lax.axis_size("seq")
    return lax.ppermute(x, "seq", [(i, (i + 2 * step) % length) for i in range(length)])


def row_gather(x):
    blocks = [x, twin(x)]
    for step in range(1, lax.axis_size("seq") // 2):
        far = chip_shift(x, -step)
        blocks += [far, twin(far)]
    return blocks


def shard_order():
    me = lax.axis_index("seq")
    length = lax.axis_size("seq")
    order = []
    for step in range(length // 2):
        far = (me + 2 * step) % length
        order += [far, far ^ 1]
    return order


def per_device(
    x_in, segments, cotangent, attn_in, attn_out, attn_bias, gains, ffn_in, ffn_bias, ffn_out,
    cross_q, cross_kv, cross_out, cross_bias, cross_gain,
):
    section = lax.axis_index("section")
    sec = section.astype(jnp.int32).reshape(1)
    micro, length, width = x_in.shape[1], x_in.shape[3], x_in.shape[4]
    seq_size = lax.axis_size("seq")
    tokens = length * seq_size
    hidden_units = ffn_in.shape[2]
    w_qkv, w_mix, w_in, w_out = attn_in[0], attn_out[0], ffn_in[0], ffn_out[0]
    b_in = ffn_bias
    vec = jnp.concatenate([attn_bias[0], gains[0]], 0)
    cross_vec = jnp.concatenate([cross_bias, cross_gain[None], jnp.zeros((3, width), F32)], 0)

    order = shard_order()
    place = jnp.arange(length, dtype=jnp.int32)
    key_place = jnp.concatenate([o * length + place for o in order])
    query_place = order[0] * length + place
    ids = jnp.moveaxis(segments[:, :, 0], 2, 0)
    all_ids = jnp.concatenate(row_gather(ids), 0)

    def allowed_bias(key_ids, query_ids, ordered):
        same = key_ids[:, None] == query_ids[None, :]
        before = (key_place[:, None] <= query_place[None, :]) | jnp.logical_not(ordered)
        return jnp.where(same & before, 0.0, MASKED).astype(F32)

    ticks = range(micro)
    last = micro - 1
    own_ids = pick(jnp.moveaxis(all_ids, 1, 0), section)
    own_queries = own_ids[:length]
    self_bias = [allowed_bias(own_ids[:, m], own_queries[:, m], section == 1) for m in ticks]
    cross_bias_of = [allowed_bias(all_ids[:, 0, m], own_queries[:, m], False) for m in ticks]

    attend_flops = 4 * length * tokens * width
    kv_flops = 4 * tokens * width * width
    square = 2 * length * width * width
    ffn_flops = 4 * length * width * hidden_units
    lw = shaped(length, width)
    lw_low = shaped(length, width, kind=BF16)
    tw_low = shaped(tokens, width, kind=BF16)
    lh_low = shaped(length, hidden_units, kind=BF16)
    pair_low = shaped(tokens, 2 * width, kind=BF16)
    half_low = shaped(tokens // 2, width, kind=BF16)
    rest_low = shaped(tokens // 2 - length, width, kind=BF16)
    lse_shape = shaped(LSE_ROWS, length)
    few = shaped(8, width)
    back_scratch = [pltpu.VMEM((length, width), BF16), pltpu.VMEM((LSE_ROWS, length), F32)]
    chips = seq_size // 2
    chain = []
    run = functools.partial(call, chain=chain, section=sec)

    def run_self(m):
        return run(
            self_kernel,
            [lw_low, tw_low, tw_low, lw_low, lse_shape, lw, lw, few],
            [x_all[m], w_qkv, w_mix, vec, self_bias[m]],
            flops=attend_flops + kv_flops + 2 * square,
        )

    def run_ffn(middle, role, into=()):
        return run(
            ffn_kernel,
            [lh_low, lh_low, lw, lw_low, lw_low],
            [middle, vec, w_in, b_in, w_out],
            flops=ffn_flops,
            role=role,
            into=into,
        )

    def run_ffn_back(grad, forward, role, into=()):
        return run(
            ffn_back_kernel,
            [lw_low, lh_low, lw, few],
            [grad, forward[2], vec, w_out, forward[1], w_in],
            flops=ffn_flops,
            role=role,
            into=into,
        )

    def run_cross(m):
        return run(
            cross_kernel,
            [lw_low, tw_low, tw_low, lw_low, lse_shape, lw, lw, lw_low],
            [selfs[m][6], cross_q, cross_vec, memory[m], cross_kv, cross_bias_of[m], cross_out],
            flops=attend_flops + kv_flops + 2 * square,
            role=1,
        )

    def run_cross_back(m):
        c = crosses[m]
        return run(
            cross_back_kernel,
            [lw_low, lw_low, pair_low, lw, half_low, half_low, few],
            [back[m][2], c[5], cross_vec, cross_out, c[3], c[0], c[1], cross_bias_of[m], c[4], c[2], cross_q, cross_kv],
            flops=3 * attend_flops + kv_flops + 2 * square,
            scratch=back_scratch,
            role=1,
        )

    def run_self_back(m, role, into=()):
        s = selfs[m]
        return run(
            self_back_kernel,
            [lw_low, lw_low, pair_low, lw, rest_low, half_low, few],
            [back[m][2], cross_back[m][3], s[5], vec, w_mix, s[3], s[0], s[1], self_bias[m], s[4], s[2], w_qkv],
            flops=3 * attend_flops + kv_flops + 2 * square,
            scratch=back_scratch,
            role=role,
            into=into,
        )

    def run_weights(products, out, role=None):
        operands, plan, flops = [], [], 0
        for lefts, rights, column in products:
            n, k = len(operands), len(lefts)
            operands += list(lefts) + list(rights)
            plan.append((tuple(range(n, n + k)), tuple(range(n + k, n + 2 * k)), column))
            rows = rights[0].shape[0]
            flops += 2 * k * rows * out.shape[0] * rights[0].shape[1]
        return run(functools.partial(weight_kernel, plan), [out], operands, flops=flops, role=role)[0]

    def run_sum(terms, outs, operands, role=None):
        return run(functools.partial(sum_kernel, terms), outs, operands, flops=0, role=role)

    def core_sums(keep, arrived, first, own_kind, role=None):
        operands = [keep, arrived] if first is None else [first, arrived, keep]
        terms, outs = [], []
        for step in range(chips):
            if first is None:
                mine = (0, step * length)
            else:
                mine = (0, 0) if step == 0 else (2, (step - 1) * length)
            terms.append((step, mine, (1, step * length)))
            outs.append(shaped(length, width, kind=own_kind if step == 0 else BF16))
        return run_sum(terms, outs, operands, role)

    def chip_sums(parts, kind, role=None):
        total = parts[0]
        for step in range(1, chips):
            out = shaped(length, width, kind=kind if step == chips - 1 else F32)
            total = run_sum([(0, (0, 0), (1, 0))], [out], [total, chip_shift(parts[step], step)], role)[0]
        return total

    x_all, selfs, enc_ffn, memory = [], [], [], []
    for m in ticks:
        x_all.append(row_gather(x_in[0, m, 0]))
        selfs.append(run_self(m))
        enc_ffn.append(run_ffn(selfs[m][6], 0))
        memory.append(row_gather(lax.ppermute(enc_ffn[m][4], "section", [(0, 1)])))

    ffn, back, crosses, cross_back, memory_grad, self_back = [], [], [], [], [], []

    def encoder_back(m):
        back[m] = run_ffn_back(memory_grad[m], ffn[m], 0, back[m])

    parts = None
    for m in ticks:
        crosses.append(run_cross(m))
        if parts is not None:
            parts = core_sums(cross_back[m - 1][4], twin(cross_back[m - 1][5]), None, F32, 1)
        ffn.append(run_ffn(crosses[m][6], 1, enc_ffn[m][:4]))
        back.append(run_ffn_back(cotangent[m, 0], ffn[m], 1))
        if parts is not None:
            total = chip_sums(parts, BF16, 1)
            memory_grad.append(lax.ppermute(total, "section", [(1, 0)]))
        cross_back.append(run_cross_back(m))
        if m > 0:
            encoder_back(m - 1)
            self_back.append(run_self_back(m - 1, 0))
        parts = True
    parts = core_sums(cross_back[last][4], twin(cross_back[last][5]), None, F32, 1)
    cross_weights = run_weights(
        [
            ([c[7] for c in crosses], [b[1] for b in cross_back], 0),
            (memory, [b[2] for b in cross_back], width),
            ([c[3] for c in crosses], [b[0] for b in cross_back], 3 * width),
        ],
        shaped(width, 4 * width, kind=BF16),
        role=1,
    )
    memory_grad.append(lax.ppermute(chip_sums(parts, BF16, 1), "section", [(1, 0)]))
    encoder_back(last)
    ffn_out_weights = run_weights(
        [([f[0] for f in ffn], [b[0] for b in back], 0)], shaped(hidden_units, width, kind=BF16)
    )
    ffn_in_weights = run_weights(
        [([f[3] for f in ffn], [b[1] for b in back], 0)], shaped(width, hidden_units, kind=BF16)
    )
    for m in range(last):
        self_back[m] = run_self_back(m, 1, self_back[m])
    self_back.append(run_self_back(last, None))
    attn_weights = run_weights(
        [
            ([x_in[0, m, 0] for m in ticks], [b[1] for b in self_back], 0),
            (x_all, [b[2] for b in self_back], width),
            ([s[3] for s in selfs], [b[0] for b in self_back], 3 * width),
        ],
        shaped(width, 4 * width, kind=BF16),
    )

    ffn_out_part = scatter_sum(ffn_out_weights)
    ffn_in_part = scatter_sum(ffn_in_weights)
    cross_part = scatter_sum(to_encoder_half(cross_weights, section))
    attn_part = scatter_sum(attn_weights)
    inputs_back = jnp.stack(
        [chip_sums(core_sums(b[4], twin(b[5]), b[3], F32), BF16) for b in self_back]
    )

    squares = sum(s[7] for s in selfs)
    f_small = sum(b[3] for b in back)
    s_small = sum(b[6] for b in self_back)
    c_small = sum(b[6] for b in cross_back)
    blocks = lax.axis_size("dp") * seq_size
    per = width // blocks
    half = per // 2
    per_hidden = hidden_units // blocks
    section_rows = jnp.stack(
        [s_small[3], s_small[4], s_small[2], f_small[2], s_small[1], f_small[1], s_small[0], f_small[0]]
    )
    cross_rows = jnp.stack([c_small[3], c_small[4], c_small[2], c_small[1], c_small[0]])
    cross_half = to_encoder_half(cross_rows.T, section)
    small = jnp.concatenate(
        [
            section_rows.T.reshape(blocks, 8 * per),
            f_small[3 : 3 + hidden_units // width].reshape(blocks, per_hidden),
            cross_half.reshape(blocks, 5 * half),
            jnp.broadcast_to(jnp.sum(squares[:2], 1)[None], (blocks, 2)),
        ],
        -1,
    )
    small = scatter_sum(small)[0]
    section_small = small[: 8 * per].reshape(per, 8).T
    ffn_bias_part = small[8 * per : 8 * per + per_hidden]
    rest = small[8 * per + per_hidden :]
    cross_small = rest[: 5 * half].reshape(half, 5).T
    count = micro * lax.axis_size("dp") * tokens * width
    stats = jnp.sqrt(rest[5 * half :] / count)[None]
    results = jnp.stack([jnp.where(section == 0, e[4], f[4]) for e, f in zip(enc_ffn, ffn)])
    return (
        results[None, :, None],
        inputs_back[None, :, None],
        stats,
        attn_part[None, :, : 3 * width],
        attn_part[None, :, 3 * width :],
        section_small[None, :6],
        section_small[None, 6:],
        ffn_in_part[None],
        ffn_bias_part[None],
        ffn_out_part[None],
        cross_part[:, :width],
        cross_part[:, width : 3 * width],
        cross_part[:, 3 * width :],
        cross_small[:4],
        cross_small[4],
    )


def solution(mesh):
    return jax.shard_map(
        per_device,
        mesh=mesh,
        in_specs=(
            P("section", None, "dp", "seq", None),
            P(None, None, "dp", "seq"),
            P(None, "dp", "seq", None),
            P("section", None, None),
            P("section", None, None),
            P("section", None, None),
            P("section", None, None),
            P("section", None, None),
            P("section", None),
            P("section", None, None),
            P(),
            P(),
            P(),
            P(),
            P(),
        ),
        out_specs=(
            P("section", None, "dp", "seq", None),
            P("section", None, "dp", "seq", None),
            P("section", None),
            P("section", ("dp", "seq"), None),
            P("section", ("dp", "seq"), None),
            P("section", None, ("dp", "seq")),
            P("section", None, ("dp", "seq")),
            P("section", ("dp", "seq"), None),
            P("section", ("dp", "seq")),
            P("section", ("dp", "seq"), None),
            P(("section", "dp", "seq"), None),
            P(("section", "dp", "seq"), None),
            P(("section", "dp", "seq"), None),
            P(None, ("section", "dp", "seq")),
            P(("section", "dp", "seq")),
        ),
        check_vma=False,
    )
```

```python
import enum
import functools
import math

import jax
import jax.numpy as jnp
from jax import lax
from jax.experimental import pallas as pl
from jax.experimental.pallas import tpu as pltpu
from jax.sharding import PartitionSpec as P

HEADS = 12
HEAD_DIM = 64
PAIR = 2 * HEAD_DIM
EPSILON = 1e-05
MASKED = -1000000000.0
SCALE = 1.0 / math.sqrt(HEAD_DIM)
VMEM_LIMIT = 58 * 1024 * 1024

F32 = jnp.float32
BF16 = jnp.bfloat16


def mm(a, b):
    return jnp.dot(a, b, preferred_element_type=F32)


def mm_nt(a, b):
    return lax.dot_general(a, b, (((1,), (1,)), ((), ())), preferred_element_type=F32)


def norm_parts(tensor):
    average = jnp.mean(tensor, -1, keepdims=True)
    centered = tensor - average
    spread = jnp.mean(centered * centered, -1, keepdims=True)
    scale = lax.rsqrt(spread + EPSILON)
    return centered * scale, scale


def norm_back(tensor, gain, grad):
    normed, scale = norm_parts(tensor)
    scaled = gain * grad
    product = grad * normed
    first = jnp.mean(scaled, -1, keepdims=True)
    second = jnp.mean(scaled * normed, -1, keepdims=True)
    out = (scaled - first - normed * second) * scale
    return out, jnp.sum(product, 0, keepdims=True), jnp.sum(grad, 0, keepdims=True)


def column_sum(tensor):
    return jnp.sum(tensor.astype(F32), 0, keepdims=True)


def gelu_pair(x):
    bell = jnp.exp(-0.5 * x * x)
    t = 1.0 / (1.0 + (0.3275911 / math.sqrt(2.0)) * jnp.abs(x))
    poly = t * (
        0.5 * 0.254829592
        + t
        * (
            0.5 * -0.284496736
            + t * (0.5 * 1.421413741 + t * (0.5 * -1.453152027 + t * (0.5 * 1.061405429)))
        )
    )
    tail = poly * bell
    cdf = jnp.where(x < 0, tail, 1.0 - tail)
    return x * cdf, cdf + x * bell * (1.0 / math.sqrt(2.0 * math.pi))


def row_blocks(count, body):
    step = min(256, count)

    def run(i, carry):
        body(pl.ds(pl.multiple_of(i * step, step), step))
        return carry

    lax.fori_loop(0, count // step, run, 0, unroll=True)


def head_halves(rows):
    lane = lax.broadcasted_iota(jnp.int32, (rows, PAIR), 1)
    return lane < HEAD_DIM, lane >= HEAD_DIM


def attend_forward(q_ref, k_ref, v_ref, bias_ref, mixed_ref, lse_ref):
    query_halves, key_halves = head_halves(q_ref.shape[0]), head_halves(k_ref.shape[0])

    def pair(p, carry):
        lanes = pl.ds(pl.multiple_of(p * PAIR, PAIR), PAIR)
        keys, values = k_ref[:, lanes], v_ref[:, lanes]
        queries = q_ref[:, lanes] * SCALE
        outs, peaks = [], []
        for a in range(2):
            own = jnp.where(query_halves[a], queries, jnp.zeros_like(queries))
            scores = mm_nt(own, keys) + bias_ref[...]
            peak = jnp.max(scores, 1, keepdims=True)
            weights = jnp.exp(scores - peak).astype(BF16)
            outs.append(mm(weights, jnp.where(key_halves[a], values, jnp.ones_like(values))))
            peaks.append(peak)
        first = query_halves[0]
        total = pltpu.roll(jnp.where(first, outs[1], outs[0]), HEAD_DIM, 1)
        lse_ref[p] = jnp.where(first, peaks[0], peaks[1]) + jnp.log(total)
        mixed_ref[:, lanes] = (jnp.where(first, outs[0], outs[1]) * (1.0 / total)).astype(BF16)
        return carry

    lax.fori_loop(0, HEADS // 2, pair, 0, unroll=2)


def attend_back(q_ref, k_ref, v_ref, grad_ref, mixed_ref, lse_ref, bias_ref, dq_ref, dkv_ref):
    length, width = q_ref.shape
    halves = head_halves(length)

    def pair(p, carry):
        lanes = pl.ds(pl.multiple_of(p * PAIR, PAIR), PAIR)
        value_lanes = pl.ds(pl.multiple_of(width + p * PAIR, PAIR), PAIR)
        keys, values = k_ref[:, lanes], v_ref[:, lanes]
        queries = q_ref[:, lanes] * SCALE
        grads = grad_ref[:, lanes]
        product = grads.astype(F32) * mixed_ref[:, lanes].astype(F32)
        queries_t, grads_t = queries.T, grads.T
        outs, key_grads, value_grads = [], [], []
        for a, half in enumerate(halves):
            own = jnp.where(half, queries, jnp.zeros_like(queries))
            own_grad = jnp.where(half, grads, jnp.zeros_like(grads))
            rows = slice(a * HEAD_DIM, (a + 1) * HEAD_DIM)
            lse = lse_ref[p, :, a * HEAD_DIM : a * HEAD_DIM + 1]
            delta = jnp.sum(jnp.where(half, product, 0.0), 1, keepdims=True)
            weights = jnp.exp(mm_nt(own, keys) + bias_ref[...] - lse)
            score_grad = (weights * (mm_nt(own_grad, values) - delta)).astype(BF16)
            outs.append(mm(score_grad, keys))
            key_grads.append(mm(queries_t[rows], score_grad))
            value_grads.append(mm(grads_t[rows], weights.astype(BF16)))
        dkv_ref[:, lanes] = jnp.concatenate(key_grads, 0).astype(BF16).T
        dkv_ref[:, value_lanes] = jnp.concatenate(value_grads, 0).astype(BF16).T
        dq_ref[:, lanes] = (jnp.where(halves[0], outs[0], outs[1]) * SCALE).astype(BF16)
        return carry

    lax.fori_loop(0, HEADS // 2, pair, 0, unroll=2)


def self_kernel(io, x_ref, w_qkv, w_mix, vec, bias, q_out, k_out, v_out, mixed, lse, summed, hidden, squares):
    length, width = q_out.shape
    io.ready(x_ref, w_qkv, vec)
    x_own = x_ref[0:length, :]
    q_out[...] = (mm(x_own, w_qkv[:, 0:width]) + vec[0:1, :]).astype(BF16)

    def keys(rows):
        x = x_ref[rows, :]
        k_out[rows, :] = mm(x, w_qkv[:, width : 2 * width]).astype(BF16)
        v_out[rows, :] = (mm(x, w_qkv[:, 2 * width : 3 * width]) + vec[1:2, :]).astype(BF16)

    row_blocks(x_ref.shape[0], keys)
    io.done(q_out, k_out, v_out)
    io.ready(bias)
    attend_forward(q_out, k_out, v_out, bias, mixed, lse)
    io.done(mixed, lse)
    io.ready(w_mix)
    branch = mm(mixed[...], w_mix[...]) + vec[2:3, :]
    total = x_own.astype(F32) + branch
    summed[...] = total
    squares[...] = jnp.zeros_like(squares)
    squares[0:1, :] = column_sum(total * total)
    squares[1:2, :] = column_sum(branch * branch)
    hidden[...] = norm_parts(total)[0] * vec[6:7, :] + vec[4:5, :]


def ffn_kernel(io, middle, vec, w_in, b_in, w_out, act, slope, final_sum, low_middle, result):
    width = middle.shape[1]
    chunks = w_in.shape[1] // width
    io.ready(middle, vec)
    mid = middle[...]
    low = mid.astype(BF16)
    low_middle[...] = low
    final_sum[...] = mid + vec[3:4, :]
    io.ready(w_in, b_in, w_out)

    def chunk(j, carry):
        columns = pl.ds(pl.multiple_of(j * width, width), width)
        inner = mm(low, w_in[:, columns]) + b_in[:, columns]
        value, derivative = gelu_pair(inner)
        value = value.astype(BF16)
        act[:, columns] = value
        slope[:, columns] = derivative.astype(BF16)
        final_sum[...] += mm(value, w_out[columns, :])
        return carry

    lax.fori_loop(0, chunks, chunk, 0, unroll=True)
    io.done(act, slope, low_middle, final_sum)
    result[...] = (norm_parts(final_sum[...])[0] * vec[7:8, :] + vec[5:6, :]).astype(BF16)


def ffn_norm_kernel(io, grad, final_sum, vec, dy, d_final, small):
    io.ready(grad, final_sum, vec)
    back, d_gain, d_shift = norm_back(final_sum[...], vec[7:8, :], grad[...].astype(F32))
    low = back.astype(BF16)
    dy[...] = low
    d_final[...] = back
    small[...] = jnp.zeros_like(small)
    small[0:1, :] = d_gain
    small[1:2, :] = d_shift
    small[2:3, :] = column_sum(low)


def ffn_rest_kernel(io, dy, d_final, small_in, w_out, slope, w_in, d_inner, d_middle, small):
    width = dy.shape[1]
    chunks = w_in.shape[1] // width
    io.ready(dy, d_final, small_in, w_out, slope, w_in)
    low = dy[...]
    small[...] = small_in[...]
    d_middle[...] = d_final[...]

    def chunk(j, carry):
        columns = pl.ds(pl.multiple_of(j * width, width), width)
        d_act = mm_nt(low, w_out[columns, :])
        inner = (d_act * slope[:, columns].astype(F32)).astype(BF16)
        d_inner[:, columns] = inner
        small[pl.ds(3 + j, 1), :] = column_sum(inner)
        d_middle[...] += mm_nt(inner, w_in[:, columns])
        return carry

    lax.fori_loop(0, chunks, chunk, 0, unroll=True)


def ffn_back_kernel(io, grad, final_sum, vec, w_out, slope, w_in, dy, d_inner, d_middle, small):
    ffn_norm_kernel(io, grad, final_sum, vec, dy, d_middle, small)
    io.done(dy)
    ffn_rest_kernel(io, dy, d_middle, small, w_out, slope, w_in, d_inner, d_middle, small)


def mask_kernel(micro, io, ids, far, *outs):
    io.ready(ids, far)
    length = ids.shape[1]
    section, me, blocks = lax.axis_index("section"), lax.axis_index("seq"), lax.axis_size("seq")
    orders = []
    for k in range(blocks // 2):
        chip = (me + 2 * k) % blocks
        orders += [chip, chip + 1 - 2 * (me % 2)]
    here = lax.broadcasted_iota(jnp.int32, (length, length), 0)
    there = lax.broadcasted_iota(jnp.int32, (length, length), 1)
    for m in range(micro):
        own = jnp.where(section == 0, ids[m : m + 1, :], ids[micro + m : micro + m + 1, :])
        query = jnp.broadcast_to(own.astype(F32), (PAIR, length)).T[:, 0:1]
        for j, order in enumerate(orders):
            block = ids if j == 0 else far.at[j]
            source, target = block[m : m + 1, :], block[micro + m : micro + m + 1, :]
            key = jnp.where(section == 0, source, target).astype(F32)
            late = (there + order * length > here + orders[0] * length) & (section == 1)
            columns = slice(j * length, (j + 1) * length)
            outs[m][:, columns] = jnp.where((query == key) & jnp.logical_not(late), 0.0, MASKED)
            outs[micro + m][:, columns] = jnp.where(query == source.astype(F32), 0.0, MASKED)


def cross_kernel(
    io, hidden, w_q, vec, memory, w_kv, bias, w_o,
    cq, ck, cv, mixed, lse, summed, middle, low_hidden,
):
    width = hidden.shape[1]
    io.ready(hidden, w_q, vec)
    low = hidden[...].astype(BF16)
    low_hidden[...] = low
    cq[...] = (mm(low, w_q[...]) + vec[0:1, :]).astype(BF16)
    io.ready(memory, w_kv)

    def keys(rows):
        mem = memory[rows, :]
        ck[rows, :] = mm(mem, w_kv[:, 0:width]).astype(BF16)
        cv[rows, :] = (mm(mem, w_kv[:, width : 2 * width]) + vec[1:2, :]).astype(BF16)

    row_blocks(memory.shape[0], keys)
    io.done(cq, ck, cv, low_hidden)
    io.ready(bias)
    attend_forward(cq, ck, cv, bias, mixed, lse)
    io.done(mixed, lse)
    io.ready(w_o)
    total = hidden[...] + mm(mixed[...], w_o[...]) + vec[2:3, :]
    summed[...] = total
    middle[...] = norm_parts(total)[0] * vec[4:5, :] + vec[3:4, :]


def cross_back_kernel(
    io, d_middle, summed, vec, w_o, mixed, cq, ck, bias, lse, cv, w_q, w_kv,
    dyc, dcq, dckv, d_hidden, keep, send, small, d_mixed,
):
    length, width = d_middle.shape
    io.ready(d_middle, summed, vec)
    d_cross, d_gain, d_shift = norm_back(summed[...], vec[4:5, :], d_middle[...])
    low = d_cross.astype(BF16)
    dyc[...] = low
    d_hidden[...] = d_cross
    io.ready(w_o, mixed)
    grads = mm_nt(low, w_o[...]).astype(BF16)
    d_mixed[...] = grads
    io.ready(cq, ck, bias, lse, cv)
    attend_back(cq, ck, cv, d_mixed, mixed, lse, bias, dcq, dckv)
    io.ready(w_q, w_kv)
    for block in range(dckv.shape[0] // length):
        target = keep if block % 2 == 0 else send
        rows = slice(block // 2 * length, (block // 2 + 1) * length)
        target[rows, :] = mm_nt(dckv[block * length : (block + 1) * length, :], w_kv[...]).astype(BF16)
    io.done(send, keep, dyc, dcq, dckv)
    d_hidden[...] += mm_nt(dcq[...], w_q[...])
    small[...] = jnp.zeros_like(small)
    small[0:1, :] = d_gain
    small[1:2, :] = d_shift
    small[2:3, :] = column_sum(low)
    small[3:4, :] = column_sum(dcq[...])
    small[4:5, :] = column_sum(dckv[:, width : 2 * width])


def self_back_kernel(
    io, grad, summed, vec, w_mix, mixed, q, k, bias, lse, v, w_qkv,
    dy, dq, dkv, own, keep, send, small, d_mixed,
):
    length, width = q.shape
    io.ready(grad, summed, vec)
    d_sum, d_gain, d_shift = norm_back(summed[...], vec[6:7, :], grad[...])
    low = d_sum.astype(BF16)
    dy[...] = low
    own[...] = d_sum
    io.ready(w_mix, mixed)
    grads = mm_nt(low, w_mix[...]).astype(BF16)
    d_mixed[...] = grads
    io.ready(q, k, bias, lse, v)
    attend_back(q, k, v, d_mixed, mixed, lse, bias, dq, dkv)
    io.done(dy, dq, dkv)
    io.ready(w_qkv)
    for block in range(dkv.shape[0] // length):
        part = mm_nt(dkv[block * length : (block + 1) * length, :], w_qkv[:, width : 3 * width])
        if block == 0:
            own[...] += part + mm_nt(dq[...], w_qkv[:, 0:width])
            continue
        target = keep if block % 2 == 0 else send
        at = (block - 2) // 2 if block % 2 == 0 else block // 2
        target[at * length : (at + 1) * length, :] = part.astype(BF16)
    io.done(send, keep, own)
    small[...] = jnp.zeros_like(small)
    small[0:1, :] = d_gain
    small[1:2, :] = d_shift
    small[2:3, :] = column_sum(low)
    small[3:4, :] = column_sum(dq[...])
    small[4:5, :] = column_sum(dkv[:, width : 2 * width])


def weight_kernel(plan, regroup, io, *refs):
    out = refs[-1] if regroup == 0 else refs[-2]
    wide_out = out if regroup == 0 else refs[-1]
    for lefts, rights, column in plan:
        inner = refs[lefts[0]].shape[1]
        cols = refs[rights[0]].shape[1]
        step = 256
        wide = min(cols, 1536)
        io.ready(*[refs[i] for i in lefts + rights])

        def tile(i, carry, lefts=lefts, rights=rights, column=column, cols=cols, wide=wide):
            rows = pl.ds(pl.multiple_of(i * step, step), step)
            turned = [refs[l][:, rows].T for l in lefts]
            for start in range(0, cols, wide):
                total = None
                for left, r in zip(turned, rights):
                    term = mm(left, refs[r][:, start : start + wide])
                    total = term if total is None else total + term
                wide_out[rows, column + start : column + start + wide] = total.astype(wide_out.dtype)
            return carry

        lax.fori_loop(0, inner // step, tile, 0, unroll=3)
    if regroup:
        half = out.shape[0] // 2

        def group(i, carry):
            first = wide_out[pl.ds(pl.multiple_of(i * regroup, regroup), regroup), :]
            second = wide_out[pl.ds(pl.multiple_of(half + i * regroup, regroup), regroup), :]
            rows = pl.ds(pl.multiple_of(2 * i * regroup, 2 * regroup), 2 * regroup)
            out[rows, :] = jnp.concatenate([first, second], 0).astype(BF16)
            return carry

        lax.fori_loop(0, half // regroup, group, 0)


def add_kernel(io, *refs):
    out = refs[-1]
    io.ready(*refs[:-1])
    total = refs[0][...].astype(F32)
    for ref in refs[1:-1]:
        total = total + ref[...].astype(F32)
    out[...] = total.astype(out.dtype)


def add_lead_kernel(io, one, many, out):
    io.ready(one, many)
    total = one[...].astype(F32)
    for i in range(many.shape[0]):
        total = total + many[i].astype(F32)
    out[...] = total.astype(out.dtype)


def small_kernel(micro, io, *refs):
    out = refs[-1]
    ins = refs[:-1]
    io.ready(*ins)
    selfs, ffns, squares, crosses = (ins[i * micro : (i + 1) * micro] for i in range(4))
    out[...] = jnp.zeros_like(out)
    for ref in selfs:
        out[0:8, :] += ref[...]
    for ref in squares:
        out[5:7, :] += ref[0:2, :]
    for ref in ffns:
        out[8:16, :] += ref[...]
    for ref in crosses:
        out[16:24, :] += jnp.where(lax.axis_index("section") == 1, ref[...], 0.0)


class Moves:
    def __init__(self, loads, stores):
        self.loads, self.stores = dict(loads), dict(stores)
        self.started, self.waited = set(), set()
        for copies in self.loads.values():
            for copy in copies:
                copy.start()

    def ready(self, *refs):
        for ref in refs:
            if id(ref) not in self.waited:
                self.waited.add(id(ref))
                for copy in self.loads.get(id(ref), ()):
                    copy.wait()

    def done(self, *refs):
        for ref in refs:
            if id(ref) not in self.started:
                self.started.add(id(ref))
                for copy in self.stores[id(ref)]:
                    copy.start()

    def finish(self, ins, outs):
        self.ready(*ins)
        self.done(*outs)
        for copies in self.stores.values():
            for copy in copies:
                copy.wait()


class Held:
    def __init__(self, ref):
        self.ref = ref


class Rows:
    def __init__(self, pieces, shape=None):
        self.pieces = list(pieces)
        rest = self.pieces[0].shape[1:] if shape is None else shape[1:]
        count = sum(p.shape[0] for p in self.pieces) if shape is None else shape[0]
        self.shape, self.dtype = (count, *rest), self.pieces[0].dtype


def as_rows(item):
    return item if isinstance(item, Rows) else Rows([item])


def step(kernel, operands, outs, scratch=()):
    operands = [o if isinstance(o, Held) else as_rows(o) for o in operands]
    moved = [o for o in operands if not isinstance(o, Held)]
    outs = [as_rows(o) for o in outs]
    n_load = sum(len(o.pieces) for o in moved)
    n_store = sum(len(o.pieces) for o in outs)

    def pairs(ref, rows):
        if len(rows.pieces) == 1:
            return [(rows.pieces[0], ref)]
        found, at = [], 0
        for piece in rows.pieces:
            found.append((piece, ref.at[pl.ds(at, piece.shape[0])]))
            at += piece.shape[0]
        return found

    def inner(*refs):
        n_in, n_out = len(moved), len(outs)
        vmem_in, vmem_out = refs[:n_in], refs[n_in : n_in + n_out]
        in_sem, out_sem = refs[n_in + n_out : n_in + n_out + 2]
        extra = refs[n_in + n_out + 2 :]
        loads, at = [], 0
        for ref, rows in zip(vmem_in, moved):
            copies = []
            for hbm, vmem in pairs(ref, rows):
                copies.append(pltpu.make_async_copy(hbm, vmem, in_sem.at[at]))
                at += 1
            loads.append((id(ref), copies))
        stores, at = [], 0
        for ref, rows in zip(vmem_out, outs):
            copies = []
            for hbm, vmem in pairs(ref, rows):
                copies.append(pltpu.make_async_copy(vmem, hbm, out_sem.at[at]))
                at += 1
            stores.append((id(ref), copies))
        moves = Moves(loads, stores)
        left = list(vmem_in)
        ins = [o.ref if isinstance(o, Held) else left.pop(0) for o in operands]
        kernel(moves, *ins, *vmem_out, *extra)
        moves.finish(vmem_in, vmem_out)

    pl.run_scoped(
        inner,
        *[pltpu.VMEM(o.shape, o.dtype) for o in moved],
        *[pltpu.VMEM(o.shape, o.dtype) for o in outs],
        pltpu.SemaphoreType.DMA((max(n_load, 1),)),
        pltpu.SemaphoreType.DMA((max(n_store, 1),)),
        *scratch,
    )


class N(enum.Enum):
    act = enum.auto()
    b_in = enum.auto()
    chip = enum.auto()
    chip_in = enum.auto()
    mid = enum.auto()
    d_final = enum.auto()
    norm_small = enum.auto()
    ids = enum.auto()
    ids_all = enum.auto()
    ck = enum.auto()
    core = enum.auto()
    core_in = enum.auto()
    core_sum = enum.auto()
    cotangent = enum.auto()
    cq = enum.auto()
    cross_bias = enum.auto()
    cross_half = enum.auto()
    cross_kv = enum.auto()
    cross_lse = enum.auto()
    cross_mixed = enum.auto()
    cross_out = enum.auto()
    cross_q = enum.auto()
    cross_small = enum.auto()
    cross_sum = enum.auto()
    cross_vec = enum.auto()
    cv = enum.auto()
    d_inner = enum.auto()
    d_memory = enum.auto()
    d_middle = enum.auto()
    dckv = enum.auto()
    dcq = enum.auto()
    dkv = enum.auto()
    dm = enum.auto()
    dm_chip = enum.auto()
    dm_chip_in = enum.auto()
    dm_core = enum.auto()
    dm_core_in = enum.auto()
    dm_keep = enum.auto()
    dm_send = enum.auto()
    dm_sum = enum.auto()
    dq = enum.auto()
    dx = enum.auto()
    dx_chip = enum.auto()
    dx_chip_in = enum.auto()
    dx_core = enum.auto()
    dx_core_in = enum.auto()
    dx_keep = enum.auto()
    dx_own = enum.auto()
    dx_rest = enum.auto()
    dx_send = enum.auto()
    dx_sum = enum.auto()
    dy = enum.auto()
    dy3 = enum.auto()
    dyc = enum.auto()
    ffn_small = enum.auto()
    final_sum = enum.auto()
    g_attn = enum.auto()
    g_cross = enum.auto()
    g_in = enum.auto()
    g_out = enum.auto()
    hidden = enum.auto()
    hop = enum.auto()
    i = enum.auto()
    input_grad = enum.auto()
    k = enum.auto()
    layer_out = enum.auto()
    low_hidden = enum.auto()
    low_middle = enum.auto()
    lse = enum.auto()
    m = enum.auto()
    memory = enum.auto()
    middle = enum.auto()
    mixed = enum.auto()
    out = enum.auto()
    q = enum.auto()
    row = enum.auto()
    row_in = enum.auto()
    self_bias = enum.auto()
    self_small = enum.auto()
    slope = enum.auto()
    small = enum.auto()
    small_chip = enum.auto()
    small_chip_in = enum.auto()
    small_chip_sum = enum.auto()
    small_core = enum.auto()
    small_core_in = enum.auto()
    small_core_sum = enum.auto()
    small_half = enum.auto()
    small_row = enum.auto()
    small_row_in = enum.auto()
    small_sum = enum.auto()
    squares = enum.auto()
    summed = enum.auto()
    v = enum.auto()
    vec = enum.auto()
    w_in = enum.auto()
    w_mix = enum.auto()
    w_out = enum.auto()
    w_qkv = enum.auto()
    x = enum.auto()
    x_all = enum.auto()


class Wires:
    def __init__(self, send_sem, recv_sem, names, buffers):
        self.send_sem, self.recv_sem, self.names = send_sem, recv_sem, names
        self.like = {(ref.shape, ref.dtype): ref for ref in buffers}
        self.section, self.dp, self.seq = (lax.axis_index(n) for n in ("section", "dp", "seq"))
        self.dp_size, self.seq_size = lax.axis_size("dp"), lax.axis_size("seq")
        self.chips = self.seq_size // 2
        self.core = self.seq % 2
        self.twin = {"seq": self.seq + 1 - 2 * self.core}
        self.across = {"section": 1 - self.section}
        self.open, self.role = [], None

    def chip(self, k):
        return {"seq": (self.seq + 2 * k) % self.seq_size}

    def row(self, k):
        return {"dp": (self.dp + k) % self.dp_size}

    def peers(self, across=True):
        found = [self.twin]
        found += [self.chip(k) for k in range(1, self.chips)]
        found += [self.row(k) for k in range(1, self.dp_size)] if across else []
        return found + ([self.across] if across else [])

    def barrier(self, across=True):
        semaphore = pltpu.get_barrier_semaphore()
        peers = self.peers(across)
        for peer in peers:
            pl.semaphore_signal(semaphore, inc=1, device_id=peer, device_id_type=pl.DeviceIdType.MESH)
        pl.semaphore_wait(semaphore, len(peers))

    def copy(self, name, source, target, device):
        at = self.names.index(name)
        return pltpu.make_async_remote_copy(
            src_ref=source,
            dst_ref=target,
            send_sem=self.send_sem.at[at],
            recv_sem=self.recv_sem.at[at],
            device_id=device,
            device_id_type=pl.DeviceIdType.MESH,
        )

    def start(self, name, moves, whole=None):
        for source, target, device in moves:
            self.copy(name, source, target, device).start()
        if whole is None:
            whole = moves[0][0]
        self.open.append((name, self.like.get((whole.shape, whole.dtype), whole), self.role))

    def arrived(self, name, target):
        self.copy(name, target, target, self.twin).wait_recv()

    def close(self):
        def wait(role):
            for name, whole, of in self.open:
                if of == role:
                    self.copy(name, whole, whole, self.twin).wait_send()

        wait(None)
        for role in (0, 1):
            if any(of == role for _, _, of in self.open):
                pl.when(self.section == role)(functools.partial(wait, role))

    def only(self, role):
        def run(body):
            def inner():
                self.role = role
                body()
                self.role = None

            pl.when(self.section == role)(inner)

        return run


def gather_start(wires, name, source, target):
    wires.start((name, N.core), [(source, target.at[1], wires.twin)])
    for k in range(1, wires.chips):
        wires.start((name, N.chip, k), [(source, target.at[2 * (wires.chips - k)], wires.chip(k))])


def gather_pass(wires, name, target):
    for k in range(1, wires.chips):
        wires.arrived((name, N.chip, k), target.at[2 * (wires.chips - k)])
        wires.start((name, N.hop, k), [(target.at[2 * (wires.chips - k)], target.at[2 * (wires.chips - k) + 1], wires.twin)])


def gather_end(wires, name, target):
    wires.arrived((name, N.core), target.at[1])
    for k in range(1, wires.chips):
        wires.arrived((name, N.hop, k), target.at[2 * (wires.chips - k) + 1])


def gather_names(name, chips):
    return [(name, N.core)] + [(name, part, k) for part in (N.chip, N.hop) for k in range(1, chips)]


class Sums:
    def __init__(self, wires, refs, key, unit, first, rows, dp_first):
        self.wires, self.key, self.dp_first = wires, key, dp_first
        self.full, self.out = refs[unit], refs[unit, N.out]
        self.first, self.rows, self.block_rows = first, rows, self.out.shape[0]
        self.core_in, self.core_sum = refs[key, N.core_in], refs[key, N.core_sum]
        self.chip_in, self.row_in, self.mid = refs[key, N.chip_in], refs[key, N.row_in], refs[key, N.mid]
        self.count, self.columns = self.core_in.shape[0], self.core_in.shape[2]

    def block(self, pair, core):
        at = (2 * pair + core) * self.block_rows + self.first
        return self.full.at[pl.ds(pl.multiple_of(at, 16), self.rows)]

    def core_start(self):
        w = self.wires
        moves = [(self.block(i, 1 - w.core), self.core_in.at[i], w.twin) for i in range(self.count)]
        w.start((self.key, N.core), moves, self.core_in)

    def core_add(self):
        w = self.wires
        w.arrived((self.key, N.core), self.core_in)
        own = Rows([self.block(i, w.core) for i in range(self.count)], (self.count * self.rows, self.columns))
        arrived = Rows([self.core_in.at[i] for i in range(self.count)], own.shape)
        sums = Rows([self.core_sum.at[i] for i in range(self.count)], own.shape)
        step(add_kernel, [own, arrived], [sums])
        if self.dp_first:
            moves = []
            for k in range(1, w.dp_size):
                source = self.core_sum.at[pl.ds((w.dp + k) % w.dp_size * w.chips, w.chips)]
                moves.append((source, self.row_in.at[k - 1], w.row(k)))
            w.start((self.key, N.row), moves, self.row_in)
            return
        for k in range(1, w.chips):
            there = (w.seq // 2 + k) % w.chips
            target = self.chip_in.at[k - 1]
            moves = [
                (self.core_sum.at[d * w.chips + there], target.at[d], w.chip(k)) for d in range(w.dp_size)
            ]
            w.start((self.key, N.chip, k), moves, target)

    def second_add(self):
        w = self.wires
        mine = w.seq // 2
        if self.dp_first:
            w.arrived((self.key, N.row), self.row_in)
            terms = [self.core_sum.at[pl.ds(w.dp * w.chips, w.chips)]]
            terms += [self.row_in.at[k] for k in range(w.dp_size - 1)]
            step(add_kernel, terms, [self.mid])
            for k in range(1, w.chips):
                source = self.mid.at[(mine + k) % w.chips]
                w.start((self.key, N.chip, k), [(source, self.chip_in.at[k - 1], w.chip(k))])
            return
        shape = (w.dp_size * self.rows, self.columns)
        terms = [Rows([self.core_sum.at[d * w.chips + mine] for d in range(w.dp_size)], shape)]
        for k in range(1, w.chips):
            w.arrived((self.key, N.chip, k), self.chip_in.at[k - 1])
            terms.append(Rows([self.chip_in.at[k - 1, d] for d in range(w.dp_size)], shape))
        step(add_kernel, terms, [Rows([self.mid.at[d] for d in range(w.dp_size)], shape)])
        moves = [
            (self.mid.at[(w.dp + k) % w.dp_size], self.row_in.at[k - 1], w.row(k)) for k in range(1, w.dp_size)
        ]
        w.start((self.key, N.row), moves, self.row_in)

    def third_add(self):
        w = self.wires
        out = self.out.at[pl.ds(self.first, self.rows)]
        if self.dp_first:
            for k in range(1, w.chips):
                w.arrived((self.key, N.chip, k), self.chip_in.at[k - 1])
            step(add_lead_kernel, [self.mid.at[w.seq // 2], self.chip_in], [out])
            return
        w.arrived((self.key, N.row), self.row_in)
        step(add_lead_kernel, [self.mid.at[w.dp], self.row_in], [out])


def sum_pieces(units, devices):
    pieces = []
    for unit, (rows, _) in units.items():
        rows //= devices
        if unit is N.g_out and rows // 2 % 16 == 0:
            pieces.append(((unit, 0), unit, 0, rows // 2, True))
            pieces.append(((unit, 1), unit, rows // 2, rows // 2, False))
        else:
            pieces.append(((unit, 0), unit, 0, rows, unit is N.g_out))
    return pieces


def sum_shapes(key, rows, columns, dp_first, dp_size, chips):
    far_chips, far_rows = max(chips - 1, 1), max(dp_size - 1, 1)
    block = (rows, columns)
    return {
        (key, N.core_in): shaped(dp_size * chips, *block, kind=BF16),
        (key, N.core_sum): shaped(dp_size * chips, *block, kind=BF16),
        (key, N.mid): shaped(chips if dp_first else dp_size, *block, kind=BF16),
        (key, N.chip_in): shaped(far_chips, *(block if dp_first else (dp_size, *block)), kind=BF16),
        (key, N.row_in): shaped(far_rows, *((chips, *block) if dp_first else block), kind=BF16),
    }


def sum_names(key, chips):
    return [(key, N.core), (key, N.row)] + [(key, N.chip, k) for k in range(1, chips)]


def final_body(count, n_in, *refs):
    n_out = 15
    ins, outs, refs = refs[:n_in], refs[n_in : n_in + n_out], refs[n_in + n_out :]
    held, refs = refs[:n_in], refs[n_in:]
    stats, bias_grad, gain_grad, hidden_grad, cross_grad, cross_gain_grad, in_sem, out_sem = refs
    layer_out, input_grad, attn, ffn_in, ffn_out, small, cross_small = held[:7]
    cross = held[7:]
    section = lax.axis_index("section")
    me = lax.axis_index("dp") * lax.axis_size("seq") + lax.axis_index("seq")
    devices = lax.axis_size("dp") * lax.axis_size("seq")
    width = small.shape[1]
    half = outs[6].shape[0]
    loads = [pltpu.make_async_copy(a, v, in_sem.at[i]) for i, (a, v) in enumerate(zip(ins, held))]
    for copy in [*loads[5:7], *loads[:5], *loads[7:]]:
        copy.start()
    moves = []

    def move(source, at):
        moves.append(pltpu.make_async_copy(source, outs[at], out_sem.at[at]))
        return moves[-1]

    loads[5].wait()
    loads[6].wait()

    def columns_of(rows, start, number):
        at = lax.broadcasted_iota(jnp.int32, (width, number), 0)
        column = lax.broadcasted_iota(jnp.int32, (width, number), 1)
        return jnp.dot(
            rows, (at == column + start).astype(F32), precision=lax.Precision.HIGHEST, preferred_element_type=F32
        )

    per, per_hidden = bias_grad.shape[1], hidden_grad.shape[1]
    mine = columns_of(small[...], me * per, per)
    for i, row in enumerate((3, 4, 2, 10, 1, 9)):
        bias_grad[i : i + 1, :] = mine[row : row + 1]
    for i, row in enumerate((0, 8)):
        gain_grad[i : i + 1, :] = mine[row : row + 1]
    place = me * per_hidden
    hidden_rows = columns_of(small[8:16, :], place % width, per_hidden)
    row = lax.broadcasted_iota(jnp.int32, hidden_rows.shape, 0)
    hidden_grad[...] = jnp.sum(jnp.where(row == 3 + place // width, hidden_rows, 0.0), 0, keepdims=True)
    rows = jnp.where(section == 0, cross_small[...], small[16:24, :])
    cross_rows = columns_of(rows, (section * devices + me) * half, half)
    for i, row in enumerate((3, 4, 2, 1)):
        cross_grad[i : i + 1, :] = cross_rows[row : row + 1]
    cross_gain_grad[...] = cross_rows[0:1]
    squares = jnp.sum(small[5:7, :], 1, keepdims=True)
    stats[...] = jnp.sqrt(jnp.concatenate([squares[0:1], squares[1:2]], 1) / count)
    for i, ref in enumerate((stats, bias_grad, gain_grad, hidden_grad, cross_grad, cross_gain_grad)):
        move(ref, 9 + i).start()
    for load, targets in zip(
        loads[:5],
        (
            [(layer_out, 0)],
            [(input_grad, 1)],
            [(attn.at[:, 0 : 3 * width], 2), (attn.at[:, 3 * width : 4 * width], 3)],
            [(ffn_in, 4)],
            [(ffn_out, 5)],
        ),
    ):
        load.wait()
        for source, at in targets:
            move(source, at).start()
    for load in loads[7:]:
        load.wait()
    if len(cross) == 2:
        cross[0][...] = jnp.where(section == 0, cross[0][...], cross[1][half : 2 * half, :])
    for i, (first, end) in enumerate([(0, width), (width, 3 * width), (3 * width, 4 * width)]):
        move(cross[0].at[:, first:end], 6 + i).start()
    for copy in moves:
        copy.wait()


def main_body(micro, pieces, in_names, out_names, wire_names, held_names, *refs):
    refs = list(refs)
    hbm = {n: refs.pop(0) for n in in_names + out_names}
    held_refs = {n: refs.pop(0) for n in held_names}
    send_sem, recv_sem, held_sem = refs
    wires = Wires(send_sem, recv_sem, wire_names, hbm.values())
    chips, dp_size = wires.chips, wires.dp_size
    length, width = hbm[N.x].shape[1:]
    hidden_units = hbm[N.w_in].shape[1]
    held_copies = {
        n: pltpu.make_async_copy(hbm[n], held_refs[n], held_sem.at[i]) for i, n in enumerate(held_names)
    }
    for copy in held_copies.values():
        copy.start()
    held = {n: Held(r) for n, r in held_refs.items()}
    vec, cross_vec = held[N.vec], held[N.cross_vec]
    ticks, last = range(micro), micro - 1
    back_scratch = (pltpu.VMEM((length, width), BF16),)

    def b(name, m):
        return hbm[(name, m)]

    def inputs(m):
        blocks = b(N.x_all, m)
        return Rows([hbm[N.x].at[m]] + [blocks.at[i] for i in range(1, wires.seq_size)])

    def memory(m):
        arrived = b(N.memory, m)
        return Rows([arrived.at[i] for i in range(wires.seq_size)])

    def self_forward(m):
        step(
            self_kernel,
            [inputs(m), held[N.w_qkv], held[N.w_mix], vec, b(N.self_bias, m)],
            [b(n, m) for n in (N.q, N.k, N.v, N.mixed, N.lse, N.summed, N.hidden, N.squares)],
        )

    def ffn_forward(m, middle):
        step(
            ffn_kernel,
            [b(middle, m), vec, held[N.w_in], held[N.b_in], held[N.w_out]],
            [b(n, m) for n in (N.act, N.slope, N.final_sum, N.low_middle)] + [hbm[N.layer_out].at[m]],
        )

    def ffn_back(m, grad):
        step(
            ffn_back_kernel,
            [grad, b(N.final_sum, m), vec, held[N.w_out], b(N.slope, m), held[N.w_in]],
            [b(n, m) for n in (N.dy3, N.d_inner, N.d_middle, N.ffn_small)],
        )

    def cross_forward(m):
        step(
            cross_kernel,
            [b(N.hidden, m), held[N.cross_q], cross_vec, memory(m), held[N.cross_kv], b(N.cross_bias, m), held[N.cross_out]],
            [b(n, m) for n in (N.cq, N.ck, N.cv, N.cross_mixed, N.cross_lse, N.cross_sum, N.middle, N.low_hidden)],
        )

    def cross_back(m):
        step(
            cross_back_kernel,
            [b(N.d_middle, m), b(N.cross_sum, m), cross_vec, held[N.cross_out], b(N.cross_mixed, m), b(N.cq, m), b(N.ck, m),
             b(N.cross_bias, m), b(N.cross_lse, m), b(N.cv, m), held[N.cross_q], held[N.cross_kv]],
            [b(n, m) for n in (N.dyc, N.dcq, N.dckv, N.d_middle, N.dm_keep, N.dm_send, N.cross_small)],
            back_scratch,
        )

    def self_back(m):
        step(
            self_back_kernel,
            [b(N.d_middle, m), b(N.summed, m), vec, held[N.w_mix], b(N.mixed, m), b(N.q, m), b(N.k, m), b(N.self_bias, m),
             b(N.lse, m), b(N.v, m), held[N.w_qkv]],
            [b(n, m) for n in (N.dy, N.dq, N.dkv, N.dx_own, N.dx_keep, N.dx_send, N.self_small)],
            back_scratch,
        )
        wires.start((N.dx_core, m), [(b(N.dx_send, m), b(N.dx_core_in, m), wires.twin)])

    def dx_core(m):
        wires.arrived((N.dx_core, m), b(N.dx_core_in, m))
        arrived, rest = b(N.dx_core_in, m), (chips - 1) * length
        step(add_kernel, [b(N.dx_own, m), arrived.at[0:length]], [b(N.dx_sum, m)])
        step(add_kernel, [b(N.dx_keep, m), arrived.at[pl.ds(length, rest)]], [b(N.dx_rest, m)])
        for k in range(1, chips):
            source = b(N.dx_rest, m).at[pl.ds((k - 1) * length, length)]
            wires.start((N.dx_chip, k, m), [(source, b(N.dx_chip_in, m).at[k - 1], wires.chip(k))])

    def dx_end(m):
        for k in range(1, chips):
            wires.arrived((N.dx_chip, k, m), b(N.dx_chip_in, m).at[k - 1])
        step(add_lead_kernel, [b(N.dx_sum, m), b(N.dx_chip_in, m)], [hbm[N.input_grad].at[m]])

    def dm_start(m):
        wires.start((N.dm_core, m), [(b(N.dm_send, m), b(N.dm_core_in, m), wires.twin)])

    def dm_core(m):
        wires.arrived((N.dm_core, m), b(N.dm_core_in, m))
        step(add_kernel, [b(N.dm_keep, m), b(N.dm_core_in, m)], [b(N.dm_sum, m)])
        for k in range(1, chips):
            source = b(N.dm_sum, m).at[pl.ds(k * length, length)]
            wires.start((N.dm_chip, k, m), [(source, b(N.dm_chip_in, m).at[k - 1], wires.chip(k))])

    def dm_chip(m):
        for k in range(1, chips):
            wires.arrived((N.dm_chip, k, m), b(N.dm_chip_in, m).at[k - 1])
        step(add_lead_kernel, [b(N.dm_sum, m).at[0:length], b(N.dm_chip_in, m)], [b(N.dm, m)])
        wires.start((N.dm, m), [(b(N.dm, m), b(N.d_memory, m), wires.across)])

    def memory_start(m):
        arrived = b(N.memory, m)
        wires.arrived((N.m, m), arrived.at[0])
        gather_start(wires, (N.m, m), arrived.at[0], arrived)

    def weights(products, out, regroup=0):
        operands, plan = [], []
        for lefts, rights, column in products:
            n, count = len(operands), len(lefts)
            operands += list(lefts) + list(rights)
            plan.append((tuple(range(n, n + count)), tuple(range(n + count, n + 2 * count)), column))
        scratch = (pltpu.VMEM(out.shape, F32),) if regroup else ()
        step(functools.partial(weight_kernel, plan, regroup), operands, [out], scratch)

    def all_b(name):
        return [b(name, m) for m in ticks]

    def cross_weights():
        regroup = width // 2 // (dp_size * wires.seq_size) if pieces else 0
        weights(
            [
                (all_b(N.low_hidden), all_b(N.dcq), 0),
                ([memory(m) for m in ticks], all_b(N.dckv), width),
                (all_b(N.cross_mixed), all_b(N.dyc), 3 * width),
            ],
            hbm[N.g_cross],
            regroup,
        )

    def out_weights():
        weights([(all_b(N.act), all_b(N.dy3), 0)], hbm[N.g_out])

    def in_weights():
        weights([(all_b(N.low_middle), all_b(N.d_inner), 0)], hbm[N.g_in])

    def attn_weights():
        weights(
            [
                ([hbm[N.x].at[m] for m in ticks], all_b(N.dq), 0),
                ([inputs(m) for m in ticks], all_b(N.dkv), width),
                (all_b(N.mixed), all_b(N.dy), 3 * width),
            ],
            hbm[N.g_attn],
        )

    units = {}
    for piece in pieces:
        units.setdefault(piece[1], []).append(Sums(wires, hbm, *piece))

    def stage(unit, which):
        for sums in units.get(unit, ()):
            which(sums)

    wires.barrier()
    gather_start(wires, N.i, hbm[N.ids], hbm[N.ids_all])
    gather_start(wires, (N.x, 0), hbm[N.x].at[0], b(N.x_all, 0))
    gather_pass(wires, N.i, hbm[N.ids_all])
    gather_end(wires, N.i, hbm[N.ids_all])
    step(
        functools.partial(mask_kernel, micro),
        [hbm[N.ids], hbm[N.ids_all]],
        all_b(N.self_bias) + all_b(N.cross_bias),
    )
    gather_pass(wires, (N.x, 0), b(N.x_all, 0))
    for m in range(1, micro):
        gather_start(wires, (N.x, m), hbm[N.x].at[m], b(N.x_all, m))
    for n in (N.vec, N.w_qkv, N.w_mix):
        held_copies[n].wait()
    gather_end(wires, (N.x, 0), b(N.x_all, 0))
    self_forward(0)
    for n in held_names:
        if n not in (N.vec, N.w_qkv, N.w_mix):
            held_copies[n].wait()
    for m in range(1, micro):
        gather_pass(wires, (N.x, m), b(N.x_all, m))

    @wires.only(0)
    def _():
        for m in ticks:
            ffn_forward(m, N.hidden)
            wires.start((N.m, m), [(hbm[N.layer_out].at[m], b(N.memory, m).at[0], wires.across)])
            if m < last:
                gather_end(wires, (N.x, m + 1), b(N.x_all, m + 1))
                self_forward(m + 1)
        for m in ticks:
            wires.arrived((N.dm, m), b(N.d_memory, m))
            if m < last:
                ffn_back(m, b(N.d_memory, m))
                self_back(m)
                dx_core(m)
        step(
            ffn_norm_kernel,
            [b(N.d_memory, last), b(N.final_sum, last), vec],
            [b(N.dy3, last), hbm[N.d_final], hbm[N.norm_small]],
        )

    @wires.only(1)
    def _():
        for m in range(1, micro):
            gather_end(wires, (N.x, m), b(N.x_all, m))
            self_forward(m)
        memory_start(0)
        gather_pass(wires, (N.m, 0), b(N.memory, 0))
        for m in ticks:
            gather_end(wires, (N.m, m), b(N.memory, m))
            cross_forward(m)
            if m < last:
                memory_start(m + 1)
            if m > 0:
                dm_core(m - 1)
            ffn_forward(m, N.middle)
            if m < last:
                gather_pass(wires, (N.m, m + 1), b(N.memory, m + 1))
            ffn_back(m, hbm[N.cotangent].at[m])
            if m > 0:
                dm_chip(m - 1)
            cross_back(m)
            dm_start(m)
        dm_core(last)
        cross_weights()
        dm_chip(last)
        stage(N.g_cross, Sums.core_start)

    out_weights()
    stage(N.g_out, Sums.core_start)

    @wires.only(0)
    def _():
        step(
            ffn_rest_kernel,
            [b(N.dy3, last), hbm[N.d_final], hbm[N.norm_small], held[N.w_out], b(N.slope, last), held[N.w_in]],
            [b(N.d_inner, last), b(N.d_middle, last), b(N.ffn_small, last)],
        )

    @wires.only(1)
    def _():
        stage(N.g_cross, Sums.core_add)

    stage(N.g_out, Sums.core_add)
    in_weights()
    stage(N.g_in, Sums.core_start)

    @wires.only(1)
    def _():
        for m in range(last):
            self_back(m)

    stage(N.g_in, Sums.core_add)

    @wires.only(1)
    def _():
        for m in range(last):
            dx_core(m)
        stage(N.g_cross, Sums.second_add)

    self_back(last)
    attn_weights()
    stage(N.g_attn, Sums.core_start)
    step(
        functools.partial(small_kernel, micro),
        all_b(N.self_small) + all_b(N.ffn_small) + all_b(N.squares) + all_b(N.cross_small),
        [hbm[N.small]],
    )
    wires.start(N.small_core, [(hbm[N.small], hbm[N.small_core_in], wires.twin)])
    stage(N.g_attn, Sums.core_add)
    stage(N.g_out, Sums.second_add)
    dx_core(last)
    wires.arrived(N.small_core, hbm[N.small_core_in])
    step(add_kernel, [hbm[N.small], hbm[N.small_core_in]], [hbm[N.small_core_sum]])
    for k in range(1, chips):
        wires.start((N.small_chip, k), [(hbm[N.small_core_sum], hbm[N.small_chip_in].at[k - 1], wires.chip(k))])

    @wires.only(1)
    def _():
        stage(N.g_cross, Sums.third_add)
        if pieces:
            half = width // 2 // (dp_size * wires.seq_size)
            wires.start(N.cross_half, [(hbm[N.g_cross, N.out].at[0:half], hbm[N.cross_half], wires.across)])

    stage(N.g_in, Sums.second_add)
    for k in range(1, chips):
        wires.arrived((N.small_chip, k), hbm[N.small_chip_in].at[k - 1])
    step(add_lead_kernel, [hbm[N.small_core_sum], hbm[N.small_chip_in]], [hbm[N.small_chip_sum]])
    moves = [(hbm[N.small_chip_sum], hbm[N.small_row_in].at[k - 1], wires.row(k)) for k in range(1, dp_size)]
    wires.start(N.small_row, moves, hbm[N.small_row_in])
    for m in range(last):
        dx_end(m)
    stage(N.g_out, Sums.third_add)
    stage(N.g_attn, Sums.second_add)
    dx_end(last)
    wires.arrived(N.small_row, hbm[N.small_row_in])
    step(add_lead_kernel, [hbm[N.small_chip_sum], hbm[N.small_row_in]], [hbm[N.small_sum]])

    @wires.only(1)
    def _():
        wires.start(N.small_half, [(hbm[N.small_sum].at[16:24], hbm[N.small_half], wires.across)])

    stage(N.g_in, Sums.third_add)
    stage(N.g_attn, Sums.third_add)

    @wires.only(0)
    def _():
        wires.arrived(N.small_half, hbm[N.small_half])
        if pieces:
            wires.arrived(N.cross_half, hbm[N.cross_half])

    wires.close()


def shaped(*shape, kind=F32):
    return jax.ShapeDtypeStruct(shape, kind)


def pick(stacked, position):
    return lax.dynamic_index_in_dim(stacked, position, 0, keepdims=False)


def section_permute(x, axis, pairs, only):
    if only is None:
        return lax.ppermute(x, axis, pairs)
    first = only * lax.axis_size(axis)
    return lax.ppermute(x, ("section", axis), [(first + i, first + j) for i, j in pairs])


def group_permute(x, axis, members, stride, step, only=None):
    pairs = []
    for i in range(lax.axis_size(axis)):
        at = (i // stride) % members
        pairs.append((i, i + ((at + step) % members - at) * stride))
    return section_permute(x, axis, pairs, only)


def place_in(axis, members, stride):
    return (lax.axis_index(axis) // stride) % members


class Scatter:
    def __init__(self, parts, only=None):
        self.dp, self.chips = lax.axis_size("dp"), lax.axis_size("seq") // 2
        self.only, self.kind = only, parts.dtype
        self.parts = jnp.moveaxis(parts, 2, 0)
        self.stages = [("seq", 2, 1), ("seq", self.chips, 2), ("dp", self.dp, 1)]

    def send(self):
        axis, members, stride = self.stages[0]
        mine = place_in(axis, members, stride)
        self.keep = pick(self.parts, mine)
        return [pick(self.parts, (mine + step) % members) for step in range(1, members)]

    def arrive(self, sent):
        axis, members, stride = self.stages.pop(0)
        total = self.keep.astype(F32)
        for step in range(1, members):
            total = total + group_permute(sent[step - 1], axis, members, stride, step, self.only).astype(F32)
        if not self.stages:
            return total
        total = total.astype(self.kind)
        self.parts = jnp.moveaxis(total, 1, 0) if len(self.stages) == 2 else total
        return None

    def finish(self, sent=None):
        while self.stages:
            total = self.arrive(self.send() if sent is None else sent)
            sent = None
        return total


def by_device(total):
    dp_size, seq_size = lax.axis_size("dp"), lax.axis_size("seq")
    return total.reshape(dp_size, seq_size // 2, 2, total.shape[0] // (dp_size * seq_size), *total.shape[1:])


def to_encoder_half(total, section):
    half = total.shape[0] // 2
    arrived = lax.ppermute(total[:half], "section", [(1, 0)])
    return jnp.where(section == 0, arrived, total[half:])


def kernel_call(body, outs, operands, scratch, collective_id, flops, name):
    anywhere = pl.BlockSpec(memory_space=pltpu.HBM)
    size = sum(math.prod(o.shape) * o.dtype.itemsize for o in list(outs) + list(operands))
    return pl.pallas_call(
        body,
        out_shape=list(outs),
        in_specs=[anywhere] * len(operands),
        out_specs=[anywhere] * len(outs),
        scratch_shapes=scratch,
        cost_estimate=pl.CostEstimate(flops=int(flops), bytes_accessed=int(size), transcendentals=0),
        compiler_params=pltpu.CompilerParams(
            vmem_limit_bytes=VMEM_LIMIT, collective_id=collective_id, has_side_effects=True
        ),
        name=name,
    )(*operands)


def per_device(
    x_in, segments, cotangent, attn_in, attn_out, attn_bias, gains, ffn_in, ffn_bias, ffn_out,
    cross_q, cross_kv, cross_out, cross_bias, cross_gain,
):
    section = lax.axis_index("section")
    micro, length, width = x_in.shape[1], x_in.shape[3], x_in.shape[4]
    dp_size, seq_size = lax.axis_size("dp"), lax.axis_size("seq")
    chips = seq_size // 2
    devices = dp_size * seq_size
    tokens = length * seq_size
    hidden_units = ffn_in.shape[2]
    fused = width // devices % 16 == 0
    ticks = range(micro)
    x = x_in[0, :, 0]
    vec = jnp.concatenate([attn_bias[0], gains[0]], 0)
    cross_vec = jnp.concatenate([cross_bias, cross_gain[None], jnp.zeros((3, width), F32)], 0)

    ids = segments[:, :, 0].reshape(2 * micro, length)
    ids = jnp.concatenate([ids, jnp.zeros((-2 * micro % 8, length), ids.dtype)], 0)
    arrays = {
        N.x: x,
        N.ids: ids,
        N.cotangent: cotangent[:, 0],
        N.w_qkv: attn_in[0],
        N.w_mix: attn_out[0],
        N.w_in: ffn_in[0],
        N.w_out: ffn_out[0],
        N.b_in: ffn_bias,
        N.vec: vec,
        N.cross_q: cross_q,
        N.cross_kv: cross_kv,
        N.cross_out: cross_out,
        N.cross_vec: cross_vec,
    }
    lw, lw_low = shaped(length, width), shaped(length, width, kind=BF16)
    tw_low = shaped(tokens, width, kind=BF16)
    lh_low = shaped(length, hidden_units, kind=BF16)
    pair_low = shaped(tokens, 2 * width, kind=BF16)
    half_low = shaped(tokens // 2, width, kind=BF16)
    rest_low = shaped(max(tokens // 2 - length, length), width, kind=BF16)
    far_low = shaped(max(chips - 1, 1), length, width, kind=BF16)
    seq_low = shaped(seq_size, length, width, kind=BF16)
    mask = shaped(length, tokens)
    lse_shape, few = shaped(HEADS // 2, length, PAIR), shaped(8, width)
    kinds = {
        N.q: lw_low, N.k: tw_low, N.v: tw_low, N.mixed: lw_low, N.lse: lse_shape, N.summed: lw, N.hidden: lw, N.squares: few,
        N.act: lh_low, N.slope: lh_low, N.final_sum: lw, N.low_middle: lw_low,
        N.dy3: lw_low, N.d_inner: lh_low, N.d_middle: lw, N.ffn_small: few,
        N.cq: lw_low, N.ck: tw_low, N.cv: tw_low, N.cross_mixed: lw_low, N.cross_lse: lse_shape, N.cross_sum: lw,
        N.middle: lw, N.low_hidden: lw_low,
        N.dyc: lw_low, N.dcq: lw_low, N.dckv: pair_low, N.dm_keep: half_low, N.dm_send: half_low,
        N.cross_small: few, N.dm_core_in: half_low, N.dm_sum: half_low, N.dm_chip_in: far_low, N.dm: lw_low, N.d_memory: lw_low,
        N.dy: lw_low, N.dq: lw_low, N.dkv: pair_low, N.dx_own: lw, N.dx_keep: rest_low, N.dx_send: half_low, N.self_small: few,
        N.dx_core_in: half_low, N.dx_sum: lw, N.dx_rest: rest_low, N.dx_chip_in: far_low,
        N.x_all: seq_low, N.memory: seq_low, N.self_bias: mask, N.cross_bias: mask,
    }
    outs = {(n, m): kind for m in ticks for n, kind in kinds.items()}
    for n in (N.layer_out, N.input_grad):
        outs[n] = shaped(micro, length, width, kind=BF16)
    outs[N.ids_all] = shaped(seq_size, *ids.shape, kind=ids.dtype)
    outs[N.d_final], outs[N.norm_small] = lw, few
    small_shape = shaped(24, width)
    for n in (N.small, N.small_core_in, N.small_core_sum, N.small_chip_sum, N.small_sum):
        outs[n] = small_shape
    outs[N.small_chip_in] = shaped(max(chips - 1, 1), 24, width)
    outs[N.small_row_in] = shaped(max(dp_size - 1, 1), 24, width)
    outs[N.small_half] = few
    totals = {
        N.g_cross: (width, 4 * width), N.g_out: (hidden_units, width), N.g_in: (width, hidden_units), N.g_attn: (width, 4 * width),
    }
    wire_names = [N.small_core, N.small_row, N.small_half] + [(N.small_chip, k) for k in range(1, chips)]
    for m in ticks:
        wire_names += gather_names((N.m, m), chips) + gather_names((N.x, m), chips)
        wire_names += [(N.m, m), (N.dm, m), (N.dm_core, m), (N.dx_core, m)]
        wire_names += [(n, k, m) for n in (N.dm_chip, N.dx_chip) for k in range(1, chips)]
    pieces = sum_pieces(totals, devices) if fused else []
    for n, total in totals.items():
        outs[n] = shaped(*total, kind=BF16)
        if fused:
            outs[n, N.out] = shaped(total[0] // devices, total[1])
    for key, n, _, rows, dp_first in pieces:
        outs.update(sum_shapes(key, rows, totals[n][1], dp_first, dp_size, chips))
        wire_names += sum_names(key, chips)
    if fused:
        outs[N.cross_half] = shaped(width // 2 // devices, 4 * width)
        wire_names.append(N.cross_half)
    wire_names += gather_names(N.i, chips)
    held_names = [N.vec, N.w_qkv, N.w_mix, N.w_in, N.b_in, N.w_out, N.cross_vec, N.cross_q, N.cross_kv, N.cross_out]
    scratch = [pltpu.VMEM(arrays[n].shape, arrays[n].dtype) for n in held_names]
    scratch += [pltpu.SemaphoreType.DMA((len(wire_names),))] * 2 + [pltpu.SemaphoreType.DMA((len(held_names),))]
    results = kernel_call(
        functools.partial(main_body, micro, pieces, list(arrays), list(outs), wire_names, held_names),
        list(outs.values()),
        list(arrays.values()),
        scratch,
        0,
        6 * micro * length * width * (12 * width + 2 * hidden_units),
        "layers",
    )
    results = dict(zip(outs, results))

    if fused:
        cross_part = None
        attn_part, ffn_in_part, ffn_out_part = (results[n, N.out] for n in (N.g_attn, N.g_in, N.g_out))
        cross_parts = [results[N.cross_half], results[N.g_cross, N.out]]
    else:
        halves = results[N.g_cross].reshape(2, width // 2, 4 * width)
        halves = jnp.stack([by_device(halves[0]), by_device(halves[1])], 3)
        cross_part = Scatter(halves, 1).finish()
        cross_part = jnp.where(
            section == 0, lax.ppermute(cross_part[0], "section", [(1, 0)]), cross_part[1]
        )
        attn_part, ffn_in_part, ffn_out_part = (
            Scatter(by_device(results[n])).finish() for n in (N.g_attn, N.g_in, N.g_out)
        )
        cross_parts = [cross_part]
    per, half, per_hidden = width // devices, width // 2 // devices, hidden_units // devices
    operands = [
        results[N.layer_out], results[N.input_grad], attn_part, ffn_in_part, ffn_out_part,
        results[N.small_sum], results[N.small_half], *cross_parts,
    ]
    final_shapes = [
        shaped(micro, length, width, kind=BF16),
        shaped(micro, length, width, kind=BF16),
        shaped(per, 3 * width),
        shaped(per, width),
        shaped(per, hidden_units),
        shaped(per_hidden, width),
        shaped(half, width),
        shaped(half, 2 * width),
        shaped(half, width),
        shaped(1, 2),
        shaped(6, per),
        shaped(2, per),
        shaped(1, per_hidden),
        shaped(4, half),
        shaped(1, half),
    ]
    anywhere = pl.BlockSpec(memory_space=pltpu.HBM)
    finals = pl.pallas_call(
        functools.partial(final_body, micro * dp_size * tokens * width, len(operands)),
        out_shape=final_shapes,
        in_specs=[anywhere] * len(operands),
        out_specs=[anywhere] * len(final_shapes),
        scratch_shapes=[pltpu.VMEM(o.shape, o.dtype) for o in operands + final_shapes[9:]]
        + [pltpu.SemaphoreType.DMA((len(operands),)), pltpu.SemaphoreType.DMA((len(final_shapes),))],
    )(*operands)
    (layer_out, input_grad, attn_in_grad, attn_out_grad, ffn_in_grad, ffn_out_grad, cross_q_grad, cross_kv_grad,
     cross_out_grad, stats, attn_bias_grad, gains_grad, ffn_bias_grad, cross_bias_grad, cross_gain_grad) = finals
    return (
        layer_out[None, :, None],
        input_grad[None, :, None],
        stats,
        attn_in_grad[None],
        attn_out_grad[None],
        attn_bias_grad[None],
        gains_grad[None],
        ffn_in_grad[None],
        ffn_bias_grad,
        ffn_out_grad[None],
        cross_q_grad,
        cross_kv_grad,
        cross_out_grad,
        cross_bias_grad,
        cross_gain_grad[0],
    )


def solution(mesh):
    return jax.shard_map(
        per_device,
        mesh=mesh,
        in_specs=(
            P("section", None, "dp", "seq", None),
            P(None, None, "dp", "seq"),
            P(None, "dp", "seq", None),
            P("section", None, None),
            P("section", None, None),
            P("section", None, None),
            P("section", None, None),
            P("section", None, None),
            P("section", None),
            P("section", None, None),
            P(),
            P(),
            P(),
            P(),
            P(),
        ),
        out_specs=(
            P("section", None, "dp", "seq", None),
            P("section", None, "dp", "seq", None),
            P("section", None),
            P("section", ("dp", "seq"), None),
            P("section", ("dp", "seq"), None),
            P("section", None, ("dp", "seq")),
            P("section", None, ("dp", "seq")),
            P("section", ("dp", "seq"), None),
            P("section", ("dp", "seq")),
            P("section", ("dp", "seq"), None),
            P(("section", "dp", "seq"), None),
            P(("section", "dp", "seq"), None),
            P(("section", "dp", "seq"), None),
            P(None, ("section", "dp", "seq")),
            P(("section", "dp", "seq")),
        ),
        check_vma=False,
    )
```

```python
import enum
import functools
import math

import jax
import jax.numpy as jnp
from jax import lax
from jax.experimental import pallas as pl
from jax.experimental.pallas import tpu as pltpu
from jax.sharding import PartitionSpec as P

HEADS = 12
HEAD_DIM = 64
PAIR = 2 * HEAD_DIM
EPSILON = 1e-05
MASKED = -1000000000.0
SCALE = 1.0 / math.sqrt(HEAD_DIM)
VMEM_LIMIT = 58 * 1024 * 1024

F32 = jnp.float32
BF16 = jnp.bfloat16


def mm(a, b):
    return jnp.dot(a, b, preferred_element_type=F32)


def mm_nt(a, b):
    return lax.dot_general(a, b, (((1,), (1,)), ((), ())), preferred_element_type=F32)


def norm_parts(tensor):
    average = jnp.mean(tensor, -1, keepdims=True)
    centered = tensor - average
    spread = jnp.mean(centered * centered, -1, keepdims=True)
    scale = lax.rsqrt(spread + EPSILON)
    return centered * scale, scale


def norm_back(tensor, gain, grad):
    normed, scale = norm_parts(tensor)
    scaled = gain * grad
    product = grad * normed
    first = jnp.mean(scaled, -1, keepdims=True)
    second = jnp.mean(scaled * normed, -1, keepdims=True)
    out = (scaled - first - normed * second) * scale
    return out, jnp.sum(product, 0, keepdims=True), jnp.sum(grad, 0, keepdims=True)


def column_sum(tensor):
    return jnp.sum(tensor.astype(F32), 0, keepdims=True)


def gelu_pair(x):
    bell = jnp.exp(-0.5 * x * x)
    t = 1.0 / (1.0 + (0.3275911 / math.sqrt(2.0)) * jnp.abs(x))
    poly = t * (
        0.5 * 0.254829592
        + t
        * (
            0.5 * -0.284496736
            + t * (0.5 * 1.421413741 + t * (0.5 * -1.453152027 + t * (0.5 * 1.061405429)))
        )
    )
    tail = poly * bell
    cdf = jnp.where(x < 0, tail, 1.0 - tail)
    return x * cdf, cdf + x * bell * (1.0 / math.sqrt(2.0 * math.pi))


def row_blocks(count, body):
    step = min(256, count)

    def run(i, carry):
        body(pl.ds(pl.multiple_of(i * step, step), step))
        return carry

    lax.fori_loop(0, count // step, run, 0, unroll=True)


def head_halves(rows):
    lane = lax.broadcasted_iota(jnp.int32, (rows, PAIR), 1)
    return lane < HEAD_DIM, lane >= HEAD_DIM


def attend_forward(q_ref, k_ref, v_ref, bias_ref, mixed_ref, lse_ref):
    query_halves, key_halves = head_halves(q_ref.shape[0]), head_halves(k_ref.shape[0])

    def pair(p, carry):
        lanes = pl.ds(pl.multiple_of(p * PAIR, PAIR), PAIR)
        keys, values = k_ref[:, lanes], v_ref[:, lanes]
        queries = q_ref[:, lanes] * SCALE
        outs, peaks = [], []
        for a in range(2):
            own = jnp.where(query_halves[a], queries, jnp.zeros_like(queries))
            scores = mm_nt(own, keys) + bias_ref[...]
            peak = jnp.max(scores, 1, keepdims=True)
            weights = jnp.exp(scores - peak).astype(BF16)
            outs.append(mm(weights, jnp.where(key_halves[a], values, jnp.ones_like(values))))
            peaks.append(peak)
        first = query_halves[0]
        total = pltpu.roll(jnp.where(first, outs[1], outs[0]), HEAD_DIM, 1)
        lse_ref[p] = jnp.where(first, peaks[0], peaks[1]) + jnp.log(total)
        mixed_ref[:, lanes] = (jnp.where(first, outs[0], outs[1]) * (1.0 / total)).astype(BF16)
        return carry

    lax.fori_loop(0, HEADS // 2, pair, 0, unroll=2)


def attend_back(q_ref, k_ref, v_ref, grad_ref, mixed_ref, lse_ref, bias_ref, dq_ref, dkv_ref):
    length, width = q_ref.shape
    halves = head_halves(length)

    def pair(p, carry):
        lanes = pl.ds(pl.multiple_of(p * PAIR, PAIR), PAIR)
        value_lanes = pl.ds(pl.multiple_of(width + p * PAIR, PAIR), PAIR)
        keys, values = k_ref[:, lanes], v_ref[:, lanes]
        queries = q_ref[:, lanes] * SCALE
        grads = grad_ref[:, lanes]
        product = grads.astype(F32) * mixed_ref[:, lanes].astype(F32)
        queries_t, grads_t = queries.T, grads.T
        outs, key_grads, value_grads = [], [], []
        for a, half in enumerate(halves):
            own = jnp.where(half, queries, jnp.zeros_like(queries))
            own_grad = jnp.where(half, grads, jnp.zeros_like(grads))
            rows = slice(a * HEAD_DIM, (a + 1) * HEAD_DIM)
            lse = lse_ref[p, :, a * HEAD_DIM : a * HEAD_DIM + 1]
            delta = jnp.sum(jnp.where(half, product, 0.0), 1, keepdims=True)
            weights = jnp.exp(mm_nt(own, keys) + bias_ref[...] - lse)
            score_grad = (weights * (mm_nt(own_grad, values) - delta)).astype(BF16)
            outs.append(mm(score_grad, keys))
            key_grads.append(mm(queries_t[rows], score_grad))
            value_grads.append(mm(grads_t[rows], weights.astype(BF16)))
        dkv_ref[:, lanes] = jnp.concatenate(key_grads, 0).astype(BF16).T
        dkv_ref[:, value_lanes] = jnp.concatenate(value_grads, 0).astype(BF16).T
        dq_ref[:, lanes] = (jnp.where(halves[0], outs[0], outs[1]) * SCALE).astype(BF16)
        return carry

    lax.fori_loop(0, HEADS // 2, pair, 0, unroll=2)


def self_kernel(io, x_ref, w_qkv, w_mix, vec, bias, q_out, k_out, v_out, mixed, lse, summed, hidden, squares):
    length, width = q_out.shape
    io.ready(x_ref, w_qkv, vec)
    x_own = x_ref[0:length, :]
    q_out[...] = (mm(x_own, w_qkv[:, 0:width]) + vec[0:1, :]).astype(BF16)

    def keys(rows):
        x = x_ref[rows, :]
        k_out[rows, :] = mm(x, w_qkv[:, width : 2 * width]).astype(BF16)
        v_out[rows, :] = (mm(x, w_qkv[:, 2 * width : 3 * width]) + vec[1:2, :]).astype(BF16)

    row_blocks(x_ref.shape[0], keys)
    io.done(q_out, k_out, v_out)
    io.ready(bias)
    attend_forward(q_out, k_out, v_out, bias, mixed, lse)
    io.done(mixed, lse)
    io.ready(w_mix)
    branch = mm(mixed[...], w_mix[...]) + vec[2:3, :]
    total = x_own.astype(F32) + branch
    summed[...] = total
    squares[...] = jnp.zeros_like(squares)
    squares[0:1, :] = column_sum(total * total)
    squares[1:2, :] = column_sum(branch * branch)
    hidden[...] = norm_parts(total)[0] * vec[6:7, :] + vec[4:5, :]


def ffn_kernel(io, middle, vec, w_in, b_in, w_out, act, slope, final_sum, low_middle, result):
    width = middle.shape[1]
    chunks = w_in.shape[1] // width
    io.ready(middle, vec)
    mid = middle[...]
    low = mid.astype(BF16)
    low_middle[...] = low
    final_sum[...] = mid + vec[3:4, :]
    io.ready(w_in, b_in, w_out)

    def chunk(j, carry):
        columns = pl.ds(pl.multiple_of(j * width, width), width)
        inner = mm(low, w_in[:, columns]) + b_in[:, columns]
        value, derivative = gelu_pair(inner)
        value = value.astype(BF16)
        act[:, columns] = value
        slope[:, columns] = derivative.astype(BF16)
        final_sum[...] += mm(value, w_out[columns, :])
        return carry

    lax.fori_loop(0, chunks, chunk, 0, unroll=True)
    io.done(act, slope, low_middle, final_sum)
    result[...] = (norm_parts(final_sum[...])[0] * vec[7:8, :] + vec[5:6, :]).astype(BF16)


def ffn_norm_kernel(io, grad, final_sum, vec, dy, d_final, small):
    io.ready(grad, final_sum, vec)
    back, d_gain, d_shift = norm_back(final_sum[...], vec[7:8, :], grad[...].astype(F32))
    low = back.astype(BF16)
    dy[...] = low
    d_final[...] = back
    small[...] = jnp.zeros_like(small)
    small[0:1, :] = d_gain
    small[1:2, :] = d_shift
    small[2:3, :] = column_sum(low)


def ffn_rest_kernel(io, dy, d_final, small_in, w_out, slope, w_in, d_inner, d_middle, small):
    width = dy.shape[1]
    chunks = w_in.shape[1] // width
    io.ready(dy, d_final, small_in, w_out, slope, w_in)
    low = dy[...]
    small[...] = small_in[...]
    d_middle[...] = d_final[...]

    def chunk(j, carry):
        columns = pl.ds(pl.multiple_of(j * width, width), width)
        d_act = mm_nt(low, w_out[columns, :])
        inner = (d_act * slope[:, columns].astype(F32)).astype(BF16)
        d_inner[:, columns] = inner
        small[pl.ds(3 + j, 1), :] = column_sum(inner)
        d_middle[...] += mm_nt(inner, w_in[:, columns])
        return carry

    lax.fori_loop(0, chunks, chunk, 0, unroll=True)


def ffn_back_kernel(io, grad, final_sum, vec, w_out, slope, w_in, dy, d_inner, d_middle, small):
    ffn_norm_kernel(io, grad, final_sum, vec, dy, d_middle, small)
    io.done(dy)
    ffn_rest_kernel(io, dy, d_middle, small, w_out, slope, w_in, d_inner, d_middle, small)


def mask_kernel(micro, io, ids, far, *outs):
    io.ready(ids, far)
    length = ids.shape[1]
    section, me, blocks = lax.axis_index("section"), lax.axis_index("seq"), lax.axis_size("seq")
    orders = []
    for k in range(blocks // 2):
        chip = (me + 2 * k) % blocks
        orders += [chip, chip + 1 - 2 * (me % 2)]
    here = lax.broadcasted_iota(jnp.int32, (length, length), 0)
    there = lax.broadcasted_iota(jnp.int32, (length, length), 1)
    for m in range(micro):
        own = jnp.where(section == 0, ids[m : m + 1, :], ids[micro + m : micro + m + 1, :])
        query = jnp.broadcast_to(own.astype(F32), (PAIR, length)).T[:, 0:1]
        for j, order in enumerate(orders):
            block = ids if j == 0 else far.at[j]
            source, target = block[m : m + 1, :], block[micro + m : micro + m + 1, :]
            key = jnp.where(section == 0, source, target).astype(F32)
            late = (there + order * length > here + orders[0] * length) & (section == 1)
            columns = slice(j * length, (j + 1) * length)
            outs[m][:, columns] = jnp.where((query == key) & jnp.logical_not(late), 0.0, MASKED)
            outs[micro + m][:, columns] = jnp.where(query == source.astype(F32), 0.0, MASKED)


def cross_kernel(
    io, hidden, w_q, vec, memory, w_kv, bias, w_o,
    cq, ck, cv, mixed, lse, summed, middle, low_hidden,
):
    width = hidden.shape[1]
    io.ready(hidden, w_q, vec)
    low = hidden[...].astype(BF16)
    low_hidden[...] = low
    cq[...] = (mm(low, w_q[...]) + vec[0:1, :]).astype(BF16)
    io.ready(memory, w_kv)

    def keys(rows):
        mem = memory[rows, :]
        ck[rows, :] = mm(mem, w_kv[:, 0:width]).astype(BF16)
        cv[rows, :] = (mm(mem, w_kv[:, width : 2 * width]) + vec[1:2, :]).astype(BF16)

    row_blocks(memory.shape[0], keys)
    io.done(cq, ck, cv, low_hidden)
    io.ready(bias)
    attend_forward(cq, ck, cv, bias, mixed, lse)
    io.done(mixed, lse)
    io.ready(w_o)
    total = hidden[...] + mm(mixed[...], w_o[...]) + vec[2:3, :]
    summed[...] = total
    middle[...] = norm_parts(total)[0] * vec[4:5, :] + vec[3:4, :]


def cross_back_kernel(
    io, d_middle, summed, vec, w_o, mixed, cq, ck, bias, lse, cv, w_q, w_kv,
    dyc, dcq, dckv, d_hidden, keep, send, small, d_mixed,
):
    length, width = d_middle.shape
    io.ready(d_middle, summed, vec)
    d_cross, d_gain, d_shift = norm_back(summed[...], vec[4:5, :], d_middle[...])
    low = d_cross.astype(BF16)
    dyc[...] = low
    d_hidden[...] = d_cross
    io.ready(w_o, mixed)
    grads = mm_nt(low, w_o[...]).astype(BF16)
    d_mixed[...] = grads
    io.ready(cq, ck, bias, lse, cv)
    attend_back(cq, ck, cv, d_mixed, mixed, lse, bias, dcq, dckv)
    io.ready(w_q, w_kv)
    for block in range(dckv.shape[0] // length):
        target = keep if block % 2 == 0 else send
        rows = slice(block // 2 * length, (block // 2 + 1) * length)
        target[rows, :] = mm_nt(dckv[block * length : (block + 1) * length, :], w_kv[...]).astype(BF16)
    io.done(send, keep, dyc, dcq, dckv)
    d_hidden[...] += mm_nt(dcq[...], w_q[...])
    io.sent(send)
    small[...] = jnp.zeros_like(small)
    small[0:1, :] = d_gain
    small[1:2, :] = d_shift
    small[2:3, :] = column_sum(low)
    small[3:4, :] = column_sum(dcq[...])
    small[4:5, :] = column_sum(dckv[:, width : 2 * width])


def self_back_kernel(
    io, grad, summed, vec, w_mix, mixed, q, k, bias, lse, v, w_qkv,
    dy, dq, dkv, own, keep, send, small, d_mixed,
):
    length, width = q.shape
    io.ready(grad, summed, vec)
    d_sum, d_gain, d_shift = norm_back(summed[...], vec[6:7, :], grad[...])
    low = d_sum.astype(BF16)
    dy[...] = low
    own[...] = d_sum
    io.ready(w_mix, mixed)
    grads = mm_nt(low, w_mix[...]).astype(BF16)
    d_mixed[...] = grads
    io.ready(q, k, bias, lse, v)
    attend_back(q, k, v, d_mixed, mixed, lse, bias, dq, dkv)
    io.done(dy, dq, dkv)
    io.ready(w_qkv)
    for block in range(dkv.shape[0] // length):
        part = mm_nt(dkv[block * length : (block + 1) * length, :], w_qkv[:, width : 3 * width])
        if block == 0:
            own[...] += part + mm_nt(dq[...], w_qkv[:, 0:width])
            continue
        target = keep if block % 2 == 0 else send
        at = (block - 2) // 2 if block % 2 == 0 else block // 2
        target[at * length : (at + 1) * length, :] = part.astype(BF16)
    io.done(send, keep, own)
    io.sent(send)
    small[...] = jnp.zeros_like(small)
    small[0:1, :] = d_gain
    small[1:2, :] = d_shift
    small[2:3, :] = column_sum(low)
    small[3:4, :] = column_sum(dq[...])
    small[4:5, :] = column_sum(dkv[:, width : 2 * width])


def weight_kernel(plan, regroup, io, *refs):
    out = refs[-1] if regroup == 0 else refs[-2]
    wide_out = out if regroup == 0 else refs[-1]
    for lefts, rights, column in plan:
        inner = refs[lefts[0]].shape[1]
        cols = refs[rights[0]].shape[1]
        step = 256
        wide = min(cols, 1536)
        io.ready(*[refs[i] for i in lefts + rights])

        def tile(i, carry, lefts=lefts, rights=rights, column=column, cols=cols, wide=wide):
            rows = pl.ds(pl.multiple_of(i * step, step), step)
            turned = [refs[l][:, rows].T for l in lefts]
            for start in range(0, cols, wide):
                total = None
                for left, r in zip(turned, rights):
                    term = mm(left, refs[r][:, start : start + wide])
                    total = term if total is None else total + term
                wide_out[rows, column + start : column + start + wide] = total.astype(wide_out.dtype)
            return carry

        lax.fori_loop(0, inner // step, tile, 0, unroll=3)
    if regroup:
        half = out.shape[0] // 2

        def group(i, carry):
            first = wide_out[pl.ds(pl.multiple_of(i * regroup, regroup), regroup), :]
            second = wide_out[pl.ds(pl.multiple_of(half + i * regroup, regroup), regroup), :]
            rows = pl.ds(pl.multiple_of(2 * i * regroup, 2 * regroup), 2 * regroup)
            out[rows, :] = jnp.concatenate([first, second], 0).astype(BF16)
            return carry

        lax.fori_loop(0, half // regroup, group, 0)


def add_kernel(io, *refs):
    out = refs[-1]
    io.ready(*refs[:-1])
    total = refs[0][...].astype(F32)
    for ref in refs[1:-1]:
        total = total + ref[...].astype(F32)
    out[...] = total.astype(out.dtype)
    io.sent(out)


def add_lead_kernel(io, one, many, out):
    io.ready(one, many)
    total = one[...].astype(F32)
    for i in range(many.shape[0]):
        total = total + many[i].astype(F32)
    out[...] = total.astype(out.dtype)


def small_kernel(micro, io, *refs):
    out = refs[-1]
    ins = refs[:-1]
    io.ready(*ins)
    selfs, ffns, squares, crosses = (ins[i * micro : (i + 1) * micro] for i in range(4))
    out[...] = jnp.zeros_like(out)
    for ref in selfs:
        out[0:8, :] += ref[...]
    for ref in squares:
        out[5:7, :] += ref[0:2, :]
    for ref in ffns:
        out[8:16, :] += ref[...]
    for ref in crosses:
        out[16:24, :] += jnp.where(lax.axis_index("section") == 1, ref[...], 0.0)


class Moves:
    def __init__(self, loads, stores):
        self.loads, self.stores, self.hook = dict(loads), dict(stores), None
        self.started, self.loaded, self.stored = set(), set(), set()
        for copies in self.loads.values():
            for copy in copies:
                copy.start()

    def ready(self, *refs):
        for ref in refs:
            if id(ref) not in self.loaded:
                self.loaded.add(id(ref))
                for copy in self.loads.get(id(ref), ()):
                    copy.wait()

    def away(self, ref):
        self.done(ref)
        if id(ref) not in self.stored:
            self.stored.add(id(ref))
            for copy in self.stores.get(id(ref), ()):
                copy.wait()

    def done(self, *refs):
        for ref in refs:
            if id(ref) not in self.started:
                self.started.add(id(ref))
                for copy in self.stores.get(id(ref), ()):
                    copy.start()

    def sent(self, ref):
        self.done(ref)
        if self.hook is not None:
            self.away(ref)
            self.hook()

    def finish(self, ins, outs):
        self.ready(*ins)
        self.done(*outs)
        for ref in outs:
            self.away(ref)


class Held:
    def __init__(self, ref):
        self.ref = ref


class Rows:
    def __init__(self, pieces, shape=None):
        self.pieces = list(pieces)
        rest = self.pieces[0].shape[1:] if shape is None else shape[1:]
        count = sum(p.shape[0] for p in self.pieces) if shape is None else shape[0]
        self.shape, self.dtype = (count, *rest), self.pieces[0].dtype


def as_rows(item):
    return item if isinstance(item, Rows) else Rows([item])


def step(kernel, operands, outs, scratch=()):
    group((kernel, operands, outs, scratch))


def group(*parts):
    made, loads, load_at, outs, owner, scratches, plans = {}, [], {}, [], {}, [], []
    for part in parts:
        if callable(part):
            plans.append(part)
            continue
        kernel, operands, results, scratch, hook = (*part, None)[:5]
        ins = []
        for o in operands:
            if isinstance(o, Held):
                ins.append((0, o.ref))
            elif id(o) in made:
                ins.append((2, made[id(o)]))
            else:
                if id(o) not in load_at:
                    load_at[id(o)] = len(loads)
                    loads.append(as_rows(o))
                ins.append((1, load_at[id(o)]))
        first = len(outs)
        for o in results:
            made[id(o)] = owner[id(o)] = len(outs)
            outs.append(o)
        plans.append((kernel, ins, range(first, len(outs)), range(len(scratches), len(scratches) + len(scratch)), hook))
        scratches += list(scratch)
    stored = [owner[id(o)] == i for i, o in enumerate(outs)]
    rows_out = [as_rows(o) for o in outs]
    n_load = sum(len(o.pieces) for o in loads)
    n_store = sum(len(o.pieces) for o in rows_out)

    def pairs(ref, rows):
        if len(rows.pieces) == 1:
            return [(rows.pieces[0], ref)]
        found, at = [], 0
        for piece in rows.pieces:
            found.append((piece, ref.at[pl.ds(at, piece.shape[0])]))
            at += piece.shape[0]
        return found

    def inner(*refs):
        n_in, n_out = len(loads), len(outs)
        vmem_in, vmem_out = refs[:n_in], refs[n_in : n_in + n_out]
        in_sem, out_sem = refs[n_in + n_out : n_in + n_out + 2]
        extra = refs[n_in + n_out + 2 :]
        coming, at = [], 0
        for ref, rows in zip(vmem_in, loads):
            copies = []
            for hbm, vmem in pairs(ref, rows):
                copies.append(pltpu.make_async_copy(hbm, vmem, in_sem.at[at]))
                at += 1
            coming.append((id(ref), copies))
        going, at = [], 0
        for ref, rows, store in zip(vmem_out, rows_out, stored):
            copies = []
            for hbm, vmem in pairs(ref, rows) if store else ():
                copies.append(pltpu.make_async_copy(vmem, hbm, out_sem.at[at]))
                at += 1
            going.append((id(ref), copies))
        moves = Moves(coming, going)
        for plan in plans:
            if callable(plan):
                plan()
                continue
            kernel, ins, results, scratch, moves.hook = plan
            given = [(None, vmem_in, vmem_out)[kind][at] if kind else at for kind, at in ins]
            kernel(moves, *given, *[vmem_out[i] for i in results], *[extra[i] for i in scratch])
            moves.done(*[vmem_out[i] for i in results])
        moves.finish(vmem_in, vmem_out)

    pl.run_scoped(
        inner,
        *[pltpu.VMEM(o.shape, o.dtype) for o in loads],
        *[pltpu.VMEM(o.shape, o.dtype) for o in rows_out],
        pltpu.SemaphoreType.DMA((max(n_load, 1),)),
        pltpu.SemaphoreType.DMA((max(n_store, 1),)),
        *scratches,
    )


class N(enum.Enum):
    act = enum.auto()
    b_in = enum.auto()
    chip = enum.auto()
    chip_in = enum.auto()
    mid = enum.auto()
    d_final = enum.auto()
    norm_small = enum.auto()
    part = enum.auto()
    ids = enum.auto()
    ids_all = enum.auto()
    ck = enum.auto()
    core = enum.auto()
    core_in = enum.auto()
    core_sum = enum.auto()
    cotangent = enum.auto()
    cq = enum.auto()
    cross_bias = enum.auto()
    cross_half = enum.auto()
    cross_kv = enum.auto()
    cross_lse = enum.auto()
    cross_mixed = enum.auto()
    cross_out = enum.auto()
    cross_q = enum.auto()
    cross_small = enum.auto()
    cross_sum = enum.auto()
    cv = enum.auto()
    d_inner = enum.auto()
    d_memory = enum.auto()
    d_middle = enum.auto()
    dckv = enum.auto()
    dcq = enum.auto()
    dkv = enum.auto()
    dm = enum.auto()
    dm_chip = enum.auto()
    dm_chip_in = enum.auto()
    dm_core = enum.auto()
    dm_core_in = enum.auto()
    dm_keep = enum.auto()
    dm_send = enum.auto()
    dm_sum = enum.auto()
    dq = enum.auto()
    dx = enum.auto()
    dx_chip = enum.auto()
    dx_chip_in = enum.auto()
    dx_core = enum.auto()
    dx_core_in = enum.auto()
    dx_keep = enum.auto()
    dx_own = enum.auto()
    dx_rest = enum.auto()
    dx_send = enum.auto()
    dx_sum = enum.auto()
    dy = enum.auto()
    dy3 = enum.auto()
    dyc = enum.auto()
    ffn_small = enum.auto()
    final_sum = enum.auto()
    g_attn = enum.auto()
    g_cross = enum.auto()
    g_in = enum.auto()
    g_out = enum.auto()
    hidden = enum.auto()
    hop = enum.auto()
    i = enum.auto()
    input_grad = enum.auto()
    k = enum.auto()
    layer_out = enum.auto()
    low_hidden = enum.auto()
    low_middle = enum.auto()
    lse = enum.auto()
    m = enum.auto()
    memory = enum.auto()
    middle = enum.auto()
    mixed = enum.auto()
    out = enum.auto()
    q = enum.auto()
    row = enum.auto()
    row_in = enum.auto()
    self_bias = enum.auto()
    self_small = enum.auto()
    slope = enum.auto()
    small = enum.auto()
    small_chip = enum.auto()
    small_chip_in = enum.auto()
    small_chip_sum = enum.auto()
    small_core = enum.auto()
    small_core_in = enum.auto()
    small_core_sum = enum.auto()
    small_half = enum.auto()
    small_row = enum.auto()
    small_row_in = enum.auto()
    small_sum = enum.auto()
    squares = enum.auto()
    summed = enum.auto()
    v = enum.auto()
    bias = enum.auto()
    gain = enum.auto()
    cross_shift = enum.auto()
    cross_scale = enum.auto()
    w_in = enum.auto()
    w_mix = enum.auto()
    w_out = enum.auto()
    w_qkv = enum.auto()
    x = enum.auto()
    x_all = enum.auto()


class Wires:
    def __init__(self, send_sem, recv_sem, names, buffers):
        self.send_sem, self.recv_sem, self.names = send_sem, recv_sem, names
        self.like = {(ref.shape, ref.dtype): ref for ref in buffers}
        self.section, self.dp, self.seq = (lax.axis_index(n) for n in ("section", "dp", "seq"))
        self.dp_size, self.seq_size = lax.axis_size("dp"), lax.axis_size("seq")
        self.chips = self.seq_size // 2
        self.core = self.seq % 2
        self.twin = {"seq": self.seq + 1 - 2 * self.core}
        self.across = {"section": 1 - self.section}
        self.open, self.role = [], None

    def chip(self, k):
        return {"seq": (self.seq + 2 * k) % self.seq_size}

    def row(self, k):
        return {"dp": (self.dp + k) % self.dp_size}

    def peers(self, across=True):
        found = [self.twin]
        found += [self.chip(k) for k in range(1, self.chips)]
        found += [self.row(k) for k in range(1, self.dp_size)] if across else []
        return found + ([self.across] if across else [])

    def barrier(self, across=True):
        semaphore = pltpu.get_barrier_semaphore()
        peers = self.peers(across)
        for peer in peers:
            pl.semaphore_signal(semaphore, inc=1, device_id=peer, device_id_type=pl.DeviceIdType.MESH)
        pl.semaphore_wait(semaphore, len(peers))

    def copy(self, name, source, target, device):
        at = self.names.index(name)
        return pltpu.make_async_remote_copy(
            src_ref=source,
            dst_ref=target,
            send_sem=self.send_sem.at[at],
            recv_sem=self.recv_sem.at[at],
            device_id=device,
            device_id_type=pl.DeviceIdType.MESH,
        )

    def start(self, name, moves, whole=None):
        for source, target, device in moves:
            self.copy(name, source, target, device).start()
        if whole is None:
            whole = moves[0][0]
        self.open.append((name, self.like.get((whole.shape, whole.dtype), whole), self.role))

    def arrived(self, name, target):
        self.copy(name, target, target, self.twin).wait_recv()

    def close(self):
        def wait(role):
            for name, whole, of in self.open:
                if of == role:
                    self.copy(name, whole, whole, self.twin).wait_send()

        wait(None)
        for role in (0, 1):
            if any(of == role for _, _, of in self.open):
                pl.when(self.section == role)(functools.partial(wait, role))

    def only(self, role):
        def run(body):
            def inner():
                self.role = role
                body()
                self.role = None

            pl.when(self.section == role)(inner)

        return run


def whole_block(target, i):
    return target.at[i]


def gather_start(wires, name, source, target, block=whole_block):
    wires.start((name, N.core), [(source, block(target, 1), wires.twin)])
    for k in range(1, wires.chips):
        wires.start((name, N.chip, k), [(source, block(target, 2 * (wires.chips - k)), wires.chip(k))])


def gather_pass(wires, name, target, block=whole_block):
    for k in range(1, wires.chips):
        at = 2 * (wires.chips - k)
        wires.arrived((name, N.chip, k), block(target, at))
        wires.start((name, N.hop, k), [(block(target, at), block(target, at + 1), wires.twin)])


def gather_end(wires, name, target, block=whole_block):
    wires.arrived((name, N.core), block(target, 1))
    for k in range(1, wires.chips):
        wires.arrived((name, N.hop, k), block(target, 2 * (wires.chips - k) + 1))


def gather_names(name, chips):
    return [(name, N.core)] + [(name, part, k) for part in (N.chip, N.hop) for k in range(1, chips)]


class Sums:
    def __init__(self, wires, refs, key, unit, first, rows, dp_first):
        self.wires, self.key, self.dp_first = wires, key, dp_first
        self.full, self.out = refs[unit], refs[unit, N.out]
        self.first, self.rows, self.block_rows = first, rows, self.out.shape[0]
        self.core_in, self.core_sum = refs[key, N.core_in], refs[key, N.core_sum]
        self.chip_in, self.row_in, self.mid = refs[key, N.chip_in], refs[key, N.row_in], refs[key, N.mid]
        self.count, self.columns = self.core_in.shape[0], self.core_in.shape[2]

    def block(self, pair, core):
        at = (2 * pair + core) * self.block_rows + self.first
        return self.full.at[pl.ds(pl.multiple_of(at, 16), self.rows)]

    def core_start(self):
        w = self.wires
        moves = [(self.block(i, 1 - w.core), self.core_in.at[i], w.twin) for i in range(self.count)]
        w.start((self.key, N.core), moves, self.core_in)

    def core_add(self):
        w = self.wires
        w.arrived((self.key, N.core), self.core_in)
        own = Rows([self.block(i, w.core) for i in range(self.count)], (self.count * self.rows, self.columns))
        arrived = Rows([self.core_in.at[i] for i in range(self.count)], own.shape)
        sums = Rows([self.core_sum.at[i] for i in range(self.count)], own.shape)
        return (add_kernel, [own, arrived], [sums], (), self.core_sent)

    def core_sent(self):
        w = self.wires
        if self.dp_first:
            moves = []
            for k in range(1, w.dp_size):
                source = self.core_sum.at[pl.ds((w.dp + k) % w.dp_size * w.chips, w.chips)]
                moves.append((source, self.row_in.at[k - 1], w.row(k)))
            w.start((self.key, N.row), moves, self.row_in)
            return
        for k in range(1, w.chips):
            there = (w.seq // 2 + k) % w.chips
            target = self.chip_in.at[k - 1]
            moves = [
                (self.core_sum.at[d * w.chips + there], target.at[d], w.chip(k)) for d in range(w.dp_size)
            ]
            w.start((self.key, N.chip, k), moves, target)

    def second_add(self):
        w = self.wires
        mine = w.seq // 2
        if self.dp_first:
            w.arrived((self.key, N.row), self.row_in)
            terms = [self.core_sum.at[pl.ds(w.dp * w.chips, w.chips)]]
            terms += [self.row_in.at[k] for k in range(w.dp_size - 1)]
            step(add_kernel, terms, [self.mid])
            for k in range(1, w.chips):
                source = self.mid.at[(mine + k) % w.chips]
                w.start((self.key, N.chip, k), [(source, self.chip_in.at[k - 1], w.chip(k))])
            return
        shape = (w.dp_size * self.rows, self.columns)
        terms = [Rows([self.core_sum.at[d * w.chips + mine] for d in range(w.dp_size)], shape)]
        for k in range(1, w.chips):
            w.arrived((self.key, N.chip, k), self.chip_in.at[k - 1])
            terms.append(Rows([self.chip_in.at[k - 1, d] for d in range(w.dp_size)], shape))
        step(add_kernel, terms, [Rows([self.mid.at[d] for d in range(w.dp_size)], shape)])
        moves = [
            (self.mid.at[(w.dp + k) % w.dp_size], self.row_in.at[k - 1], w.row(k)) for k in range(1, w.dp_size)
        ]
        w.start((self.key, N.row), moves, self.row_in)

    def third_add(self):
        w = self.wires
        out = self.out.at[pl.ds(self.first, self.rows)]
        if self.dp_first:
            for k in range(1, w.chips):
                w.arrived((self.key, N.chip, k), self.chip_in.at[k - 1])
            step(add_lead_kernel, [self.mid.at[w.seq // 2], self.chip_in], [out])
            return
        w.arrived((self.key, N.row), self.row_in)
        step(add_lead_kernel, [self.mid.at[w.dp], self.row_in], [out])


def sum_pieces(units, devices):
    pieces = []
    for unit, (rows, _) in units.items():
        rows //= devices
        parts = 2 if unit is N.g_out else 3 if unit is N.g_attn else 1
        if rows // parts % 16:
            parts = 1
        for i in range(parts):
            dp_first = i == 0 and unit is N.g_out
            pieces.append(((unit, i), unit, i * (rows // parts), rows // parts, dp_first))
    return pieces


def sum_shapes(key, rows, columns, dp_first, dp_size, chips):
    far_chips, far_rows = max(chips - 1, 1), max(dp_size - 1, 1)
    block = (rows, columns)
    return {
        (key, N.core_in): shaped(dp_size * chips, *block, kind=BF16),
        (key, N.core_sum): shaped(dp_size * chips, *block, kind=BF16),
        (key, N.mid): shaped(chips if dp_first else dp_size, *block, kind=BF16),
        (key, N.chip_in): shaped(far_chips, *(block if dp_first else (dp_size, *block)), kind=BF16),
        (key, N.part): shaped(*block, kind=BF16),
        (key, N.row_in): shaped(far_rows, *((chips, *block) if dp_first else block), kind=BF16),
    }


def sum_names(key, chips):
    return [(key, N.core), (key, N.row)] + [(key, N.chip, k) for k in range(1, chips)]


def final_body(count, n_in, *refs):
    n_out = 15
    ins, outs, refs = refs[:n_in], refs[n_in : n_in + n_out], refs[n_in + n_out :]
    held, refs = refs[:n_in], refs[n_in:]
    stats, bias_grad, gain_grad, hidden_grad, cross_grad, cross_gain_grad, in_sem, out_sem = refs
    layer_out, input_grad, attn, ffn_in, ffn_out, small, cross_small = held[:7]
    cross = held[7:]
    section = lax.axis_index("section")
    me = lax.axis_index("dp") * lax.axis_size("seq") + lax.axis_index("seq")
    devices = lax.axis_size("dp") * lax.axis_size("seq")
    width = small.shape[1]
    half = outs[6].shape[0]
    loads = [pltpu.make_async_copy(a, v, in_sem.at[i]) for i, (a, v) in enumerate(zip(ins, held))]
    for copy in [*loads[5:7], *loads[:5], *loads[7:]]:
        copy.start()
    moves = []

    def move(source, at):
        moves.append(pltpu.make_async_copy(source, outs[at], out_sem.at[at]))
        return moves[-1]

    loads[5].wait()
    loads[6].wait()

    def columns_of(rows, start, number):
        at = lax.broadcasted_iota(jnp.int32, (width, number), 0)
        column = lax.broadcasted_iota(jnp.int32, (width, number), 1)
        return jnp.dot(
            rows, (at == column + start).astype(F32), precision=lax.Precision.HIGHEST, preferred_element_type=F32
        )

    per, per_hidden = bias_grad.shape[1], hidden_grad.shape[1]
    mine = columns_of(small[...], me * per, per)
    for i, row in enumerate((3, 4, 2, 10, 1, 9)):
        bias_grad[i : i + 1, :] = mine[row : row + 1]
    for i, row in enumerate((0, 8)):
        gain_grad[i : i + 1, :] = mine[row : row + 1]
    place = me * per_hidden
    hidden_rows = columns_of(small[8:16, :], place % width, per_hidden)
    row = lax.broadcasted_iota(jnp.int32, hidden_rows.shape, 0)
    hidden_grad[...] = jnp.sum(jnp.where(row == 3 + place // width, hidden_rows, 0.0), 0, keepdims=True)
    rows = jnp.where(section == 0, cross_small[...], small[16:24, :])
    cross_rows = columns_of(rows, (section * devices + me) * half, half)
    for i, row in enumerate((3, 4, 2, 1)):
        cross_grad[i : i + 1, :] = cross_rows[row : row + 1]
    cross_gain_grad[...] = cross_rows[0:1]
    squares = jnp.sum(small[5:7, :], 1, keepdims=True)
    stats[...] = jnp.sqrt(jnp.concatenate([squares[0:1], squares[1:2]], 1) / count)
    for i, ref in enumerate((stats, bias_grad, gain_grad, hidden_grad, cross_grad, cross_gain_grad)):
        move(ref, 9 + i).start()
    for load, targets in zip(
        loads[:5],
        (
            [(layer_out, 0)],
            [(input_grad, 1)],
            [(attn.at[:, 0 : 3 * width], 2), (attn.at[:, 3 * width : 4 * width], 3)],
            [(ffn_in, 4)],
            [(ffn_out, 5)],
        ),
    ):
        load.wait()
        for source, at in targets:
            move(source, at).start()
    for load in loads[7:]:
        load.wait()
    if len(cross) == 2:
        cross[0][...] = jnp.where(section == 0, cross[0][...], cross[1][half : 2 * half, :])
    for i, (first, end) in enumerate([(0, width), (width, 3 * width), (3 * width, 4 * width)]):
        move(cross[0].at[:, first:end], 6 + i).start()
    for copy in moves:
        copy.wait()


def main_body(micro, pieces, in_names, out_names, wire_names, held_names, *refs):
    refs = list(refs)
    hbm = {n: refs.pop(0) for n in in_names + out_names}
    held_refs = {n: refs.pop(0) for n in held_names}
    vec_ref, cross_vec_ref, send_sem, recv_sem, held_sem = refs
    wires = Wires(send_sem, recv_sem, wire_names, hbm.values())
    chips, dp_size = wires.chips, wires.dp_size
    length, width = hbm[N.x].shape[1:]
    hidden_units = hbm[N.w_in].shape[1]
    held_copies = {
        n: pltpu.make_async_copy(hbm[n], held_refs[n], held_sem.at[i]) for i, n in enumerate(held_names)
    }
    for copy in held_copies.values():
        copy.start()
    held = {n: Held(r) for n, r in held_refs.items()}
    vec, cross_vec = Held(vec_ref), Held(cross_vec_ref)
    ticks, last = range(micro), micro - 1
    back_scratch = (pltpu.VMEM((length, width), BF16),)

    def b(name, m):
        return hbm[(name, m)]

    def inputs(m):
        blocks = b(N.x_all, m)
        return Rows([hbm[N.x].at[m]] + [blocks.at[i] for i in range(1, wires.seq_size)])

    def memory(m):
        arrived = b(N.memory, m)
        return Rows([arrived.at[i] for i in range(wires.seq_size)])

    def self_forward(m):
        return (
            self_kernel,
            [inputs(m), held[N.w_qkv], held[N.w_mix], vec, b(N.self_bias, m)],
            [b(n, m) for n in (N.q, N.k, N.v, N.mixed, N.lse, N.summed, N.hidden, N.squares)],
            (),
        )

    def ffn_forward(m, middle):
        return (
            ffn_kernel,
            [b(middle, m), vec, held[N.w_in], held[N.b_in], held[N.w_out]],
            [b(n, m) for n in (N.act, N.slope, N.final_sum, N.low_middle)] + [hbm[N.layer_out].at[m]],
            (),
        )

    def ffn_back(m, grad):
        return (
            ffn_back_kernel,
            [grad, b(N.final_sum, m), vec, held[N.w_out], b(N.slope, m), held[N.w_in]],
            [b(n, m) for n in (N.dy3, N.d_inner, N.d_middle, N.ffn_small)],
            (),
        )

    def cross_forward(m):
        return (
            cross_kernel,
            [b(N.hidden, m), held[N.cross_q], cross_vec, memory(m), held[N.cross_kv], b(N.cross_bias, m), held[N.cross_out]],
            [b(n, m) for n in (N.cq, N.ck, N.cv, N.cross_mixed, N.cross_lse, N.cross_sum, N.middle, N.low_hidden)],
            (),
        )

    def cross_back(m):
        return (
            cross_back_kernel,
            [b(N.d_middle, m), b(N.cross_sum, m), cross_vec, held[N.cross_out], b(N.cross_mixed, m), b(N.cq, m), b(N.ck, m),
             b(N.cross_bias, m), b(N.cross_lse, m), b(N.cv, m), held[N.cross_q], held[N.cross_kv]],
            [b(n, m) for n in (N.dyc, N.dcq, N.dckv, N.d_middle, N.dm_keep, N.dm_send, N.cross_small)],
            back_scratch,
            lambda: wires.start((N.dm_core, m), [(b(N.dm_send, m), b(N.dm_core_in, m), wires.twin)]),
        )

    def self_back(m):
        return (
            self_back_kernel,
            [b(N.d_middle, m), b(N.summed, m), vec, held[N.w_mix], b(N.mixed, m), b(N.q, m), b(N.k, m), b(N.self_bias, m),
             b(N.lse, m), b(N.v, m), held[N.w_qkv]],
            [b(n, m) for n in (N.dy, N.dq, N.dkv, N.dx_own, N.dx_keep, N.dx_send, N.self_small)],
            back_scratch,
            lambda: wires.start((N.dx_core, m), [(b(N.dx_send, m), b(N.dx_core_in, m), wires.twin)]),
        )

    def dx_core(m):
        wires.arrived((N.dx_core, m), b(N.dx_core_in, m))
        arrived, rest = b(N.dx_core_in, m), (chips - 1) * length
        step(add_kernel, [b(N.dx_own, m), arrived.at[0:length]], [b(N.dx_sum, m)])
        step(add_kernel, [b(N.dx_keep, m), arrived.at[pl.ds(length, rest)]], [b(N.dx_rest, m)])
        for k in range(1, chips):
            source = b(N.dx_rest, m).at[pl.ds((k - 1) * length, length)]
            wires.start((N.dx_chip, k, m), [(source, b(N.dx_chip_in, m).at[k - 1], wires.chip(k))])

    def dx_end(m):
        for k in range(1, chips):
            wires.arrived((N.dx_chip, k, m), b(N.dx_chip_in, m).at[k - 1])
        step(add_lead_kernel, [b(N.dx_sum, m), b(N.dx_chip_in, m)], [hbm[N.input_grad].at[m]])

    part_rows = length // 2

    def part(h):
        return pl.ds(h * part_rows, part_rows)

    def dm_core(m):
        wires.arrived((N.dm_core, m), b(N.dm_core_in, m))
        step(add_kernel, [b(N.dm_keep, m), b(N.dm_core_in, m)], [b(N.dm_sum, m)])
        for h in range(2):
            for k in range(1, chips):
                source = b(N.dm_sum, m).at[pl.ds(k * length + h * part_rows, part_rows)]
                wires.start((N.dm_chip, k, m, h), [(source, b(N.dm_chip_in, m).at[k - 1, part(h)], wires.chip(k))])

    def dm_chip(m):
        for h in range(2):
            terms = [b(N.dm_sum, m).at[part(h)]]
            for k in range(1, chips):
                terms.append(b(N.dm_chip_in, m).at[k - 1, part(h)])
                wires.arrived((N.dm_chip, k, m, h), terms[-1])
            step(add_kernel, terms, [b(N.dm, m).at[part(h)]])
            wires.start((N.dm, m, h), [(b(N.dm, m).at[part(h)], b(N.d_memory, m).at[part(h)], wires.across)])

    def dm_end(m):
        for h in range(2):
            wires.arrived((N.dm, m, h), b(N.d_memory, m).at[part(h)])

    def memory_send(m):
        for h in range(2):
            source, target = hbm[N.layer_out].at[m, part(h)], b(N.memory, m).at[0, part(h)]
            wires.start((N.m, m, h), [(source, target, wires.across)])

    def memory_block(h):
        return lambda target, i: target.at[i, part(h)]

    def memory_start(m):
        arrived = b(N.memory, m)
        for h in range(2):
            wires.arrived((N.m, m, h), arrived.at[0, part(h)])
            gather_start(wires, ((N.m, m), h), arrived.at[0, part(h)], arrived, memory_block(h))

    def memory_pass(m):
        for h in range(2):
            gather_pass(wires, ((N.m, m), h), b(N.memory, m), memory_block(h))

    def memory_end(m):
        for h in range(2):
            gather_end(wires, ((N.m, m), h), b(N.memory, m), memory_block(h))

    def weights(products, out, regroup=0):
        operands, plan = [], []
        for lefts, rights, column in products:
            n, count = len(operands), len(lefts)
            operands += list(lefts) + list(rights)
            plan.append((tuple(range(n, n + count)), tuple(range(n + count, n + 2 * count)), column))
        scratch = (pltpu.VMEM(out.shape, F32),) if regroup else ()
        return (functools.partial(weight_kernel, plan, regroup), operands, [out], scratch)

    def all_b(name):
        return [b(name, m) for m in ticks]

    def cross_weights():
        regroup = width // 2 // (dp_size * wires.seq_size) if pieces else 0
        return weights(
            [
                (all_b(N.low_hidden), all_b(N.dcq), 0),
                ([memory(m) for m in ticks], all_b(N.dckv), width),
                (all_b(N.cross_mixed), all_b(N.dyc), 3 * width),
            ],
            hbm[N.g_cross],
            regroup,
        )

    def out_weights():
        return weights([(all_b(N.act), all_b(N.dy3), 0)], hbm[N.g_out])

    def in_weights():
        return weights([(all_b(N.low_middle), all_b(N.d_inner), 0)], hbm[N.g_in])

    def attn_weights():
        return weights(
            [
                ([hbm[N.x].at[m] for m in ticks], all_b(N.dq), 0),
                ([inputs(m) for m in ticks], all_b(N.dkv), width),
                (all_b(N.mixed), all_b(N.dy), 3 * width),
            ],
            hbm[N.g_attn],
        )

    units = {}
    for piece in pieces:
        units.setdefault(piece[1], []).append(Sums(wires, hbm, *piece))

    def stage(unit, which):
        for sums in units.get(unit, ()):
            which(sums)

    def second_adds(unit, dp_first):
        for sums in units.get(unit, ()):
            if sums.dp_first == dp_first:
                sums.second_add()

    def core_adds(unit):
        if unit in units:
            group(*[sums.core_add() for sums in units[unit]])

    wires.barrier()
    gather_start(wires, N.i, hbm[N.ids], hbm[N.ids_all])
    gather_start(wires, (N.x, 0), hbm[N.x].at[0], b(N.x_all, 0))
    gather_pass(wires, N.i, hbm[N.ids_all])
    gather_end(wires, N.i, hbm[N.ids_all])
    step(
        functools.partial(mask_kernel, micro),
        [hbm[N.ids], hbm[N.ids_all]],
        all_b(N.self_bias) + all_b(N.cross_bias),
    )
    gather_pass(wires, (N.x, 0), b(N.x_all, 0))
    for m in range(1, micro):
        gather_start(wires, (N.x, m), hbm[N.x].at[m], b(N.x_all, m))
    for n in (N.bias, N.gain, N.w_qkv, N.w_mix):
        held_copies[n].wait()
    vec_ref[0:6, :] = held_refs[N.bias][...]
    vec_ref[6:8, :] = held_refs[N.gain][...]
    gather_end(wires, (N.x, 0), b(N.x_all, 0))
    group(self_forward(0))
    for n in held_names:
        if n not in (N.bias, N.gain, N.w_qkv, N.w_mix):
            held_copies[n].wait()
    cross_vec_ref[0:4, :] = held_refs[N.cross_shift][...]
    cross_vec_ref[4:5, :] = held_refs[N.cross_scale][...]
    for m in range(1, micro):
        gather_pass(wires, (N.x, m), b(N.x_all, m))

    @wires.only(0)
    def _():
        for m in ticks:
            group(ffn_forward(m, N.hidden))
            memory_send(m)
            if m < last:
                gather_end(wires, (N.x, m + 1), b(N.x_all, m + 1))
                group(self_forward(m + 1))
        for m in range(last):
            dm_end(m)
            group(ffn_back(m, b(N.d_memory, m)), self_back(m))
            dx_core(m)
        dm_end(last)
        group(
            (
                ffn_norm_kernel,
                [b(N.d_memory, last), b(N.final_sum, last), vec],
                [b(N.dy3, last), hbm[N.d_final], hbm[N.norm_small]],
                (),
            ),
            out_weights(),
        )
        stage(N.g_out, Sums.core_start)
        group(
            (
                ffn_rest_kernel,
                [b(N.dy3, last), hbm[N.d_final], hbm[N.norm_small], held[N.w_out], b(N.slope, last), held[N.w_in]],
                [b(N.d_inner, last), b(N.d_middle, last), b(N.ffn_small, last)],
                (),
            )
        )
        core_adds(N.g_out)

    @wires.only(1)
    def _():
        for m in range(1, micro):
            gather_end(wires, (N.x, m), b(N.x_all, m))
            group(self_forward(m))
        memory_start(0)
        memory_pass(0)
        for m in ticks:
            memory_end(m)

            def between_forward(m=m):
                if m < last:
                    memory_start(m + 1)
                if m > 0:
                    dm_core(m - 1)

            def between_back(m=m):
                if m < last:
                    memory_pass(m + 1)
                if m > 0:
                    dm_chip(m - 1)

            group(cross_forward(m), between_forward, ffn_forward(m, N.middle))
            group(ffn_back(m, hbm[N.cotangent].at[m]), between_back, cross_back(m))
        dm_core(last)
        group(out_weights())
        stage(N.g_out, Sums.core_start)
        dm_chip(last)
        core_adds(N.g_out)
        group(cross_weights())
        stage(N.g_cross, Sums.core_start)
        second_adds(N.g_out, False)
        core_adds(N.g_cross)

    group(in_weights())
    stage(N.g_in, Sums.core_start)

    @wires.only(1)
    def _():
        for m in range(last):
            group(self_back(m))

    core_adds(N.g_in)

    @wires.only(1)
    def _():
        stage(N.g_cross, Sums.second_add)
        second_adds(N.g_out, True)
        for m in range(last):
            dx_core(m)

    group(self_back(last))
    step(
        functools.partial(small_kernel, micro),
        all_b(N.self_small) + all_b(N.ffn_small) + all_b(N.squares) + all_b(N.cross_small),
        [hbm[N.small]],
    )
    wires.start(N.small_core, [(hbm[N.small], hbm[N.small_core_in], wires.twin)])

    @wires.only(0)
    def _():
        second_adds(N.g_out, False)
        second_adds(N.g_out, True)

    group(attn_weights())
    stage(N.g_attn, Sums.core_start)
    wires.arrived(N.small_core, hbm[N.small_core_in])
    step(add_kernel, [hbm[N.small], hbm[N.small_core_in]], [hbm[N.small_core_sum]])
    for k in range(1, chips):
        wires.start((N.small_chip, k), [(hbm[N.small_core_sum], hbm[N.small_chip_in].at[k - 1], wires.chip(k))])
    stage(N.g_in, Sums.second_add)
    core_adds(N.g_attn)
    dx_core(last)

    @wires.only(1)
    def _():
        stage(N.g_cross, Sums.third_add)
        if pieces:
            half = width // 2 // (dp_size * wires.seq_size)
            wires.start(N.cross_half, [(hbm[N.g_cross, N.out].at[0:half], hbm[N.cross_half], wires.across)])

    for k in range(1, chips):
        wires.arrived((N.small_chip, k), hbm[N.small_chip_in].at[k - 1])
    step(add_lead_kernel, [hbm[N.small_core_sum], hbm[N.small_chip_in]], [hbm[N.small_chip_sum]])
    moves = [(hbm[N.small_chip_sum], hbm[N.small_row_in].at[k - 1], wires.row(k)) for k in range(1, dp_size)]
    wires.start(N.small_row, moves, hbm[N.small_row_in])
    stage(N.g_out, Sums.third_add)
    for m in range(last):
        dx_end(m)
    stage(N.g_attn, Sums.second_add)
    wires.arrived(N.small_row, hbm[N.small_row_in])
    step(add_lead_kernel, [hbm[N.small_chip_sum], hbm[N.small_row_in]], [hbm[N.small_sum]])

    @wires.only(1)
    def _():
        wires.start(N.small_half, [(hbm[N.small_sum].at[16:24], hbm[N.small_half], wires.across)])

    dx_end(last)
    stage(N.g_in, Sums.third_add)
    stage(N.g_attn, Sums.third_add)

    @wires.only(0)
    def _():
        wires.arrived(N.small_half, hbm[N.small_half])
        if pieces:
            wires.arrived(N.cross_half, hbm[N.cross_half])

    wires.close()


def shaped(*shape, kind=F32):
    return jax.ShapeDtypeStruct(shape, kind)


def pick(stacked, position):
    return lax.dynamic_index_in_dim(stacked, position, 0, keepdims=False)


def section_permute(x, axis, pairs, only):
    if only is None:
        return lax.ppermute(x, axis, pairs)
    first = only * lax.axis_size(axis)
    return lax.ppermute(x, ("section", axis), [(first + i, first + j) for i, j in pairs])


def group_permute(x, axis, members, stride, step, only=None):
    pairs = []
    for i in range(lax.axis_size(axis)):
        at = (i // stride) % members
        pairs.append((i, i + ((at + step) % members - at) * stride))
    return section_permute(x, axis, pairs, only)


def place_in(axis, members, stride):
    return (lax.axis_index(axis) // stride) % members


class Scatter:
    def __init__(self, parts, only=None):
        self.dp, self.chips = lax.axis_size("dp"), lax.axis_size("seq") // 2
        self.only, self.kind = only, parts.dtype
        self.parts = jnp.moveaxis(parts, 2, 0)
        self.stages = [("seq", 2, 1), ("seq", self.chips, 2), ("dp", self.dp, 1)]

    def send(self):
        axis, members, stride = self.stages[0]
        mine = place_in(axis, members, stride)
        self.keep = pick(self.parts, mine)
        return [pick(self.parts, (mine + step) % members) for step in range(1, members)]

    def arrive(self, sent):
        axis, members, stride = self.stages.pop(0)
        total = self.keep.astype(F32)
        for step in range(1, members):
            total = total + group_permute(sent[step - 1], axis, members, stride, step, self.only).astype(F32)
        if not self.stages:
            return total
        total = total.astype(self.kind)
        self.parts = jnp.moveaxis(total, 1, 0) if len(self.stages) == 2 else total
        return None

    def finish(self, sent=None):
        while self.stages:
            total = self.arrive(self.send() if sent is None else sent)
            sent = None
        return total


def by_device(total):
    dp_size, seq_size = lax.axis_size("dp"), lax.axis_size("seq")
    return total.reshape(dp_size, seq_size // 2, 2, total.shape[0] // (dp_size * seq_size), *total.shape[1:])


def to_encoder_half(total, section):
    half = total.shape[0] // 2
    arrived = lax.ppermute(total[:half], "section", [(1, 0)])
    return jnp.where(section == 0, arrived, total[half:])


def kernel_call(body, outs, operands, scratch, collective_id, flops, name):
    anywhere = pl.BlockSpec(memory_space=pltpu.HBM)
    size = sum(math.prod(o.shape) * o.dtype.itemsize for o in list(outs) + list(operands))
    return pl.pallas_call(
        body,
        out_shape=list(outs),
        in_specs=[anywhere] * len(operands),
        out_specs=[anywhere] * len(outs),
        scratch_shapes=scratch,
        cost_estimate=pl.CostEstimate(flops=int(flops), bytes_accessed=int(size), transcendentals=0),
        compiler_params=pltpu.CompilerParams(
            vmem_limit_bytes=VMEM_LIMIT, collective_id=collective_id, has_side_effects=True
        ),
        name=name,
    )(*operands)


def per_device(
    x_in, segments, cotangent, attn_in, attn_out, attn_bias, gains, ffn_in, ffn_bias, ffn_out,
    cross_q, cross_kv, cross_out, cross_bias, cross_gain,
):
    section = lax.axis_index("section")
    micro, length, width = x_in.shape[1], x_in.shape[3], x_in.shape[4]
    dp_size, seq_size = lax.axis_size("dp"), lax.axis_size("seq")
    chips = seq_size // 2
    devices = dp_size * seq_size
    tokens = length * seq_size
    hidden_units = ffn_in.shape[2]
    fused = width // devices % 16 == 0
    ticks = range(micro)
    x = x_in[0, :, 0]

    ids = segments.reshape(2 * micro, length)
    arrays = {
        N.x: x,
        N.ids: ids,
        N.cotangent: cotangent[:, 0],
        N.w_qkv: attn_in[0],
        N.w_mix: attn_out[0],
        N.w_in: ffn_in[0],
        N.w_out: ffn_out[0],
        N.b_in: ffn_bias,
        N.bias: attn_bias[0],
        N.gain: gains[0],
        N.cross_q: cross_q,
        N.cross_kv: cross_kv,
        N.cross_out: cross_out,
        N.cross_shift: cross_bias,
        N.cross_scale: cross_gain[None],
    }
    lw, lw_low = shaped(length, width), shaped(length, width, kind=BF16)
    tw_low = shaped(tokens, width, kind=BF16)
    lh_low = shaped(length, hidden_units, kind=BF16)
    pair_low = shaped(tokens, 2 * width, kind=BF16)
    half_low = shaped(tokens // 2, width, kind=BF16)
    rest_low = shaped(max(tokens // 2 - length, length), width, kind=BF16)
    far_low = shaped(max(chips - 1, 1), length, width, kind=BF16)
    seq_low = shaped(seq_size, length, width, kind=BF16)
    mask = shaped(length, tokens)
    lse_shape, few = shaped(HEADS // 2, length, PAIR), shaped(8, width)
    kinds = {
        N.q: lw_low, N.k: tw_low, N.v: tw_low, N.mixed: lw_low, N.lse: lse_shape, N.summed: lw, N.hidden: lw, N.squares: few,
        N.act: lh_low, N.slope: lh_low, N.final_sum: lw, N.low_middle: lw_low,
        N.dy3: lw_low, N.d_inner: lh_low, N.d_middle: lw, N.ffn_small: few,
        N.cq: lw_low, N.ck: tw_low, N.cv: tw_low, N.cross_mixed: lw_low, N.cross_lse: lse_shape, N.cross_sum: lw,
        N.middle: lw, N.low_hidden: lw_low,
        N.dyc: lw_low, N.dcq: lw_low, N.dckv: pair_low, N.dm_keep: half_low, N.dm_send: half_low,
        N.cross_small: few, N.dm_core_in: half_low, N.dm_sum: half_low, N.dm_chip_in: far_low, N.dm: lw_low, N.d_memory: lw_low,
        N.dy: lw_low, N.dq: lw_low, N.dkv: pair_low, N.dx_own: lw, N.dx_keep: rest_low, N.dx_send: half_low, N.self_small: few,
        N.dx_core_in: half_low, N.dx_sum: lw, N.dx_rest: rest_low, N.dx_chip_in: far_low,
        N.x_all: seq_low, N.memory: seq_low, N.self_bias: mask, N.cross_bias: mask,
    }
    outs = {(n, m): kind for m in ticks for n, kind in kinds.items()}
    for n in (N.layer_out, N.input_grad):
        outs[n] = shaped(micro, length, width, kind=BF16)
    outs[N.ids_all] = shaped(seq_size, *ids.shape, kind=ids.dtype)
    outs[N.d_final], outs[N.norm_small] = lw, few
    outs[N.part] = shaped(length // 2, width, kind=BF16)
    small_shape = shaped(24, width)
    for n in (N.small, N.small_core_in, N.small_core_sum, N.small_chip_sum, N.small_sum):
        outs[n] = small_shape
    outs[N.small_chip_in] = shaped(max(chips - 1, 1), 24, width)
    outs[N.small_row_in] = shaped(max(dp_size - 1, 1), 24, width)
    outs[N.small_half] = few
    totals = {
        N.g_cross: (width, 4 * width), N.g_out: (hidden_units, width), N.g_in: (width, hidden_units), N.g_attn: (width, 4 * width),
    }
    wire_names = [N.small_core, N.small_row, N.small_half] + [(N.small_chip, k) for k in range(1, chips)]
    for m in ticks:
        wire_names += gather_names((N.x, m), chips) + [(N.dm_core, m), (N.dx_core, m)]
        wire_names += [(N.dx_chip, k, m) for k in range(1, chips)]
        for h in range(2):
            wire_names += gather_names(((N.m, m), h), chips) + [(N.m, m, h), (N.dm, m, h)]
            wire_names += [(N.dm_chip, k, m, h) for k in range(1, chips)]
    pieces = sum_pieces(totals, devices) if fused else []
    for n, total in totals.items():
        outs[n] = shaped(*total, kind=BF16)
        if fused:
            outs[n, N.out] = shaped(total[0] // devices, total[1])
    for key, n, _, rows, dp_first in pieces:
        outs.update(sum_shapes(key, rows, totals[n][1], dp_first, dp_size, chips))
        wire_names += sum_names(key, chips)
    if fused:
        outs[N.cross_half] = shaped(width // 2 // devices, 4 * width)
        wire_names.append(N.cross_half)
    wire_names += gather_names(N.i, chips)
    held_names = [N.bias, N.gain, N.w_qkv, N.w_mix, N.w_in, N.b_in, N.w_out, N.cross_shift, N.cross_scale, N.cross_q, N.cross_kv, N.cross_out]
    scratch = [pltpu.VMEM(arrays[n].shape, arrays[n].dtype) for n in held_names]
    scratch += [pltpu.VMEM((8, width), F32)] * 2
    scratch += [pltpu.SemaphoreType.DMA((len(wire_names),))] * 2 + [pltpu.SemaphoreType.DMA((len(held_names),))]
    results = kernel_call(
        functools.partial(main_body, micro, pieces, list(arrays), list(outs), wire_names, held_names),
        list(outs.values()),
        list(arrays.values()),
        scratch,
        0,
        6 * micro * length * width * (12 * width + 2 * hidden_units),
        "layers",
    )
    results = dict(zip(outs, results))

    if fused:
        cross_part = None
        attn_part, ffn_in_part, ffn_out_part = (results[n, N.out] for n in (N.g_attn, N.g_in, N.g_out))
        cross_parts = [results[N.cross_half], results[N.g_cross, N.out]]
    else:
        halves = results[N.g_cross].reshape(2, width // 2, 4 * width)
        halves = jnp.stack([by_device(halves[0]), by_device(halves[1])], 3)
        cross_part = Scatter(halves, 1).finish()
        cross_part = jnp.where(
            section == 0, lax.ppermute(cross_part[0], "section", [(1, 0)]), cross_part[1]
        )
        attn_part, ffn_in_part, ffn_out_part = (
            Scatter(by_device(results[n])).finish() for n in (N.g_attn, N.g_in, N.g_out)
        )
        cross_parts = [cross_part]
    per, half, per_hidden = width // devices, width // 2 // devices, hidden_units // devices
    operands = [
        results[N.layer_out], results[N.input_grad], attn_part, ffn_in_part, ffn_out_part,
        results[N.small_sum], results[N.small_half], *cross_parts,
    ]
    final_shapes = [
        shaped(micro, length, width, kind=BF16),
        shaped(micro, length, width, kind=BF16),
        shaped(per, 3 * width),
        shaped(per, width),
        shaped(per, hidden_units),
        shaped(per_hidden, width),
        shaped(half, width),
        shaped(half, 2 * width),
        shaped(half, width),
        shaped(1, 2),
        shaped(6, per),
        shaped(2, per),
        shaped(1, per_hidden),
        shaped(4, half),
        shaped(1, half),
    ]
    anywhere = pl.BlockSpec(memory_space=pltpu.HBM)
    finals = pl.pallas_call(
        functools.partial(final_body, micro * dp_size * tokens * width, len(operands)),
        out_shape=final_shapes,
        in_specs=[anywhere] * len(operands),
        out_specs=[anywhere] * len(final_shapes),
        scratch_shapes=[pltpu.VMEM(o.shape, o.dtype) for o in operands + final_shapes[9:]]
        + [pltpu.SemaphoreType.DMA((len(operands),)), pltpu.SemaphoreType.DMA((len(final_shapes),))],
    )(*operands)
    (layer_out, input_grad, attn_in_grad, attn_out_grad, ffn_in_grad, ffn_out_grad, cross_q_grad, cross_kv_grad,
     cross_out_grad, stats, attn_bias_grad, gains_grad, ffn_bias_grad, cross_bias_grad, cross_gain_grad) = finals
    return (
        layer_out[None, :, None],
        input_grad[None, :, None],
        stats,
        attn_in_grad[None],
        attn_out_grad[None],
        attn_bias_grad[None],
        gains_grad[None],
        ffn_in_grad[None],
        ffn_bias_grad,
        ffn_out_grad[None],
        cross_q_grad,
        cross_kv_grad,
        cross_out_grad,
        cross_bias_grad,
        cross_gain_grad[0],
    )


def solution(mesh):
    return jax.shard_map(
        per_device,
        mesh=mesh,
        in_specs=(
            P("section", None, "dp", "seq", None),
            P(None, None, "dp", "seq"),
            P(None, "dp", "seq", None),
            P("section", None, None),
            P("section", None, None),
            P("section", None, None),
            P("section", None, None),
            P("section", None, None),
            P("section", None),
            P("section", None, None),
            P(),
            P(),
            P(),
            P(),
            P(),
        ),
        out_specs=(
            P("section", None, "dp", "seq", None),
            P("section", None, "dp", "seq", None),
            P("section", None),
            P("section", ("dp", "seq"), None),
            P("section", ("dp", "seq"), None),
            P("section", None, ("dp", "seq")),
            P("section", None, ("dp", "seq")),
            P("section", ("dp", "seq"), None),
            P("section", ("dp", "seq")),
            P("section", ("dp", "seq"), None),
            P(("section", "dp", "seq"), None),
            P(("section", "dp", "seq"), None),
            P(("section", "dp", "seq"), None),
            P(None, ("section", "dp", "seq")),
            P(("section", "dp", "seq")),
        ),
        check_vma=False,
    )
```

```python
import enum
import functools
import math

import jax
import jax.numpy as jnp
from jax import lax
from jax.experimental import pallas as pl
from jax.experimental.pallas import tpu as pltpu
from jax.sharding import PartitionSpec as P

HEADS = 12
HEAD_DIM = 64
PAIR = 2 * HEAD_DIM
EPSILON = 1e-05
MASKED = -1000000000.0
SCALE = 1.0 / math.sqrt(HEAD_DIM)
VMEM_LIMIT = 58 * 1024 * 1024

F32 = jnp.float32
BF16 = jnp.bfloat16


def mm(a, b):
    return jnp.dot(a, b, preferred_element_type=F32)


def mm_nt(a, b):
    return lax.dot_general(a, b, (((1,), (1,)), ((), ())), preferred_element_type=F32)


def norm_parts(tensor):
    average = jnp.mean(tensor, -1, keepdims=True)
    centered = tensor - average
    spread = jnp.mean(centered * centered, -1, keepdims=True)
    scale = lax.rsqrt(spread + EPSILON)
    return centered * scale, scale


def norm_back(tensor, gain, grad):
    normed, scale = norm_parts(tensor)
    scaled = gain * grad
    product = grad * normed
    first = jnp.mean(scaled, -1, keepdims=True)
    second = jnp.mean(scaled * normed, -1, keepdims=True)
    out = (scaled - first - normed * second) * scale
    return out, jnp.sum(product, 0, keepdims=True), jnp.sum(grad, 0, keepdims=True)


def column_sum(tensor):
    return jnp.sum(tensor.astype(F32), 0, keepdims=True)


def gelu_pair(x):
    bell = jnp.exp(-0.5 * x * x)
    t = 1.0 / (1.0 + (0.3275911 / math.sqrt(2.0)) * jnp.abs(x))
    poly = t * (
        0.5 * 0.254829592
        + t
        * (
            0.5 * -0.284496736
            + t * (0.5 * 1.421413741 + t * (0.5 * -1.453152027 + t * (0.5 * 1.061405429)))
        )
    )
    tail = poly * bell
    cdf = jnp.where(x < 0, tail, 1.0 - tail)
    return x * cdf, cdf + x * bell * (1.0 / math.sqrt(2.0 * math.pi))


def row_blocks(count, body):
    step = min(256, count)

    def run(i, carry):
        body(pl.ds(pl.multiple_of(i * step, step), step))
        return carry

    lax.fori_loop(0, count // step, run, 0, unroll=True)


def head_halves(rows):
    lane = lax.broadcasted_iota(jnp.int32, (rows, PAIR), 1)
    return lane < HEAD_DIM, lane >= HEAD_DIM


def attend_forward(q_ref, k_ref, v_ref, bias_ref, mixed_ref, lse_ref):
    query_halves, key_halves = head_halves(q_ref.shape[0]), head_halves(k_ref.shape[0])

    def pair(p, carry):
        lanes = pl.ds(pl.multiple_of(p * PAIR, PAIR), PAIR)
        keys, values = k_ref[:, lanes], v_ref[:, lanes]
        queries = q_ref[:, lanes] * SCALE
        outs, peaks = [], []
        for a in range(2):
            own = jnp.where(query_halves[a], queries, jnp.zeros_like(queries))
            scores = mm_nt(own, keys) + bias_ref[...]
            peak = jnp.max(scores, 1, keepdims=True)
            weights = jnp.exp(scores - peak).astype(BF16)
            outs.append(mm(weights, jnp.where(key_halves[a], values, jnp.ones_like(values))))
            peaks.append(peak)
        first = query_halves[0]
        total = pltpu.roll(jnp.where(first, outs[1], outs[0]), HEAD_DIM, 1)
        lse_ref[p] = jnp.where(first, peaks[0], peaks[1]) + jnp.log(total)
        mixed_ref[:, lanes] = (jnp.where(first, outs[0], outs[1]) * (1.0 / total)).astype(BF16)
        return carry

    lax.fori_loop(0, HEADS // 2, pair, 0, unroll=2)


def attend_back(q_ref, k_ref, v_ref, grad_ref, mixed_ref, lse_ref, bias_ref, dq_ref, dkv_ref):
    length, width = q_ref.shape
    halves = head_halves(length)

    def pair(p, carry):
        lanes = pl.ds(pl.multiple_of(p * PAIR, PAIR), PAIR)
        value_lanes = pl.ds(pl.multiple_of(width + p * PAIR, PAIR), PAIR)
        keys, values = k_ref[:, lanes], v_ref[:, lanes]
        queries = q_ref[:, lanes] * SCALE
        grads = grad_ref[:, lanes]
        product = grads.astype(F32) * mixed_ref[:, lanes].astype(F32)
        queries_t, grads_t = queries.T, grads.T
        outs, key_grads, value_grads = [], [], []
        for a, half in enumerate(halves):
            own = jnp.where(half, queries, jnp.zeros_like(queries))
            own_grad = jnp.where(half, grads, jnp.zeros_like(grads))
            rows = slice(a * HEAD_DIM, (a + 1) * HEAD_DIM)
            lse = lse_ref[p, :, a * HEAD_DIM : a * HEAD_DIM + 1]
            delta = jnp.sum(jnp.where(half, product, 0.0), 1, keepdims=True)
            weights = jnp.exp(mm_nt(own, keys) + bias_ref[...] - lse)
            score_grad = (weights * (mm_nt(own_grad, values) - delta)).astype(BF16)
            outs.append(mm(score_grad, keys))
            key_grads.append(mm(queries_t[rows], score_grad))
            value_grads.append(mm(grads_t[rows], weights.astype(BF16)))
        dkv_ref[:, lanes] = jnp.concatenate(key_grads, 0).astype(BF16).T
        dkv_ref[:, value_lanes] = jnp.concatenate(value_grads, 0).astype(BF16).T
        dq_ref[:, lanes] = (jnp.where(halves[0], outs[0], outs[1]) * SCALE).astype(BF16)
        return carry

    lax.fori_loop(0, HEADS // 2, pair, 0, unroll=2)


def self_kernel(io, x_ref, w_qkv, w_mix, vec, bias, q_out, k_out, v_out, mixed, lse, summed, hidden, squares):
    length, width = q_out.shape
    io.ready(x_ref, w_qkv, vec)
    x_own = x_ref[0:length, :]
    q_out[...] = (mm(x_own, w_qkv[:, 0:width]) + vec[0:1, :]).astype(BF16)

    def keys(rows):
        x = x_ref[rows, :]
        k_out[rows, :] = mm(x, w_qkv[:, width : 2 * width]).astype(BF16)
        v_out[rows, :] = (mm(x, w_qkv[:, 2 * width : 3 * width]) + vec[1:2, :]).astype(BF16)

    row_blocks(x_ref.shape[0], keys)
    io.done(q_out, k_out, v_out)
    io.ready(bias)
    attend_forward(q_out, k_out, v_out, bias, mixed, lse)
    io.done(mixed, lse)
    io.ready(w_mix)
    branch = mm(mixed[...], w_mix[...]) + vec[2:3, :]
    total = x_own.astype(F32) + branch
    summed[...] = total
    squares[...] = jnp.zeros_like(squares)
    squares[0:1, :] = column_sum(total * total)
    squares[1:2, :] = column_sum(branch * branch)
    hidden[...] = norm_parts(total)[0] * vec[6:7, :] + vec[4:5, :]


def ffn_kernel(io, middle, vec, w_in, b_in, w_out, act, slope, final_sum, low_middle, result):
    width = middle.shape[1]
    chunks = w_in.shape[1] // width
    io.ready(middle, vec)
    mid = middle[...]
    low = mid.astype(BF16)
    low_middle[...] = low
    final_sum[...] = mid + vec[3:4, :]
    io.ready(w_in, b_in, w_out)

    def chunk(j, carry):
        columns = pl.ds(pl.multiple_of(j * width, width), width)
        inner = mm(low, w_in[:, columns]) + b_in[:, columns]
        value, derivative = gelu_pair(inner)
        value = value.astype(BF16)
        act[:, columns] = value
        slope[:, columns] = derivative.astype(BF16)
        final_sum[...] += mm(value, w_out[columns, :])
        return carry

    lax.fori_loop(0, chunks, chunk, 0, unroll=True)
    io.done(act, slope, low_middle, final_sum)
    result[...] = (norm_parts(final_sum[...])[0] * vec[7:8, :] + vec[5:6, :]).astype(BF16)


def ffn_norm_kernel(io, grad, final_sum, vec, dy, d_final, small):
    io.ready(grad, final_sum, vec)
    back, d_gain, d_shift = norm_back(final_sum[...], vec[7:8, :], grad[...].astype(F32))
    low = back.astype(BF16)
    dy[...] = low
    d_final[...] = back
    small[...] = jnp.zeros_like(small)
    small[0:1, :] = d_gain
    small[1:2, :] = d_shift
    small[2:3, :] = column_sum(low)


def ffn_rest_kernel(io, dy, d_final, small_in, w_out, slope, w_in, d_inner, d_middle, small):
    width = dy.shape[1]
    chunks = w_in.shape[1] // width
    io.ready(dy, d_final, small_in, w_out, slope, w_in)
    low = dy[...]
    small[...] = small_in[...]
    d_middle[...] = d_final[...]

    def chunk(j, carry):
        columns = pl.ds(pl.multiple_of(j * width, width), width)
        d_act = mm_nt(low, w_out[columns, :])
        inner = (d_act * slope[:, columns].astype(F32)).astype(BF16)
        d_inner[:, columns] = inner
        small[pl.ds(3 + j, 1), :] = column_sum(inner)
        d_middle[...] += mm_nt(inner, w_in[:, columns])
        return carry

    lax.fori_loop(0, chunks, chunk, 0, unroll=True)


def ffn_back_kernel(io, grad, final_sum, vec, w_out, slope, w_in, dy, d_inner, d_middle, small):
    ffn_norm_kernel(io, grad, final_sum, vec, dy, d_middle, small)
    io.done(dy)
    ffn_rest_kernel(io, dy, d_middle, small, w_out, slope, w_in, d_inner, d_middle, small)


def mask_kernel(micro, io, ids, far, *outs):
    io.ready(ids, far)
    length = ids.shape[1]
    section, me, blocks = lax.axis_index("section"), lax.axis_index("seq"), lax.axis_size("seq")
    orders = []
    for k in range(blocks // 2):
        chip = (me + 2 * k) % blocks
        orders += [chip, chip + 1 - 2 * (me % 2)]
    here = lax.broadcasted_iota(jnp.int32, (length, length), 0)
    there = lax.broadcasted_iota(jnp.int32, (length, length), 1)
    for m in range(micro):
        own = jnp.where(section == 0, ids[m : m + 1, :], ids[micro + m : micro + m + 1, :])
        query = jnp.broadcast_to(own.astype(F32), (PAIR, length)).T[:, 0:1]
        for j, order in enumerate(orders):
            block = ids if j == 0 else far.at[j]
            source, target = block[m : m + 1, :], block[micro + m : micro + m + 1, :]
            key = jnp.where(section == 0, source, target).astype(F32)
            late = (there + order * length > here + orders[0] * length) & (section == 1)
            columns = slice(j * length, (j + 1) * length)
            outs[m][:, columns] = jnp.where((query == key) & jnp.logical_not(late), 0.0, MASKED)
            outs[micro + m][:, columns] = jnp.where(query == source.astype(F32), 0.0, MASKED)


def cross_kernel(
    io, hidden, w_q, vec, memory, w_kv, bias, w_o,
    cq, ck, cv, mixed, lse, summed, middle, low_hidden,
):
    width = hidden.shape[1]
    io.ready(hidden, w_q, vec)
    low = hidden[...].astype(BF16)
    low_hidden[...] = low
    cq[...] = (mm(low, w_q[...]) + vec[0:1, :]).astype(BF16)
    io.ready(memory, w_kv)

    def keys(rows):
        mem = memory[rows, :]
        ck[rows, :] = mm(mem, w_kv[:, 0:width]).astype(BF16)
        cv[rows, :] = (mm(mem, w_kv[:, width : 2 * width]) + vec[1:2, :]).astype(BF16)

    row_blocks(memory.shape[0], keys)
    io.done(cq, ck, cv, low_hidden)
    io.ready(bias)
    attend_forward(cq, ck, cv, bias, mixed, lse)
    io.done(mixed, lse)
    io.ready(w_o)
    total = hidden[...] + mm(mixed[...], w_o[...]) + vec[2:3, :]
    summed[...] = total
    middle[...] = norm_parts(total)[0] * vec[4:5, :] + vec[3:4, :]


def cross_back_kernel(
    io, d_middle, summed, vec, w_o, mixed, cq, ck, bias, lse, cv, w_q, w_kv,
    dyc, dcq, dckv, d_hidden, keep, send, small, d_mixed,
):
    length, width = d_middle.shape
    io.ready(d_middle, summed, vec)
    d_cross, d_gain, d_shift = norm_back(summed[...], vec[4:5, :], d_middle[...])
    low = d_cross.astype(BF16)
    dyc[...] = low
    d_hidden[...] = d_cross
    io.ready(w_o, mixed)
    grads = mm_nt(low, w_o[...]).astype(BF16)
    d_mixed[...] = grads
    io.ready(cq, ck, bias, lse, cv)
    attend_back(cq, ck, cv, d_mixed, mixed, lse, bias, dcq, dckv)
    io.ready(w_q, w_kv)
    for block in range(dckv.shape[0] // length):
        target = keep if block % 2 == 0 else send
        rows = slice(block // 2 * length, (block // 2 + 1) * length)
        target[rows, :] = mm_nt(dckv[block * length : (block + 1) * length, :], w_kv[...]).astype(BF16)
    io.done(send, keep, dyc, dcq, dckv)
    d_hidden[...] += mm_nt(dcq[...], w_q[...])
    io.sent(send)
    small[...] = jnp.zeros_like(small)
    small[0:1, :] = d_gain
    small[1:2, :] = d_shift
    small[2:3, :] = column_sum(low)
    small[3:4, :] = column_sum(dcq[...])
    small[4:5, :] = column_sum(dckv[:, width : 2 * width])


def self_back_kernel(
    io, grad, summed, vec, w_mix, mixed, q, k, bias, lse, v, w_qkv,
    dy, dq, dkv, own, keep, send, small, d_mixed,
):
    length, width = q.shape
    io.ready(grad, summed, vec)
    d_sum, d_gain, d_shift = norm_back(summed[...], vec[6:7, :], grad[...])
    low = d_sum.astype(BF16)
    dy[...] = low
    own[...] = d_sum
    io.ready(w_mix, mixed)
    grads = mm_nt(low, w_mix[...]).astype(BF16)
    d_mixed[...] = grads
    io.ready(q, k, bias, lse, v)
    attend_back(q, k, v, d_mixed, mixed, lse, bias, dq, dkv)
    io.done(dy, dq, dkv)
    io.ready(w_qkv)
    for block in range(dkv.shape[0] // length):
        part = mm_nt(dkv[block * length : (block + 1) * length, :], w_qkv[:, width : 3 * width])
        if block == 0:
            own[...] += part + mm_nt(dq[...], w_qkv[:, 0:width])
            continue
        target = keep if block % 2 == 0 else send
        at = (block - 2) // 2 if block % 2 == 0 else block // 2
        target[at * length : (at + 1) * length, :] = part.astype(BF16)
    io.done(send, keep, own)
    io.sent(send)
    small[...] = jnp.zeros_like(small)
    small[0:1, :] = d_gain
    small[1:2, :] = d_shift
    small[2:3, :] = column_sum(low)
    small[3:4, :] = column_sum(dq[...])
    small[4:5, :] = column_sum(dkv[:, width : 2 * width])


def weight_kernel(plan, regroup, io, *refs):
    out = refs[-1] if regroup == 0 else refs[-2]
    wide_out = out if regroup == 0 else refs[-1]
    for lefts, rights, column in plan:
        inner = refs[lefts[0]].shape[1]
        cols = refs[rights[0]].shape[1]
        step = 256
        wide = min(cols, 1536)
        io.ready(*[refs[i] for i in lefts + rights])

        def tile(i, carry, lefts=lefts, rights=rights, column=column, cols=cols, wide=wide):
            rows = pl.ds(pl.multiple_of(i * step, step), step)
            turned = [refs[l][:, rows].T for l in lefts]
            for start in range(0, cols, wide):
                total = None
                for left, r in zip(turned, rights):
                    term = mm(left, refs[r][:, start : start + wide])
                    total = term if total is None else total + term
                wide_out[rows, column + start : column + start + wide] = total.astype(wide_out.dtype)
            return carry

        lax.fori_loop(0, inner // step, tile, 0, unroll=3)
    if regroup:
        half = out.shape[0] // 2

        def group(i, carry):
            first = wide_out[pl.ds(pl.multiple_of(i * regroup, regroup), regroup), :]
            second = wide_out[pl.ds(pl.multiple_of(half + i * regroup, regroup), regroup), :]
            rows = pl.ds(pl.multiple_of(2 * i * regroup, 2 * regroup), 2 * regroup)
            out[rows, :] = jnp.concatenate([first, second], 0).astype(BF16)
            return carry

        lax.fori_loop(0, half // regroup, group, 0)


def add_kernel(io, *refs):
    out = refs[-1]
    io.ready(*refs[:-1])
    total = refs[0][...].astype(F32)
    for ref in refs[1:-1]:
        total = total + ref[...].astype(F32)
    out[...] = total.astype(out.dtype)
    io.sent(out)


def add_lead_kernel(io, one, many, out):
    io.ready(one, many)
    total = one[...].astype(F32)
    for i in range(many.shape[0]):
        total = total + many[i].astype(F32)
    out[...] = total.astype(out.dtype)


def small_kernel(micro, io, *refs):
    out = refs[-1]
    ins = refs[:-1]
    io.ready(*ins)
    selfs, ffns, squares, crosses = (ins[i * micro : (i + 1) * micro] for i in range(4))
    out[...] = jnp.zeros_like(out)
    for ref in selfs:
        out[0:8, :] += ref[...]
    for ref in squares:
        out[5:7, :] += ref[0:2, :]
    for ref in ffns:
        out[8:16, :] += ref[...]
    for ref in crosses:
        out[16:24, :] += jnp.where(lax.axis_index("section") == 1, ref[...], 0.0)
    io.sent(out)


class Moves:
    def __init__(self, loads, stores):
        self.loads, self.stores, self.hook = dict(loads), dict(stores), None
        self.started, self.loaded, self.stored = set(), set(), set()
        for copies in self.loads.values():
            for copy in copies:
                copy.start()

    def ready(self, *refs):
        for ref in refs:
            if id(ref) not in self.loaded:
                self.loaded.add(id(ref))
                for copy in self.loads.get(id(ref), ()):
                    copy.wait()

    def away(self, ref):
        self.done(ref)
        if id(ref) not in self.stored:
            self.stored.add(id(ref))
            for copy in self.stores.get(id(ref), ()):
                copy.wait()

    def done(self, *refs):
        for ref in refs:
            if id(ref) not in self.started:
                self.started.add(id(ref))
                for copy in self.stores.get(id(ref), ()):
                    copy.start()

    def sent(self, ref):
        self.done(ref)
        if self.hook is not None:
            self.away(ref)
            self.hook()

    def finish(self, ins, outs):
        self.ready(*ins)
        self.done(*outs)
        for ref in outs:
            self.away(ref)


class Held:
    def __init__(self, ref):
        self.ref = ref


class Rows:
    def __init__(self, pieces, shape=None):
        self.pieces = list(pieces)
        rest = self.pieces[0].shape[1:] if shape is None else shape[1:]
        count = sum(p.shape[0] for p in self.pieces) if shape is None else shape[0]
        self.shape, self.dtype = (count, *rest), self.pieces[0].dtype


def as_rows(item):
    return item if isinstance(item, Rows) else Rows([item])


def step(kernel, operands, outs, scratch=()):
    group((kernel, operands, outs, scratch))


def group(*parts):
    made, loads, load_at, outs, owner, scratches, plans = {}, [], {}, [], {}, [], []
    for part in parts:
        if callable(part):
            plans.append(part)
            continue
        kernel, operands, results, scratch, hook = (*part, None)[:5]
        ins = []
        for o in operands:
            if isinstance(o, Held):
                ins.append((0, o.ref))
            elif id(o) in made:
                ins.append((2, made[id(o)]))
            else:
                if id(o) not in load_at:
                    load_at[id(o)] = len(loads)
                    loads.append(as_rows(o))
                ins.append((1, load_at[id(o)]))
        first = len(outs)
        for o in results:
            made[id(o)] = owner[id(o)] = len(outs)
            outs.append(o)
        plans.append((kernel, ins, range(first, len(outs)), range(len(scratches), len(scratches) + len(scratch)), hook))
        scratches += list(scratch)
    stored = [owner[id(o)] == i for i, o in enumerate(outs)]
    rows_out = [as_rows(o) for o in outs]
    n_load = sum(len(o.pieces) for o in loads)
    n_store = sum(len(o.pieces) for o in rows_out)

    def pairs(ref, rows):
        if len(rows.pieces) == 1:
            return [(rows.pieces[0], ref)]
        found, at = [], 0
        for piece in rows.pieces:
            found.append((piece, ref.at[pl.ds(at, piece.shape[0])]))
            at += piece.shape[0]
        return found

    def inner(*refs):
        n_in, n_out = len(loads), len(outs)
        vmem_in, vmem_out = refs[:n_in], refs[n_in : n_in + n_out]
        in_sem, out_sem = refs[n_in + n_out : n_in + n_out + 2]
        extra = refs[n_in + n_out + 2 :]
        coming, at = [], 0
        for ref, rows in zip(vmem_in, loads):
            copies = []
            for hbm, vmem in pairs(ref, rows):
                copies.append(pltpu.make_async_copy(hbm, vmem, in_sem.at[at]))
                at += 1
            coming.append((id(ref), copies))
        going, at = [], 0
        for ref, rows, store in zip(vmem_out, rows_out, stored):
            copies = []
            for hbm, vmem in pairs(ref, rows) if store else ():
                copies.append(pltpu.make_async_copy(vmem, hbm, out_sem.at[at]))
                at += 1
            going.append((id(ref), copies))
        moves = Moves(coming, going)
        for plan in plans:
            if callable(plan):
                plan()
                continue
            kernel, ins, results, scratch, moves.hook = plan
            given = [(None, vmem_in, vmem_out)[kind][at] if kind else at for kind, at in ins]
            kernel(moves, *given, *[vmem_out[i] for i in results], *[extra[i] for i in scratch])
            moves.done(*[vmem_out[i] for i in results])
        moves.finish(vmem_in, vmem_out)

    pl.run_scoped(
        inner,
        *[pltpu.VMEM(o.shape, o.dtype) for o in loads],
        *[pltpu.VMEM(o.shape, o.dtype) for o in rows_out],
        pltpu.SemaphoreType.DMA((max(n_load, 1),)),
        pltpu.SemaphoreType.DMA((max(n_store, 1),)),
        *scratches,
    )


class N(enum.Enum):
    act = enum.auto()
    b_in = enum.auto()
    chip = enum.auto()
    chip_in = enum.auto()
    mid = enum.auto()
    d_final = enum.auto()
    norm_small = enum.auto()
    part = enum.auto()
    ids = enum.auto()
    ids_all = enum.auto()
    ck = enum.auto()
    core = enum.auto()
    core_in = enum.auto()
    core_sum = enum.auto()
    cotangent = enum.auto()
    cq = enum.auto()
    cross_bias = enum.auto()
    cross_half = enum.auto()
    cross_kv = enum.auto()
    cross_lse = enum.auto()
    cross_mixed = enum.auto()
    cross_out = enum.auto()
    cross_q = enum.auto()
    cross_small = enum.auto()
    cross_sum = enum.auto()
    cv = enum.auto()
    d_inner = enum.auto()
    d_memory = enum.auto()
    d_middle = enum.auto()
    dckv = enum.auto()
    dcq = enum.auto()
    dkv = enum.auto()
    dm = enum.auto()
    dm_chip = enum.auto()
    dm_chip_in = enum.auto()
    dm_core = enum.auto()
    dm_core_in = enum.auto()
    dm_keep = enum.auto()
    dm_send = enum.auto()
    dm_sum = enum.auto()
    dq = enum.auto()
    dx = enum.auto()
    dx_chip = enum.auto()
    dx_chip_in = enum.auto()
    dx_core = enum.auto()
    dx_core_in = enum.auto()
    dx_keep = enum.auto()
    dx_own = enum.auto()
    dx_rest = enum.auto()
    dx_send = enum.auto()
    dx_sum = enum.auto()
    dy = enum.auto()
    dy3 = enum.auto()
    dyc = enum.auto()
    ffn_small = enum.auto()
    final_sum = enum.auto()
    g_attn = enum.auto()
    g_cross = enum.auto()
    g_in = enum.auto()
    g_out = enum.auto()
    hidden = enum.auto()
    hop = enum.auto()
    i = enum.auto()
    input_grad = enum.auto()
    k = enum.auto()
    layer_out = enum.auto()
    low_hidden = enum.auto()
    low_middle = enum.auto()
    lse = enum.auto()
    m = enum.auto()
    memory = enum.auto()
    middle = enum.auto()
    mixed = enum.auto()
    out = enum.auto()
    q = enum.auto()
    row = enum.auto()
    row_in = enum.auto()
    self_bias = enum.auto()
    self_small = enum.auto()
    slope = enum.auto()
    small = enum.auto()
    small_chip = enum.auto()
    small_chip_in = enum.auto()
    small_chip_sum = enum.auto()
    small_core = enum.auto()
    small_core_in = enum.auto()
    small_core_sum = enum.auto()
    small_half = enum.auto()
    small_row = enum.auto()
    small_row_in = enum.auto()
    small_sum = enum.auto()
    squares = enum.auto()
    summed = enum.auto()
    v = enum.auto()
    bias = enum.auto()
    gain = enum.auto()
    cross_shift = enum.auto()
    cross_scale = enum.auto()
    w_in = enum.auto()
    w_mix = enum.auto()
    w_out = enum.auto()
    w_qkv = enum.auto()
    x = enum.auto()
    x_all = enum.auto()


class Wires:
    def __init__(self, send_sem, recv_sem, names, buffers):
        self.send_sem, self.recv_sem, self.names = send_sem, recv_sem, names
        self.like = {(ref.shape, ref.dtype): ref for ref in buffers}
        self.section, self.dp, self.seq = (lax.axis_index(n) for n in ("section", "dp", "seq"))
        self.dp_size, self.seq_size = lax.axis_size("dp"), lax.axis_size("seq")
        self.chips = self.seq_size // 2
        self.core = self.seq % 2
        self.twin = {"seq": self.seq + 1 - 2 * self.core}
        self.across = {"section": 1 - self.section}
        self.open, self.role = [], None

    def chip(self, k):
        return {"seq": (self.seq + 2 * k) % self.seq_size}

    def row(self, k):
        return {"dp": (self.dp + k) % self.dp_size}

    def peers(self, across=True):
        found = [self.twin]
        found += [self.chip(k) for k in range(1, self.chips)]
        found += [self.row(k) for k in range(1, self.dp_size)] if across else []
        return found + ([self.across] if across else [])

    def barrier(self, across=True):
        semaphore = pltpu.get_barrier_semaphore()
        peers = self.peers(across)
        for peer in peers:
            pl.semaphore_signal(semaphore, inc=1, device_id=peer, device_id_type=pl.DeviceIdType.MESH)
        pl.semaphore_wait(semaphore, len(peers))

    def copy(self, name, source, target, device):
        at = self.names.index(name)
        return pltpu.make_async_remote_copy(
            src_ref=source,
            dst_ref=target,
            send_sem=self.send_sem.at[at],
            recv_sem=self.recv_sem.at[at],
            device_id=device,
            device_id_type=pl.DeviceIdType.MESH,
        )

    def start(self, name, moves, whole=None):
        for source, target, device in moves:
            self.copy(name, source, target, device).start()
        if whole is None:
            whole = moves[0][0]
        self.open.append((name, self.like.get((whole.shape, whole.dtype), whole), self.role))

    def arrived(self, name, target):
        self.copy(name, target, target, self.twin).wait_recv()

    def close(self):
        def wait(role):
            for name, whole, of in self.open:
                if of == role:
                    self.copy(name, whole, whole, self.twin).wait_send()

        wait(None)
        for role in (0, 1):
            if any(of == role for _, _, of in self.open):
                pl.when(self.section == role)(functools.partial(wait, role))

    def only(self, role):
        def run(body):
            def inner():
                self.role = role
                body()
                self.role = None

            pl.when(self.section == role)(inner)

        return run


def whole_block(target, i):
    return target.at[i]


def gather_start(wires, name, source, target, block=whole_block):
    wires.start((name, N.core), [(source, block(target, 1), wires.twin)])
    for k in range(1, wires.chips):
        wires.start((name, N.chip, k), [(source, block(target, 2 * (wires.chips - k)), wires.chip(k))])


def gather_pass(wires, name, target, block=whole_block):
    for k in range(1, wires.chips):
        at = 2 * (wires.chips - k)
        wires.arrived((name, N.chip, k), block(target, at))
        wires.start((name, N.hop, k), [(block(target, at), block(target, at + 1), wires.twin)])


def gather_end(wires, name, target, block=whole_block):
    wires.arrived((name, N.core), block(target, 1))
    for k in range(1, wires.chips):
        wires.arrived((name, N.hop, k), block(target, 2 * (wires.chips - k) + 1))


def gather_names(name, chips):
    return [(name, N.core)] + [(name, part, k) for part in (N.chip, N.hop) for k in range(1, chips)]


class Sums:
    def __init__(self, wires, refs, key, unit, first, rows, dp_first):
        self.wires, self.key, self.dp_first = wires, key, dp_first
        self.full, self.out = refs[unit], refs[unit, N.out]
        self.first, self.rows, self.block_rows = first, rows, self.out.shape[0]
        self.core_in, self.core_sum = refs[key, N.core_in], refs[key, N.core_sum]
        self.chip_in, self.row_in, self.mid = refs[key, N.chip_in], refs[key, N.row_in], refs[key, N.mid]
        self.count, self.columns = self.core_in.shape[0], self.core_in.shape[2]

    def block(self, pair, core):
        at = (2 * pair + core) * self.block_rows + self.first
        return self.full.at[pl.ds(pl.multiple_of(at, 16), self.rows)]

    def core_start(self):
        w = self.wires
        moves = [(self.block(i, 1 - w.core), self.core_in.at[i], w.twin) for i in range(self.count)]
        w.start((self.key, N.core), moves, self.core_in)

    def core_add(self):
        w = self.wires
        w.arrived((self.key, N.core), self.core_in)
        own = Rows([self.block(i, w.core) for i in range(self.count)], (self.count * self.rows, self.columns))
        arrived = Rows([self.core_in.at[i] for i in range(self.count)], own.shape)
        sums = Rows([self.core_sum.at[i] for i in range(self.count)], own.shape)
        return (add_kernel, [own, arrived], [sums], (), self.core_sent)

    def core_sent(self):
        w = self.wires
        if self.dp_first:
            moves = []
            for k in range(1, w.dp_size):
                source = self.core_sum.at[pl.ds((w.dp + k) % w.dp_size * w.chips, w.chips)]
                moves.append((source, self.row_in.at[k - 1], w.row(k)))
            w.start((self.key, N.row), moves, self.row_in)
            return
        for k in range(1, w.chips):
            there = (w.seq // 2 + k) % w.chips
            target = self.chip_in.at[k - 1]
            moves = [
                (self.core_sum.at[d * w.chips + there], target.at[d], w.chip(k)) for d in range(w.dp_size)
            ]
            w.start((self.key, N.chip, k), moves, target)

    def second_add(self):
        w = self.wires
        mine = w.seq // 2
        if self.dp_first:
            w.arrived((self.key, N.row), self.row_in)
            terms = [self.core_sum.at[pl.ds(w.dp * w.chips, w.chips)]]
            terms += [self.row_in.at[k] for k in range(w.dp_size - 1)]
            step(add_kernel, terms, [self.mid])
            for k in range(1, w.chips):
                source = self.mid.at[(mine + k) % w.chips]
                w.start((self.key, N.chip, k), [(source, self.chip_in.at[k - 1], w.chip(k))])
            return
        shape = (w.dp_size * self.rows, self.columns)
        terms = [Rows([self.core_sum.at[d * w.chips + mine] for d in range(w.dp_size)], shape)]
        for k in range(1, w.chips):
            w.arrived((self.key, N.chip, k), self.chip_in.at[k - 1])
            terms.append(Rows([self.chip_in.at[k - 1, d] for d in range(w.dp_size)], shape))
        step(add_kernel, terms, [Rows([self.mid.at[d] for d in range(w.dp_size)], shape)])
        moves = [
            (self.mid.at[(w.dp + k) % w.dp_size], self.row_in.at[k - 1], w.row(k)) for k in range(1, w.dp_size)
        ]
        w.start((self.key, N.row), moves, self.row_in)

    def third_add(self):
        w = self.wires
        out = self.out.at[pl.ds(self.first, self.rows)]
        if self.dp_first:
            for k in range(1, w.chips):
                w.arrived((self.key, N.chip, k), self.chip_in.at[k - 1])
            step(add_lead_kernel, [self.mid.at[w.seq // 2], self.chip_in], [out])
            return
        w.arrived((self.key, N.row), self.row_in)
        step(add_lead_kernel, [self.mid.at[w.dp], self.row_in], [out])


def sum_pieces(units, devices):
    pieces = []
    for unit, (rows, _) in units.items():
        rows //= devices
        parts = 2 if unit is N.g_out else 3 if unit is N.g_attn else 1
        if rows // parts % 16:
            parts = 1
        for i in range(parts):
            dp_first = i == 0 and unit is N.g_out
            pieces.append(((unit, i), unit, i * (rows // parts), rows // parts, dp_first))
    return pieces


def sum_shapes(key, rows, columns, dp_first, dp_size, chips):
    far_chips, far_rows = max(chips - 1, 1), max(dp_size - 1, 1)
    block = (rows, columns)
    return {
        (key, N.core_in): shaped(dp_size * chips, *block, kind=BF16),
        (key, N.core_sum): shaped(dp_size * chips, *block, kind=BF16),
        (key, N.mid): shaped(chips if dp_first else dp_size, *block, kind=BF16),
        (key, N.chip_in): shaped(far_chips, *(block if dp_first else (dp_size, *block)), kind=BF16),
        (key, N.part): shaped(*block, kind=BF16),
        (key, N.row_in): shaped(far_rows, *((chips, *block) if dp_first else block), kind=BF16),
    }


def sum_names(key, chips):
    return [(key, N.core), (key, N.row)] + [(key, N.chip, k) for k in range(1, chips)]


def final_body(count, n_in, *refs):
    n_out = 15
    ins, outs, refs = refs[:n_in], refs[n_in : n_in + n_out], refs[n_in + n_out :]
    held, refs = refs[:n_in], refs[n_in:]
    stats, bias_grad, gain_grad, hidden_grad, cross_grad, cross_gain_grad, in_sem, out_sem = refs
    layer_out, input_grad, attn, ffn_in, ffn_out, small, cross_small = held[:7]
    cross = held[7:]
    section = lax.axis_index("section")
    me = lax.axis_index("dp") * lax.axis_size("seq") + lax.axis_index("seq")
    devices = lax.axis_size("dp") * lax.axis_size("seq")
    width = small.shape[1]
    half = outs[6].shape[0]
    loads = [pltpu.make_async_copy(a, v, in_sem.at[i]) for i, (a, v) in enumerate(zip(ins, held))]
    for copy in [*loads[5:7], *loads[:5], *loads[7:]]:
        copy.start()
    moves = []

    def move(source, at):
        moves.append(pltpu.make_async_copy(source, outs[at], out_sem.at[at]))
        return moves[-1]

    loads[5].wait()
    loads[6].wait()

    def columns_of(rows, start, number):
        at = lax.broadcasted_iota(jnp.int32, (width, number), 0)
        column = lax.broadcasted_iota(jnp.int32, (width, number), 1)
        return jnp.dot(
            rows, (at == column + start).astype(F32), precision=lax.Precision.HIGHEST, preferred_element_type=F32
        )

    per, per_hidden = bias_grad.shape[1], hidden_grad.shape[1]
    mine = columns_of(small[...], me * per, per)
    for i, row in enumerate((3, 4, 2, 10, 1, 9)):
        bias_grad[i : i + 1, :] = mine[row : row + 1]
    for i, row in enumerate((0, 8)):
        gain_grad[i : i + 1, :] = mine[row : row + 1]
    place = me * per_hidden
    hidden_rows = columns_of(small[8:16, :], place % width, per_hidden)
    row = lax.broadcasted_iota(jnp.int32, hidden_rows.shape, 0)
    hidden_grad[...] = jnp.sum(jnp.where(row == 3 + place // width, hidden_rows, 0.0), 0, keepdims=True)
    rows = jnp.where(section == 0, cross_small[...], small[16:24, :])
    cross_rows = columns_of(rows, (section * devices + me) * half, half)
    for i, row in enumerate((3, 4, 2, 1)):
        cross_grad[i : i + 1, :] = cross_rows[row : row + 1]
    cross_gain_grad[...] = cross_rows[0:1]
    squares = jnp.sum(small[5:7, :], 1, keepdims=True)
    stats[...] = jnp.sqrt(jnp.concatenate([squares[0:1], squares[1:2]], 1) / count)
    for i, ref in enumerate((stats, bias_grad, gain_grad, hidden_grad, cross_grad, cross_gain_grad)):
        move(ref, 9 + i).start()
    for load, targets in zip(
        loads[:5],
        (
            [(layer_out, 0)],
            [(input_grad, 1)],
            [(attn.at[:, 0 : 3 * width], 2), (attn.at[:, 3 * width : 4 * width], 3)],
            [(ffn_in, 4)],
            [(ffn_out, 5)],
        ),
    ):
        load.wait()
        for source, at in targets:
            move(source, at).start()
    for load in loads[7:]:
        load.wait()
    if len(cross) == 2:
        cross[0][...] = jnp.where(section == 0, cross[0][...], cross[1][half : 2 * half, :])
    for i, (first, end) in enumerate([(0, width), (width, 3 * width), (3 * width, 4 * width)]):
        move(cross[0].at[:, first:end], 6 + i).start()
    for copy in moves:
        copy.wait()


def main_body(micro, pieces, in_names, out_names, wire_names, held_names, *refs):
    refs = list(refs)
    hbm = {n: refs.pop(0) for n in in_names + out_names}
    held_refs = {n: refs.pop(0) for n in held_names}
    vec_ref, cross_vec_ref, send_sem, recv_sem, held_sem = refs
    wires = Wires(send_sem, recv_sem, wire_names, hbm.values())
    chips, dp_size = wires.chips, wires.dp_size
    length, width = hbm[N.x].shape[1:]
    hidden_units = hbm[N.w_in].shape[1]
    held_copies = {
        n: pltpu.make_async_copy(hbm[n], held_refs[n], held_sem.at[i]) for i, n in enumerate(held_names)
    }
    for copy in held_copies.values():
        copy.start()
    held = {n: Held(r) for n, r in held_refs.items()}
    vec, cross_vec = Held(vec_ref), Held(cross_vec_ref)
    ticks, last = range(micro), micro - 1
    back_scratch = (pltpu.VMEM((length, width), BF16),)

    def b(name, m):
        return hbm[(name, m)]

    def inputs(m):
        blocks = b(N.x_all, m)
        return Rows([hbm[N.x].at[m]] + [blocks.at[i] for i in range(1, wires.seq_size)])

    def memory(m):
        arrived = b(N.memory, m)
        return Rows([arrived.at[i] for i in range(wires.seq_size)])

    def self_forward(m):
        return (
            self_kernel,
            [inputs(m), held[N.w_qkv], held[N.w_mix], vec, b(N.self_bias, m)],
            [b(n, m) for n in (N.q, N.k, N.v, N.mixed, N.lse, N.summed, N.hidden, N.squares)],
            (),
        )

    def ffn_forward(m, middle):
        return (
            ffn_kernel,
            [b(middle, m), vec, held[N.w_in], held[N.b_in], held[N.w_out]],
            [b(n, m) for n in (N.act, N.slope, N.final_sum, N.low_middle)] + [hbm[N.layer_out].at[m]],
            (),
        )

    def ffn_back(m, grad):
        return (
            ffn_back_kernel,
            [grad, b(N.final_sum, m), vec, held[N.w_out], b(N.slope, m), held[N.w_in]],
            [b(n, m) for n in (N.dy3, N.d_inner, N.d_middle, N.ffn_small)],
            (),
        )

    def cross_forward(m):
        return (
            cross_kernel,
            [b(N.hidden, m), held[N.cross_q], cross_vec, memory(m), held[N.cross_kv], b(N.cross_bias, m), held[N.cross_out]],
            [b(n, m) for n in (N.cq, N.ck, N.cv, N.cross_mixed, N.cross_lse, N.cross_sum, N.middle, N.low_hidden)],
            (),
        )

    def cross_back(m):
        return (
            cross_back_kernel,
            [b(N.d_middle, m), b(N.cross_sum, m), cross_vec, held[N.cross_out], b(N.cross_mixed, m), b(N.cq, m), b(N.ck, m),
             b(N.cross_bias, m), b(N.cross_lse, m), b(N.cv, m), held[N.cross_q], held[N.cross_kv]],
            [b(n, m) for n in (N.dyc, N.dcq, N.dckv, N.d_middle, N.dm_keep, N.dm_send, N.cross_small)],
            back_scratch,
            lambda: wires.start((N.dm_core, m), [(b(N.dm_send, m), b(N.dm_core_in, m), wires.twin)]),
        )

    def self_back(m):
        return (
            self_back_kernel,
            [b(N.d_middle, m), b(N.summed, m), vec, held[N.w_mix], b(N.mixed, m), b(N.q, m), b(N.k, m), b(N.self_bias, m),
             b(N.lse, m), b(N.v, m), held[N.w_qkv]],
            [b(n, m) for n in (N.dy, N.dq, N.dkv, N.dx_own, N.dx_keep, N.dx_send, N.self_small)],
            back_scratch,
            lambda: wires.start((N.dx_core, m), [(b(N.dx_send, m), b(N.dx_core_in, m), wires.twin)]),
        )

    def dx_core(m):
        wires.arrived((N.dx_core, m), b(N.dx_core_in, m))
        arrived, rest = b(N.dx_core_in, m), (chips - 1) * length
        group(
            (add_kernel, [b(N.dx_keep, m), arrived.at[pl.ds(length, rest)]], [b(N.dx_rest, m)], ()),
            (add_kernel, [b(N.dx_own, m), arrived.at[0:length]], [b(N.dx_sum, m)], ()),
        )
        for k in range(1, chips):
            source = b(N.dx_rest, m).at[pl.ds((k - 1) * length, length)]
            wires.start((N.dx_chip, k, m), [(source, b(N.dx_chip_in, m).at[k - 1], wires.chip(k))])

    def dx_end(m):
        for k in range(1, chips):
            wires.arrived((N.dx_chip, k, m), b(N.dx_chip_in, m).at[k - 1])
        step(add_lead_kernel, [b(N.dx_sum, m), b(N.dx_chip_in, m)], [hbm[N.input_grad].at[m]])

    part_rows = length // 2

    def part(h):
        return pl.ds(h * part_rows, part_rows)

    def dm_core(m):
        wires.arrived((N.dm_core, m), b(N.dm_core_in, m))
        step(add_kernel, [b(N.dm_keep, m), b(N.dm_core_in, m)], [b(N.dm_sum, m)])
        for h in range(2):
            for k in range(1, chips):
                source = b(N.dm_sum, m).at[pl.ds(k * length + h * part_rows, part_rows)]
                wires.start((N.dm_chip, k, m, h), [(source, b(N.dm_chip_in, m).at[k - 1, part(h)], wires.chip(k))])

    def dm_chip(m):
        for h in range(2):
            terms = [b(N.dm_sum, m).at[part(h)]]
            for k in range(1, chips):
                terms.append(b(N.dm_chip_in, m).at[k - 1, part(h)])
                wires.arrived((N.dm_chip, k, m, h), terms[-1])
            step(add_kernel, terms, [b(N.dm, m).at[part(h)]])
            wires.start((N.dm, m, h), [(b(N.dm, m).at[part(h)], b(N.d_memory, m).at[part(h)], wires.across)])

    def dm_end(m):
        for h in range(2):
            wires.arrived((N.dm, m, h), b(N.d_memory, m).at[part(h)])

    def memory_send(m):
        for h in range(2):
            source, target = hbm[N.layer_out].at[m, part(h)], b(N.memory, m).at[0, part(h)]
            wires.start((N.m, m, h), [(source, target, wires.across)])

    def memory_block(h):
        return lambda target, i: target.at[i, part(h)]

    def memory_start(m):
        arrived = b(N.memory, m)
        for h in range(2):
            wires.arrived((N.m, m, h), arrived.at[0, part(h)])
            gather_start(wires, ((N.m, m), h), arrived.at[0, part(h)], arrived, memory_block(h))

    def memory_pass(m):
        for h in range(2):
            gather_pass(wires, ((N.m, m), h), b(N.memory, m), memory_block(h))

    def memory_end(m):
        for h in range(2):
            gather_end(wires, ((N.m, m), h), b(N.memory, m), memory_block(h))

    def weights(products, out, regroup=0):
        operands, plan = [], []
        for lefts, rights, column in products:
            n, count = len(operands), len(lefts)
            operands += list(lefts) + list(rights)
            plan.append((tuple(range(n, n + count)), tuple(range(n + count, n + 2 * count)), column))
        scratch = (pltpu.VMEM(out.shape, F32),) if regroup else ()
        return (functools.partial(weight_kernel, plan, regroup), operands, [out], scratch)

    def all_b(name):
        return [b(name, m) for m in ticks]

    def cross_weights():
        regroup = width // 2 // (dp_size * wires.seq_size) if pieces else 0
        return weights(
            [
                (all_b(N.low_hidden), all_b(N.dcq), 0),
                ([memory(m) for m in ticks], all_b(N.dckv), width),
                (all_b(N.cross_mixed), all_b(N.dyc), 3 * width),
            ],
            hbm[N.g_cross],
            regroup,
        )

    def out_weights():
        return weights([(all_b(N.act), all_b(N.dy3), 0)], hbm[N.g_out])

    def in_weights():
        return weights([(all_b(N.low_middle), all_b(N.d_inner), 0)], hbm[N.g_in])

    def attn_weights():
        return weights(
            [
                ([hbm[N.x].at[m] for m in ticks], all_b(N.dq), 0),
                ([inputs(m) for m in ticks], all_b(N.dkv), width),
                (all_b(N.mixed), all_b(N.dy), 3 * width),
            ],
            hbm[N.g_attn],
        )

    units = {}
    for piece in pieces:
        units.setdefault(piece[1], []).append(Sums(wires, hbm, *piece))

    def stage(unit, which):
        for sums in units.get(unit, ()):
            which(sums)

    def second_adds(unit, dp_first):
        for sums in units.get(unit, ()):
            if sums.dp_first == dp_first:
                sums.second_add()

    def core_adds(unit):
        if unit in units:
            group(*[sums.core_add() for sums in units[unit]])

    wires.barrier()
    gather_start(wires, N.i, hbm[N.ids], hbm[N.ids_all])
    gather_start(wires, (N.x, 0), hbm[N.x].at[0], b(N.x_all, 0))
    gather_pass(wires, N.i, hbm[N.ids_all])
    gather_end(wires, N.i, hbm[N.ids_all])
    step(
        functools.partial(mask_kernel, micro),
        [hbm[N.ids], hbm[N.ids_all]],
        all_b(N.self_bias) + all_b(N.cross_bias),
    )
    gather_pass(wires, (N.x, 0), b(N.x_all, 0))
    for m in range(1, micro):
        gather_start(wires, (N.x, m), hbm[N.x].at[m], b(N.x_all, m))
    for n in (N.bias, N.gain, N.w_qkv, N.w_mix):
        held_copies[n].wait()
    vec_ref[0:6, :] = held_refs[N.bias][0]
    vec_ref[6:8, :] = held_refs[N.gain][0]
    gather_end(wires, (N.x, 0), b(N.x_all, 0))
    group(self_forward(0))
    for n in held_names:
        if n not in (N.bias, N.gain, N.w_qkv, N.w_mix):
            held_copies[n].wait()
    cross_vec_ref[0:4, :] = held_refs[N.cross_shift][...]
    cross_vec_ref[4:5, :] = held_refs[N.cross_scale][...]
    for m in range(1, micro):
        gather_pass(wires, (N.x, m), b(N.x_all, m))

    @wires.only(0)
    def _():
        for m in ticks:
            group(ffn_forward(m, N.hidden))
            memory_send(m)
            if m < last:
                gather_end(wires, (N.x, m + 1), b(N.x_all, m + 1))
                group(self_forward(m + 1))
        for m in range(last):
            dm_end(m)
            group(ffn_back(m, b(N.d_memory, m)), self_back(m))
            dx_core(m)
        dm_end(last)
        group(
            (
                ffn_norm_kernel,
                [b(N.d_memory, last), b(N.final_sum, last), vec],
                [b(N.dy3, last), hbm[N.d_final], hbm[N.norm_small]],
                (),
            ),
            out_weights(),
        )
        stage(N.g_out, Sums.core_start)
        group(
            (
                ffn_rest_kernel,
                [b(N.dy3, last), hbm[N.d_final], hbm[N.norm_small], held[N.w_out], b(N.slope, last), held[N.w_in]],
                [b(N.d_inner, last), b(N.d_middle, last), b(N.ffn_small, last)],
                (),
            )
        )
        core_adds(N.g_out)

    @wires.only(1)
    def _():
        for m in range(1, micro):
            gather_end(wires, (N.x, m), b(N.x_all, m))
            group(self_forward(m))
        memory_start(0)
        memory_pass(0)
        for m in ticks:
            memory_end(m)

            def between_forward(m=m):
                if m < last:
                    memory_start(m + 1)
                if m > 0:
                    dm_core(m - 1)

            def between_back(m=m):
                if m < last:
                    memory_pass(m + 1)
                if m > 0:
                    dm_chip(m - 1)

            group(cross_forward(m), between_forward, ffn_forward(m, N.middle))
            group(ffn_back(m, hbm[N.cotangent].at[m]), between_back, cross_back(m))
        dm_core(last)
        group(out_weights())
        stage(N.g_out, Sums.core_start)
        dm_chip(last)
        core_adds(N.g_out)
        group(cross_weights())
        stage(N.g_cross, Sums.core_start)
        second_adds(N.g_out, False)
        core_adds(N.g_cross)

    group(in_weights())
    stage(N.g_in, Sums.core_start)

    @wires.only(1)
    def _():
        for m in range(last):
            group(self_back(m))

    core_adds(N.g_in)

    @wires.only(1)
    def _():
        stage(N.g_cross, Sums.second_add)
        second_adds(N.g_out, True)
        for m in range(last):
            dx_core(m)

    group(
        self_back(last),
        (
            functools.partial(small_kernel, micro),
            all_b(N.self_small) + all_b(N.ffn_small) + all_b(N.squares) + all_b(N.cross_small),
            [hbm[N.small]],
            (),
            lambda: wires.start(N.small_core, [(hbm[N.small], hbm[N.small_core_in], wires.twin)]),
        ),
    )

    @wires.only(0)
    def _():
        second_adds(N.g_out, False)
        second_adds(N.g_out, True)

    group(attn_weights())
    stage(N.g_attn, Sums.core_start)
    wires.arrived(N.small_core, hbm[N.small_core_in])
    step(add_kernel, [hbm[N.small], hbm[N.small_core_in]], [hbm[N.small_core_sum]])
    for k in range(1, chips):
        wires.start((N.small_chip, k), [(hbm[N.small_core_sum], hbm[N.small_chip_in].at[k - 1], wires.chip(k))])
    stage(N.g_in, Sums.second_add)
    core_adds(N.g_attn)
    dx_core(last)

    @wires.only(1)
    def _():
        stage(N.g_cross, Sums.third_add)
        if pieces:
            half = width // 2 // (dp_size * wires.seq_size)
            wires.start(N.cross_half, [(hbm[N.g_cross, N.out].at[0:half], hbm[N.cross_half], wires.across)])

    for k in range(1, chips):
        wires.arrived((N.small_chip, k), hbm[N.small_chip_in].at[k - 1])
    step(add_lead_kernel, [hbm[N.small_core_sum], hbm[N.small_chip_in]], [hbm[N.small_chip_sum]])
    moves = [(hbm[N.small_chip_sum], hbm[N.small_row_in].at[k - 1], wires.row(k)) for k in range(1, dp_size)]
    wires.start(N.small_row, moves, hbm[N.small_row_in])
    stage(N.g_out, Sums.third_add)
    for m in range(last):
        dx_end(m)
    stage(N.g_attn, Sums.second_add)
    wires.arrived(N.small_row, hbm[N.small_row_in])
    step(add_lead_kernel, [hbm[N.small_chip_sum], hbm[N.small_row_in]], [hbm[N.small_sum]])

    @wires.only(1)
    def _():
        wires.start(N.small_half, [(hbm[N.small_sum].at[16:24], hbm[N.small_half], wires.across)])

    dx_end(last)
    stage(N.g_in, Sums.third_add)
    stage(N.g_attn, Sums.third_add)

    @wires.only(0)
    def _():
        wires.arrived(N.small_half, hbm[N.small_half])
        if pieces:
            wires.arrived(N.cross_half, hbm[N.cross_half])

    wires.close()


def shaped(*shape, kind=F32):
    return jax.ShapeDtypeStruct(shape, kind)


def pick(stacked, position):
    return lax.dynamic_index_in_dim(stacked, position, 0, keepdims=False)


def section_permute(x, axis, pairs, only):
    if only is None:
        return lax.ppermute(x, axis, pairs)
    first = only * lax.axis_size(axis)
    return lax.ppermute(x, ("section", axis), [(first + i, first + j) for i, j in pairs])


def group_permute(x, axis, members, stride, step, only=None):
    pairs = []
    for i in range(lax.axis_size(axis)):
        at = (i // stride) % members
        pairs.append((i, i + ((at + step) % members - at) * stride))
    return section_permute(x, axis, pairs, only)


def place_in(axis, members, stride):
    return (lax.axis_index(axis) // stride) % members


class Scatter:
    def __init__(self, parts, only=None):
        self.dp, self.chips = lax.axis_size("dp"), lax.axis_size("seq") // 2
        self.only, self.kind = only, parts.dtype
        self.parts = jnp.moveaxis(parts, 2, 0)
        self.stages = [("seq", 2, 1), ("seq", self.chips, 2), ("dp", self.dp, 1)]

    def send(self):
        axis, members, stride = self.stages[0]
        mine = place_in(axis, members, stride)
        self.keep = pick(self.parts, mine)
        return [pick(self.parts, (mine + step) % members) for step in range(1, members)]

    def arrive(self, sent):
        axis, members, stride = self.stages.pop(0)
        total = self.keep.astype(F32)
        for step in range(1, members):
            total = total + group_permute(sent[step - 1], axis, members, stride, step, self.only).astype(F32)
        if not self.stages:
            return total
        total = total.astype(self.kind)
        self.parts = jnp.moveaxis(total, 1, 0) if len(self.stages) == 2 else total
        return None

    def finish(self, sent=None):
        while self.stages:
            total = self.arrive(self.send() if sent is None else sent)
            sent = None
        return total


def by_device(total):
    dp_size, seq_size = lax.axis_size("dp"), lax.axis_size("seq")
    return total.reshape(dp_size, seq_size // 2, 2, total.shape[0] // (dp_size * seq_size), *total.shape[1:])


def to_encoder_half(total, section):
    half = total.shape[0] // 2
    arrived = lax.ppermute(total[:half], "section", [(1, 0)])
    return jnp.where(section == 0, arrived, total[half:])


def kernel_call(body, outs, operands, scratch, collective_id, flops, name):
    anywhere = pl.BlockSpec(memory_space=pltpu.HBM)
    size = sum(math.prod(o.shape) * o.dtype.itemsize for o in list(outs) + list(operands))
    return pl.pallas_call(
        body,
        out_shape=list(outs),
        in_specs=[anywhere] * len(operands),
        out_specs=[anywhere] * len(outs),
        scratch_shapes=scratch,
        cost_estimate=pl.CostEstimate(flops=int(flops), bytes_accessed=int(size), transcendentals=0),
        compiler_params=pltpu.CompilerParams(
            vmem_limit_bytes=VMEM_LIMIT, collective_id=collective_id, has_side_effects=True
        ),
        name=name,
    )(*operands)


def per_device(
    x_in, segments, cotangent, attn_in, attn_out, attn_bias, gains, ffn_in, ffn_bias, ffn_out,
    cross_q, cross_kv, cross_out, cross_bias, cross_gain,
):
    section = lax.axis_index("section")
    micro, length, width = x_in.shape[1], x_in.shape[3], x_in.shape[4]
    dp_size, seq_size = lax.axis_size("dp"), lax.axis_size("seq")
    chips = seq_size // 2
    devices = dp_size * seq_size
    tokens = length * seq_size
    hidden_units = ffn_in.shape[2]
    fused = width // devices % 16 == 0
    ticks = range(micro)
    x = x_in[0, :, 0]

    ids = segments.reshape(2 * micro, length)
    arrays = {
        N.x: x,
        N.ids: ids,
        N.cotangent: cotangent[:, 0],
        N.w_qkv: attn_in[0],
        N.w_mix: attn_out[0],
        N.w_in: ffn_in[0],
        N.w_out: ffn_out[0],
        N.b_in: ffn_bias,
        N.bias: attn_bias,
        N.gain: gains,
        N.cross_q: cross_q,
        N.cross_kv: cross_kv,
        N.cross_out: cross_out,
        N.cross_shift: cross_bias,
        N.cross_scale: cross_gain[None],
    }
    lw, lw_low = shaped(length, width), shaped(length, width, kind=BF16)
    tw_low = shaped(tokens, width, kind=BF16)
    lh_low = shaped(length, hidden_units, kind=BF16)
    pair_low = shaped(tokens, 2 * width, kind=BF16)
    half_low = shaped(tokens // 2, width, kind=BF16)
    rest_low = shaped(max(tokens // 2 - length, length), width, kind=BF16)
    far_low = shaped(max(chips - 1, 1), length, width, kind=BF16)
    seq_low = shaped(seq_size, length, width, kind=BF16)
    mask = shaped(length, tokens)
    lse_shape, few = shaped(HEADS // 2, length, PAIR), shaped(8, width)
    kinds = {
        N.q: lw_low, N.k: tw_low, N.v: tw_low, N.mixed: lw_low, N.lse: lse_shape, N.summed: lw, N.hidden: lw, N.squares: few,
        N.act: lh_low, N.slope: lh_low, N.final_sum: lw, N.low_middle: lw_low,
        N.dy3: lw_low, N.d_inner: lh_low, N.d_middle: lw, N.ffn_small: few,
        N.cq: lw_low, N.ck: tw_low, N.cv: tw_low, N.cross_mixed: lw_low, N.cross_lse: lse_shape, N.cross_sum: lw,
        N.middle: lw, N.low_hidden: lw_low,
        N.dyc: lw_low, N.dcq: lw_low, N.dckv: pair_low, N.dm_keep: half_low, N.dm_send: half_low,
        N.cross_small: few, N.dm_core_in: half_low, N.dm_sum: half_low, N.dm_chip_in: far_low, N.dm: lw_low, N.d_memory: lw_low,
        N.dy: lw_low, N.dq: lw_low, N.dkv: pair_low, N.dx_own: lw, N.dx_keep: rest_low, N.dx_send: half_low, N.self_small: few,
        N.dx_core_in: half_low, N.dx_sum: lw, N.dx_rest: rest_low, N.dx_chip_in: far_low,
        N.x_all: seq_low, N.memory: seq_low, N.self_bias: mask, N.cross_bias: mask,
    }
    outs = {(n, m): kind for m in ticks for n, kind in kinds.items()}
    for n in (N.layer_out, N.input_grad):
        outs[n] = shaped(micro, length, width, kind=BF16)
    outs[N.ids_all] = shaped(seq_size, *ids.shape, kind=ids.dtype)
    outs[N.d_final], outs[N.norm_small] = lw, few
    outs[N.part] = shaped(length // 2, width, kind=BF16)
    small_shape = shaped(24, width)
    for n in (N.small, N.small_core_in, N.small_core_sum, N.small_chip_sum, N.small_sum):
        outs[n] = small_shape
    outs[N.small_chip_in] = shaped(max(chips - 1, 1), 24, width)
    outs[N.small_row_in] = shaped(max(dp_size - 1, 1), 24, width)
    outs[N.small_half] = few
    totals = {
        N.g_cross: (width, 4 * width), N.g_out: (hidden_units, width), N.g_in: (width, hidden_units), N.g_attn: (width, 4 * width),
    }
    wire_names = [N.small_core, N.small_row, N.small_half] + [(N.small_chip, k) for k in range(1, chips)]
    for m in ticks:
        wire_names += gather_names((N.x, m), chips) + [(N.dm_core, m), (N.dx_core, m)]
        wire_names += [(N.dx_chip, k, m) for k in range(1, chips)]
        for h in range(2):
            wire_names += gather_names(((N.m, m), h), chips) + [(N.m, m, h), (N.dm, m, h)]
            wire_names += [(N.dm_chip, k, m, h) for k in range(1, chips)]
    pieces = sum_pieces(totals, devices) if fused else []
    for n, total in totals.items():
        outs[n] = shaped(*total, kind=BF16)
        if fused:
            outs[n, N.out] = shaped(total[0] // devices, total[1])
    for key, n, _, rows, dp_first in pieces:
        outs.update(sum_shapes(key, rows, totals[n][1], dp_first, dp_size, chips))
        wire_names += sum_names(key, chips)
    if fused:
        outs[N.cross_half] = shaped(width // 2 // devices, 4 * width)
        wire_names.append(N.cross_half)
    wire_names += gather_names(N.i, chips)
    held_names = [N.bias, N.gain, N.w_qkv, N.w_mix, N.w_in, N.b_in, N.w_out, N.cross_shift, N.cross_scale, N.cross_q, N.cross_kv, N.cross_out]
    scratch = [pltpu.VMEM(arrays[n].shape, arrays[n].dtype) for n in held_names]
    scratch += [pltpu.VMEM((8, width), F32)] * 2
    scratch += [pltpu.SemaphoreType.DMA((len(wire_names),))] * 2 + [pltpu.SemaphoreType.DMA((len(held_names),))]
    results = kernel_call(
        functools.partial(main_body, micro, pieces, list(arrays), list(outs), wire_names, held_names),
        list(outs.values()),
        list(arrays.values()),
        scratch,
        0,
        6 * micro * length * width * (12 * width + 2 * hidden_units),
        "layers",
    )
    results = dict(zip(outs, results))

    if fused:
        cross_part = None
        attn_part, ffn_in_part, ffn_out_part = (results[n, N.out] for n in (N.g_attn, N.g_in, N.g_out))
        cross_parts = [results[N.cross_half], results[N.g_cross, N.out]]
    else:
        halves = results[N.g_cross].reshape(2, width // 2, 4 * width)
        halves = jnp.stack([by_device(halves[0]), by_device(halves[1])], 3)
        cross_part = Scatter(halves, 1).finish()
        cross_part = jnp.where(
            section == 0, lax.ppermute(cross_part[0], "section", [(1, 0)]), cross_part[1]
        )
        attn_part, ffn_in_part, ffn_out_part = (
            Scatter(by_device(results[n])).finish() for n in (N.g_attn, N.g_in, N.g_out)
        )
        cross_parts = [cross_part]
    per, half, per_hidden = width // devices, width // 2 // devices, hidden_units // devices
    operands = [
        results[N.layer_out], results[N.input_grad], attn_part, ffn_in_part, ffn_out_part,
        results[N.small_sum], results[N.small_half], *cross_parts,
    ]
    final_shapes = [
        shaped(micro, length, width, kind=BF16),
        shaped(micro, length, width, kind=BF16),
        shaped(per, 3 * width),
        shaped(per, width),
        shaped(per, hidden_units),
        shaped(per_hidden, width),
        shaped(half, width),
        shaped(half, 2 * width),
        shaped(half, width),
        shaped(1, 2),
        shaped(6, per),
        shaped(2, per),
        shaped(1, per_hidden),
        shaped(4, half),
        shaped(1, half),
    ]
    anywhere = pl.BlockSpec(memory_space=pltpu.HBM)
    finals = pl.pallas_call(
        functools.partial(final_body, micro * dp_size * tokens * width, len(operands)),
        out_shape=final_shapes,
        in_specs=[anywhere] * len(operands),
        out_specs=[anywhere] * len(final_shapes),
        scratch_shapes=[pltpu.VMEM(o.shape, o.dtype) for o in operands + final_shapes[9:]]
        + [pltpu.SemaphoreType.DMA((len(operands),)), pltpu.SemaphoreType.DMA((len(final_shapes),))],
    )(*operands)
    (layer_out, input_grad, attn_in_grad, attn_out_grad, ffn_in_grad, ffn_out_grad, cross_q_grad, cross_kv_grad,
     cross_out_grad, stats, attn_bias_grad, gains_grad, ffn_bias_grad, cross_bias_grad, cross_gain_grad) = finals
    return (
        layer_out[None, :, None],
        input_grad[None, :, None],
        stats,
        attn_in_grad[None],
        attn_out_grad[None],
        attn_bias_grad[None],
        gains_grad[None],
        ffn_in_grad[None],
        ffn_bias_grad,
        ffn_out_grad[None],
        cross_q_grad,
        cross_kv_grad,
        cross_out_grad,
        cross_bias_grad,
        cross_gain_grad[0],
    )


def solution(mesh):
    return jax.shard_map(
        per_device,
        mesh=mesh,
        in_specs=(
            P("section", None, "dp", "seq", None),
            P(None, None, "dp", "seq"),
            P(None, "dp", "seq", None),
            P("section", None, None),
            P("section", None, None),
            P("section", None, None),
            P("section", None, None),
            P("section", None, None),
            P("section", None),
            P("section", None, None),
            P(),
            P(),
            P(),
            P(),
            P(),
        ),
        out_specs=(
            P("section", None, "dp", "seq", None),
            P("section", None, "dp", "seq", None),
            P("section", None),
            P("section", ("dp", "seq"), None),
            P("section", ("dp", "seq"), None),
            P("section", None, ("dp", "seq")),
            P("section", None, ("dp", "seq")),
            P("section", ("dp", "seq"), None),
            P("section", ("dp", "seq")),
            P("section", ("dp", "seq"), None),
            P(("section", "dp", "seq"), None),
            P(("section", "dp", "seq"), None),
            P(("section", "dp", "seq"), None),
            P(None, ("section", "dp", "seq")),
            P(("section", "dp", "seq")),
        ),
        check_vma=False,
    )
```
